512 devices in a mesh: tx: 32 (over z, core), ty: 16 (over x, y).
Axes of the slice: x: 4, y: 4, z: 16, core: 2. Of those that a mesh axis runs over, the one named last changes fastest.
Arguments:
- rhs: bfloat16 [16, 262144], P(None, ('tx', 'ty')), may hold values from -6 to 6
- diag_blocks: bfloat16 [262144, 512], P(('tx', 'ty')), may hold values from -0.25 to 0.25
- leaf_in: bfloat16 [262144, 128], P(('tx', 'ty')), may hold values from -0.25 to 0.25
- leaf_out: bfloat16 [65536, 512], P(('tx', 'ty')), may hold values from -0.5 to 0.5
- up_maps: bfloat16 [2, 512, 512, 512], P(None, ('tx', 'ty')), may hold values from -0.25 to 0.25
- cross_maps: bfloat16 [2, 512, 512, 512], P(None, ('tx', 'ty')), may hold values from -0.3125 to 0.3125
- down_maps: bfloat16 [2, 512, 512, 512], P(None, ('tx', 'ty')), may hold values from -0.3125 to 0.3125
- node_rank: int32 [512, 2], P(('tx', 'ty')), may hold values from 64 to 512, as said below
Outputs:
- product: float32 [16, 262144], P(None, ('tx', 'ty'))
The draws below stay inside these ranges and needn't reach their ends.
Inputs may be any that keep to these rules, and one draw needn't show every extreme that they name: node_rank[d,0] is a multiple of 16 from 64 to 128; node_rank[d,1] is a multiple of 64 from 128 to 512, and the root's owner has 512; device 0 owns no upper node.
All inputs are finite; a program needn't handle non-finite values.
Results may differ from the reference program's by a relative error of at most 0.023.
Values may be sent and summed in bfloat16 or wider, within the bound.
A program may use at most 64 MiB of HBM per device.

```python
import jax
import jax.numpy as jnp
import numpy as np

P_SIZE = 512
S = 16
RLEAF = 128
RMAX = 512
N = 262144
N_TX = 32
N_TY = 16


def draw_node_rank(key, part):
    key = jax.random.fold_in(key, 7)
    first, second = jax.random.split(key)
    device_count = N_TX * N_TY
    leaf_rank = RLEAF // 2 + RLEAF // 8 * jax.random.randint(first, (device_count,), 0, 5)
    choices_count = (RMAX - RLEAF) // (RLEAF // 2) + 1
    upper_rank = RLEAF + RLEAF // 2 * jax.random.randint(second, (device_count,), 0, choices_count)
    leaf_rank = leaf_rank.at[0].set(RLEAF).at[1].set(RLEAF // 2)
    upper_rank = upper_rank.at[device_count // 2].set(RMAX).at[1].set(RLEAF)
    return jnp.stack([leaf_rank, upper_rank], axis=1).astype(jnp.int32)


def block_levels(own_key, extent, pieces, low, top_value):
    loudness, own = 1.0, jax.random.fold_in(own_key, 6)
    for axis_at, shards_of in pieces:
        steps = jnp.exp(jax.random.uniform(jax.random.fold_in(own, axis_at), (shards_of,), jnp.float32, low / len(pieces), top_value / len(pieces)))
        loudness = loudness * jnp.repeat(steps, extent[axis_at] // shards_of).reshape([-1 if axis == axis_at else 1 for axis in range(len(extent))])
    return loudness


def scatter_about(own_key, shape, deviation, reach, cuts=(), held_as=jnp.bfloat16):
    loudness = block_levels(own_key, shape, cuts, -0.22, 0.18) if cuts else 1.0
    array = jax.random.normal(own_key, shape, jnp.float32) * deviation * loudness
    return jnp.minimum(jnp.maximum(array, -reach), reach).astype(held_as)


def setup_inputs(seed: int = 0) -> dict:
    arg_keys = jax.random.split(jax.random.key(seed), 9)
    return {
        "rhs": scatter_about(arg_keys[0], (S, N), 1.0, 6.0, ((1, 512),)),
        "diag_blocks": scatter_about(arg_keys[1], (N, P_SIZE), P_SIZE ** -0.5, 0.25, ((0, 512),)),
        "leaf_in": scatter_about(arg_keys[2], (N, RLEAF), P_SIZE ** -0.5, 0.25, ((0, 512),)),
        "leaf_out": scatter_about(arg_keys[3], (N_TX * N_TY * RLEAF, P_SIZE), RLEAF ** -0.5, 0.5, ((0, 512),)),
        "up_maps": scatter_about(arg_keys[4], (2, N_TX * N_TY, RMAX, RMAX), (RMAX + RMAX // 4) ** -0.5, 0.25, ((1, 512),)),
        "cross_maps": scatter_about(arg_keys[5], (2, N_TX * N_TY, RMAX, RMAX), (RMAX * 5 // 8) ** -0.5, 0.3125, ((1, 512),)),
        "down_maps": scatter_about(arg_keys[6], (2, N_TX * N_TY, RMAX, RMAX), (RMAX * 5 // 8) ** -0.5, 0.3125, ((1, 512),)),
        "node_rank": draw_node_rank(jax.random.fold_in(arg_keys[8], 71), 0),
    }


def reference(rhs, diag_blocks, leaf_in, leaf_out, up_maps, cross_maps, down_maps, node_rank):
    f32 = jnp.float32
    device_count = N_TX * N_TY
    levels = device_count.bit_length() - 1
    rhs_blocks = rhs.reshape(S, device_count, P_SIZE).transpose(1, 0, 2).astype(f32)
    columns = jnp.arange(RMAX, dtype=jnp.int32)
    leaf_keep = columns[None, None, :] < node_rank[:, 0][:, None, None]
    node_keep = columns[None, None, :] < node_rank[:, 1][:, None, None]
    projected = jnp.einsum("dsp,dpr->dsr", rhs_blocks, leaf_in.reshape(device_count, P_SIZE, RLEAF).astype(f32))
    projected = jnp.pad(projected, ((0, 0), (0, 0), (0, RMAX - RLEAF)))
    coeffs = [jnp.where(leaf_keep, projected, 0.0).astype(jnp.bfloat16)]
    for height in range(1, levels):
        owners = np.arange(device_count >> height) * 2 ** height + 2 ** (height - 1)
        child = coeffs[-1].astype(f32)
        summed = jnp.einsum("nsr,nrq->nsq", child[0::2], up_maps[0, owners].astype(f32))
        summed = summed + jnp.einsum("nsr,nrq->nsq", child[1::2], up_maps[1, owners].astype(f32))
        coeffs.append(jnp.where(node_keep[owners], summed, 0.0).astype(jnp.bfloat16))
    down_coef = jnp.zeros((1, S, RMAX), f32)
    for height in range(levels, 0, -1):
        owners = np.arange(device_count >> height) * 2 ** height + 2 ** (height - 1)
        child = coeffs[height - 1].astype(f32)
        to_left = jnp.einsum("nsr,nrq->nsq", child[1::2], cross_maps[0, owners].astype(f32))
        to_left = (to_left + jnp.einsum("nsr,nrq->nsq", down_coef, down_maps[0, owners].astype(f32))).astype(jnp.bfloat16)
        to_right = jnp.einsum("nsr,nrq->nsq", child[0::2], cross_maps[1, owners].astype(f32))
        to_right = (to_right + jnp.einsum("nsr,nrq->nsq", down_coef, down_maps[1, owners].astype(f32))).astype(jnp.bfloat16)
        merged = jnp.stack([to_left, to_right], axis=1).reshape(-1, S, RMAX)
        if height > 1:
            child_owners = np.arange(2 * len(owners)) * 2 ** (height - 1) + 2 ** (height - 2)
            keep = node_keep[child_owners]
        else:
            keep = leaf_keep
        down_coef = jnp.where(keep, merged, 0.0).astype(f32)
    result = jnp.einsum("dsp,dpq->dsq", rhs_blocks, diag_blocks.reshape(device_count, P_SIZE, P_SIZE).astype(f32))
    result = result + jnp.einsum("dsr,drq->dsq", down_coef[:, :, :RLEAF], leaf_out.reshape(device_count, RLEAF, P_SIZE).astype(f32))
    return result.transpose(1, 0, 2).reshape(S, device_count * P_SIZE)
```

```python
import functools

import jax
import jax.numpy as jnp
from jax import lax
from jax.experimental import pallas as pl
from jax.experimental.pallas import tpu as pltpu
from jax.sharding import PartitionSpec as P

MESH = pl.DeviceIdType.MESH
F32 = jnp.float32
BF16 = jnp.bfloat16


def kernel(
    row_len,
    levels,
    rhs_hbm,
    diag_hbm,
    in_hbm,
    out_hbm,
    up_hbm,
    cross_hbm,
    down_hbm,
    rank_hbm,
    product,
    rhs,
    diag,
    leaf_in,
    leaf_out,
    up,
    cross,
    down,
    rank,
    leaf_coef,
    coef,
    child,
    cross_sum,
    to_child,
    down_in,
    leaf_down,
    load_sem,
    send_sem,
    recv_sem,
):
    me = lax.axis_index("tx") * row_len + lax.axis_index("ty")
    rows, width = coef.shape
    leaf_width = leaf_coef.shape[1]
    half = 1
    for height in range(2, levels + 1):
        half = jnp.where(me % 2 ** (height - 1) == 0, 2 ** (height - 1), half)
    is_leaf_only = me == 0
    is_odd = me % 2 == 1
    is_root = me == 2 ** (levels - 1)
    is_upper = jnp.logical_and(me % 2 == 0, me > 0)
    sends_up = jnp.logical_and(me > 0, jnp.logical_not(is_root))
    on_left = (me // (2 * half)) % 2 == 0
    parent = jnp.where(on_left, me + half, me - half)
    quarter = half // 2
    peer = jnp.where(is_odd, me - 1, me + 1)

    def device(number):
        return (number // row_len, number % row_len)

    loads = [
        pltpu.make_async_copy(source, target, load_sem.at[at])
        for at, (source, target) in enumerate(
            (
                (rhs_hbm, rhs),
                (in_hbm, leaf_in),
                (rank_hbm, rank),
                (up_hbm, up),
                (cross_hbm, cross),
                (down_hbm, down),
                (diag_hbm, diag),
                (out_hbm, leaf_out),
            )
        )
    ]
    load_rhs, load_in, load_rank, load_up, load_cross, load_down, load_diag, load_out = loads
    for load in loads:
        load.start()

    barrier = pltpu.get_barrier_semaphore()

    def greet(number):
        pl.semaphore_signal(barrier, inc=1, device_id=device(number), device_id_type=MESH)

    greet(peer)

    @pl.when(sends_up)
    def _():
        greet(parent)

    @pl.when(is_upper)
    def _():
        greet(me - quarter)
        greet(me + quarter)

    def remote(source, target, at_send, at_recv, number):
        return pltpu.make_async_remote_copy(
            src_ref=source,
            dst_ref=target,
            send_sem=send_sem.at[at_send],
            recv_sem=recv_sem.at[at_recv],
            device_id=device(number),
            device_id_type=MESH,
        )

    left_part, right_part = pl.ds(0, width), pl.ds(width, width)
    narrow, narrow_right = pl.ds(0, leaf_width), pl.ds(width, leaf_width)

    load_rhs.wait()
    load_in.wait()
    load_rank.wait()
    leaf_keep = lax.broadcasted_iota(jnp.int32, (rows, leaf_width), 1) < rank[0, 0]
    node_keep = lax.broadcasted_iota(jnp.int32, (rows, width), 1) < rank[0, 1]
    projected = jnp.dot(rhs[...], leaf_in[...], preferred_element_type=F32)
    leaf_coef[...] = jnp.where(leaf_keep, projected, 0.0).astype(BF16)

    greeted = 1 + sends_up.astype(jnp.int32) + 2 * is_upper.astype(jnp.int32)
    pl.semaphore_wait(barrier, greeted)

    leaf_up = remote(leaf_coef, child.at[:, narrow], 0, 0, peer)
    up_left = remote(coef, child.at[:, left_part], 1, 0, parent)
    up_right = remote(coef, child.at[:, right_part], 1, 1, parent)
    down_left = remote(to_child.at[0], down_in, 2, 2, me - quarter)
    down_right = remote(to_child.at[1], down_in, 3, 2, me + quarter)
    leaf_left = remote(to_child.at[0, :, narrow], leaf_down, 2, 3, peer)

    def send_up(summed):
        coef[...] = jnp.where(node_keep, summed, 0.0).astype(BF16)

        @pl.when(on_left)
        def _():
            up_left.start()

        @pl.when(jnp.logical_not(on_left))
        def _():
            up_right.start()

    @pl.when(jnp.logical_not(is_odd))
    def _():
        leaf_up.start()

    @pl.when(is_odd)
    def _():
        load_up.wait()
        summed = jnp.dot(leaf_coef[...], up[1, 0, narrow, :], preferred_element_type=F32)
        leaf_up.wait_recv()
        summed += jnp.dot(child[:, narrow], up[0, 0, narrow, :], preferred_element_type=F32)
        send_up(summed)
        load_cross.wait()
        cross_sum[0, :, narrow] = jnp.dot(leaf_coef[...], cross[0, 0, narrow, narrow], preferred_element_type=F32)
        cross_sum[1, :, narrow] = jnp.dot(child[:, narrow], cross[1, 0, narrow, narrow], preferred_element_type=F32)

    @pl.when(is_upper)
    def _():
        load_up.wait()
        up_left.wait_recv()

        @pl.when(sends_up)
        def _():
            summed = jnp.dot(child[:, left_part], up[0, 0], preferred_element_type=F32)
            up_right.wait_recv()
            summed += jnp.dot(child[:, right_part], up[1, 0], preferred_element_type=F32)
            send_up(summed)
            load_cross.wait()
            cross_sum[0] = jnp.dot(child[:, right_part], cross[0, 0], preferred_element_type=F32)
            cross_sum[1] = jnp.dot(child[:, left_part], cross[1, 0], preferred_element_type=F32)

        @pl.when(is_root)
        def _():
            load_cross.wait()
            to_child[1] = jnp.dot(child[:, left_part], cross[1, 0], preferred_element_type=F32).astype(BF16)
            down_right.start()
            up_right.wait_recv()
            to_child[0] = jnp.dot(child[:, right_part], cross[0, 0], preferred_element_type=F32).astype(BF16)
            down_left.start()

    load_diag.wait()
    product[...] = jnp.dot(rhs[...], diag[...], preferred_element_type=F32)
    load_out.wait()
    load_down.wait()

    @pl.when(sends_up)
    def _():
        down_left.wait_recv()
        down_in[...] = jnp.where(node_keep, down_in[...], jnp.zeros_like(down_in))

    @pl.when(is_odd)
    def _():
        to_left = cross_sum[0, :, narrow] + jnp.dot(down_in[...], down[0, 0, :, narrow], preferred_element_type=F32)
        to_child[0, :, narrow] = to_left.astype(BF16)
        leaf_left.start()
        to_right = cross_sum[1, :, narrow] + jnp.dot(down_in[...], down[1, 0, :, narrow], preferred_element_type=F32)
        leaf_down[...] = to_right.astype(BF16)

    @pl.when(jnp.logical_and(is_upper, sends_up))
    def _():
        to_left = cross_sum[0] + jnp.dot(down_in[...], down[0, 0], preferred_element_type=F32)
        to_child[0] = to_left.astype(BF16)
        down_left.start()
        to_right = cross_sum[1] + jnp.dot(down_in[...], down[1, 0], preferred_element_type=F32)
        to_child[1] = to_right.astype(BF16)
        down_right.start()

    @pl.when(jnp.logical_not(is_odd))
    def _():
        leaf_left.wait_recv()

    kept = jnp.where(leaf_keep, leaf_down[...], jnp.zeros_like(leaf_down))
    product[...] += jnp.dot(kept, leaf_out[...], preferred_element_type=F32)

    @pl.when(is_leaf_only)
    def _():
        load_up.wait()
        load_cross.wait()

    @pl.when(is_root)
    def _():
        pass

    @pl.when(jnp.logical_not(is_odd))
    def _():
        leaf_up.wait_send()

    @pl.when(is_odd)
    def _():
        leaf_left.wait_send()

    @pl.when(sends_up)
    def _():
        up_left.wait_send()

    @pl.when(is_upper)
    def _():
        down_left.wait_send()
        down_right.wait_send()


def on_device(levels, row_len, rhs, diag_blocks, leaf_in, leaf_out, up_maps, cross_maps, down_maps, node_rank):
    rows, leaf = rhs.shape
    width, leaf_width = up_maps.shape[-1], leaf_in.shape[1]
    operands = (rhs, diag_blocks, leaf_in, leaf_out, up_maps, cross_maps, down_maps)
    return pl.pallas_call(
        functools.partial(kernel, row_len, levels),
        out_shape=jax.ShapeDtypeStruct((rows, leaf), F32),
        in_specs=[pl.BlockSpec(memory_space=pl.ANY)] * 8,
        out_specs=pl.BlockSpec(memory_space=pltpu.VMEM),
        scratch_shapes=[pltpu.VMEM(each.shape, each.dtype) for each in operands]
        + [
            pltpu.SMEM(node_rank.shape, node_rank.dtype),
            pltpu.VMEM((rows, leaf_width), BF16),
            pltpu.VMEM((rows, width), BF16),
            pltpu.VMEM((rows, 2 * width), BF16),
            pltpu.VMEM((2, rows, width), F32),
            pltpu.VMEM((2, rows, width), BF16),
            pltpu.VMEM((rows, width), BF16),
            pltpu.VMEM((rows, leaf_width), BF16),
            pltpu.SemaphoreType.DMA((8,)),
            pltpu.SemaphoreType.DMA((4,)),
            pltpu.SemaphoreType.DMA((4,)),
        ],
        compiler_params=pltpu.CompilerParams(
            collective_id=0, has_side_effects=True, vmem_limit_bytes=48 * 2**20
        ),
    )(*operands, node_rank)


def solution(mesh):
    row_len = mesh.shape["ty"]
    levels = (mesh.shape["tx"] * row_len).bit_length() - 1
    in_specs = (
        P(None, ("tx", "ty")),
        P(("tx", "ty"), None),
        P(("tx", "ty"), None),
        P(("tx", "ty"), None),
        P(None, ("tx", "ty"), None, None),
        P(None, ("tx", "ty"), None, None),
        P(None, ("tx", "ty"), None, None),
        P(("tx", "ty"), None),
    )
    return jax.shard_map(
        functools.partial(on_device, levels, row_len),
        mesh=mesh,
        in_specs=in_specs,
        out_specs=P(None, ("tx", "ty")),
        check_vma=False,
    )
```

```python
import functools

import jax
import jax.numpy as jnp
from jax import lax
from jax.experimental import pallas as pl
from jax.experimental.pallas import tpu as pltpu
from jax.sharding import PartitionSpec as P

MESH = pl.DeviceIdType.MESH
F32 = jnp.float32
BF16 = jnp.bfloat16


def kernel(
    row_len,
    levels,
    rhs_hbm,
    diag_hbm,
    in_hbm,
    out_hbm,
    up_hbm,
    cross_hbm,
    down_hbm,
    rank_hbm,
    product,
    rhs,
    diag,
    leaf_in,
    leaf_out,
    up,
    cross,
    down,
    rank,
    leaf_coef,
    coef,
    child,
    cross_sum,
    to_child,
    down_in,
    leaf_down,
    load_sem,
    send_sem,
    recv_sem,
):
    me = lax.axis_index("tx") * row_len + lax.axis_index("ty")
    rows, width = coef.shape
    leaf_width = leaf_coef.shape[1]
    half = 1
    for height in range(2, levels + 1):
        half = jnp.where(me % 2 ** (height - 1) == 0, 2 ** (height - 1), half)
    is_leaf_only = me == 0
    is_odd = me % 2 == 1
    is_root = me == 2 ** (levels - 1)
    is_upper = jnp.logical_and(me % 2 == 0, me > 0)
    sends_up = jnp.logical_and(me > 0, jnp.logical_not(is_root))
    on_left = (me // (2 * half)) % 2 == 0
    parent = jnp.where(on_left, me + half, me - half)
    quarter = half // 2
    peer = jnp.where(is_odd, me - 1, me + 1)

    def device(number):
        return (number // row_len, number % row_len)

    loads = [
        pltpu.make_async_copy(source, target, load_sem.at[at])
        for at, (source, target) in enumerate(
            (
                (rhs_hbm, rhs),
                (in_hbm, leaf_in),
                (rank_hbm, rank),
                (up_hbm, up),
                (cross_hbm, cross),
                (down_hbm, down),
                (diag_hbm, diag),
                (out_hbm, leaf_out),
            )
        )
    ]
    load_rhs, load_in, load_rank, load_up, load_cross, load_down, load_diag, load_out = loads
    for load in loads:
        load.start()

    barrier = pltpu.get_barrier_semaphore()

    def greet(number):
        pl.semaphore_signal(barrier, inc=1, device_id=device(number), device_id_type=MESH)

    greet(peer)

    @pl.when(sends_up)
    def _():
        greet(parent)

    @pl.when(is_upper)
    def _():
        greet(me - quarter)
        greet(me + quarter)

    def remote(source, target, at_send, at_recv, number):
        return pltpu.make_async_remote_copy(
            src_ref=source,
            dst_ref=target,
            send_sem=send_sem.at[at_send],
            recv_sem=recv_sem.at[at_recv],
            device_id=device(number),
            device_id_type=MESH,
        )

    left_part, right_part = pl.ds(0, width), pl.ds(width, width)
    narrow, narrow_right = pl.ds(0, leaf_width), pl.ds(width, leaf_width)

    load_rhs.wait()
    load_in.wait()
    load_rank.wait()
    leaf_keep = lax.broadcasted_iota(jnp.int32, (rows, leaf_width), 1) < rank[0, 0]
    node_keep = lax.broadcasted_iota(jnp.int32, (rows, width), 1) < rank[0, 1]
    projected = jnp.dot(rhs[...], leaf_in[...], preferred_element_type=F32)
    leaf_coef[...] = jnp.where(leaf_keep, projected, 0.0).astype(BF16)

    greeted = 1 + sends_up.astype(jnp.int32) + 2 * is_upper.astype(jnp.int32)
    pl.semaphore_wait(barrier, greeted)

    leaf_up = remote(leaf_coef, child.at[:, narrow], 0, 0, peer)
    up_left = remote(coef, child.at[:, left_part], 1, 0, parent)
    up_right = remote(coef, child.at[:, right_part], 1, 1, parent)
    down_left = remote(to_child.at[0], down_in, 2, 2, me - quarter)
    down_right = remote(to_child.at[1], down_in, 3, 2, me + quarter)
    leaf_left = remote(to_child.at[0, :, narrow], leaf_down, 2, 3, peer)

    def send_up(summed):
        coef[...] = jnp.where(node_keep, summed, 0.0).astype(BF16)

        @pl.when(on_left)
        def _():
            up_left.start()

        @pl.when(jnp.logical_not(on_left))
        def _():
            up_right.start()

    @pl.when(jnp.logical_not(is_odd))
    def _():
        leaf_up.start()

    @pl.when(is_odd)
    def _():
        load_up.wait()
        summed = jnp.dot(leaf_coef[...], up[1, 0, narrow, :], preferred_element_type=F32)
        leaf_up.wait_recv()
        summed += jnp.dot(child[:, narrow], up[0, 0, narrow, :], preferred_element_type=F32)
        send_up(summed)
        load_cross.wait()
        cross_sum[0, :, narrow] = jnp.dot(leaf_coef[...], cross[0, 0, narrow, narrow], preferred_element_type=F32)
        cross_sum[1, :, narrow] = jnp.dot(child[:, narrow], cross[1, 0, narrow, narrow], preferred_element_type=F32)

    @pl.when(is_upper)
    def _():
        load_up.wait()
        up_left.wait_recv()

        @pl.when(sends_up)
        def _():
            summed = jnp.dot(child[:, left_part], up[0, 0], preferred_element_type=F32)
            up_right.wait_recv()
            summed += jnp.dot(child[:, right_part], up[1, 0], preferred_element_type=F32)
            send_up(summed)
            load_cross.wait()
            cross_sum[0] = jnp.dot(child[:, right_part], cross[0, 0], preferred_element_type=F32)
            cross_sum[1] = jnp.dot(child[:, left_part], cross[1, 0], preferred_element_type=F32)

        @pl.when(is_root)
        def _():
            load_cross.wait()
            to_child[1] = jnp.dot(child[:, left_part], cross[1, 0], preferred_element_type=F32).astype(BF16)
            down_right.start()
            up_right.wait_recv()
            to_child[0] = jnp.dot(child[:, right_part], cross[0, 0], preferred_element_type=F32).astype(BF16)
            down_left.start()

    load_diag.wait()
    product[...] = jnp.dot(rhs[...], diag[...], preferred_element_type=F32)
    load_out.wait()
    load_down.wait()

    @pl.when(sends_up)
    def _():
        down_left.wait_recv()
        down_in[...] = jnp.where(node_keep, down_in[...], jnp.zeros_like(down_in))

    @pl.when(is_odd)
    def _():
        to_left = cross_sum[0, :, narrow] + jnp.dot(down_in[...], down[0, 0, :, narrow], preferred_element_type=F32)
        to_child[0, :, narrow] = to_left.astype(BF16)
        leaf_left.start()
        to_right = cross_sum[1, :, narrow] + jnp.dot(down_in[...], down[1, 0, :, narrow], preferred_element_type=F32)
        leaf_down[...] = to_right.astype(BF16)

    @pl.when(jnp.logical_and(is_upper, sends_up))
    def _():
        to_left = cross_sum[0] + jnp.dot(down_in[...], down[0, 0], preferred_element_type=F32)
        to_child[0] = to_left.astype(BF16)
        down_left.start()
        to_right = cross_sum[1] + jnp.dot(down_in[...], down[1, 0], preferred_element_type=F32)
        to_child[1] = to_right.astype(BF16)
        down_right.start()

    @pl.when(jnp.logical_not(is_odd))
    def _():
        leaf_left.wait_recv()

    kept = jnp.where(leaf_keep, leaf_down[...], jnp.zeros_like(leaf_down))
    product[...] += jnp.dot(kept, leaf_out[...], preferred_element_type=F32)

    @pl.when(is_leaf_only)
    def _():
        load_up.wait()
        load_cross.wait()

    @pl.when(is_root)
    def _():
        pass

    @pl.when(jnp.logical_not(is_odd))
    def _():
        leaf_up.wait_send()

    @pl.when(is_odd)
    def _():
        leaf_left.wait_send()

    @pl.when(sends_up)
    def _():
        up_left.wait_send()

    @pl.when(is_upper)
    def _():
        down_left.wait_send()
        down_right.wait_send()


def on_device(levels, row_len, rhs, diag_blocks, leaf_in, leaf_out, up_maps, cross_maps, down_maps, node_rank):
    rows, leaf = rhs.shape
    width, leaf_width = up_maps.shape[-1], leaf_in.shape[1]
    operands = (rhs, diag_blocks, leaf_in, leaf_out, up_maps, cross_maps, down_maps)
    return pl.pallas_call(
        functools.partial(kernel, row_len, levels),
        out_shape=jax.ShapeDtypeStruct((rows, leaf), F32),
        in_specs=[pl.BlockSpec(memory_space=pltpu.HBM)] * 8,
        out_specs=pl.BlockSpec(memory_space=pltpu.VMEM),
        scratch_shapes=[pltpu.VMEM(each.shape, each.dtype) for each in operands]
        + [
            pltpu.SMEM(node_rank.shape, node_rank.dtype),
            pltpu.VMEM((rows, leaf_width), BF16),
            pltpu.VMEM((rows, width), BF16),
            pltpu.VMEM((rows, 2 * width), BF16),
            pltpu.VMEM((2, rows, width), F32),
            pltpu.VMEM((2, rows, width), BF16),
            pltpu.VMEM((rows, width), BF16),
            pltpu.VMEM((rows, leaf_width), BF16),
            pltpu.SemaphoreType.DMA((8,)),
            pltpu.SemaphoreType.DMA((4,)),
            pltpu.SemaphoreType.DMA((4,)),
        ],
        compiler_params=pltpu.CompilerParams(
            collective_id=0, has_side_effects=True, vmem_limit_bytes=32 * 2**20
        ),
    )(*operands, node_rank)


def solution(mesh):
    row_len = mesh.shape["ty"]
    levels = (mesh.shape["tx"] * row_len).bit_length() - 1
    in_specs = (
        P(None, ("tx", "ty")),
        P(("tx", "ty"), None),
        P(("tx", "ty"), None),
        P(("tx", "ty"), None),
        P(None, ("tx", "ty"), None, None),
        P(None, ("tx", "ty"), None, None),
        P(None, ("tx", "ty"), None, None),
        P(("tx", "ty"), None),
    )
    return jax.shard_map(
        functools.partial(on_device, levels, row_len),
        mesh=mesh,
        in_specs=in_specs,
        out_specs=P(None, ("tx", "ty")),
        check_vma=False,
    )
```

```python
import functools

import jax
import jax.numpy as jnp
from jax import lax
from jax.experimental import pallas as pl
from jax.experimental.pallas import tpu as pltpu
from jax.sharding import PartitionSpec as P

MESH = pl.DeviceIdType.MESH
F32 = jnp.float32
BF16 = jnp.bfloat16


def kernel(
    row_len,
    levels,
    rhs_hbm,
    diag_hbm,
    in_hbm,
    out_hbm,
    up_hbm,
    cross_hbm,
    down_hbm,
    rank_hbm,
    product,
    rhs,
    diag,
    leaf_in,
    leaf_out,
    up,
    cross,
    down,
    rank,
    leaf_coef,
    coef,
    child,
    cross_sum,
    to_child,
    down_in,
    leaf_down,
    load_sem,
    send_sem,
    recv_sem,
):
    me = lax.axis_index("tx") * row_len + lax.axis_index("ty")
    rows, width = coef.shape
    leaf_width = leaf_coef.shape[1]
    half = 1
    for height in range(2, levels + 1):
        half = jnp.where(me % 2 ** (height - 1) == 0, 2 ** (height - 1), half)
    is_leaf_only = me == 0
    is_odd = me % 2 == 1
    is_root = me == 2 ** (levels - 1)
    is_upper = jnp.logical_and(me % 2 == 0, me > 0)
    sends_up = jnp.logical_and(me > 0, jnp.logical_not(is_root))
    on_left = (me // (2 * half)) % 2 == 0
    parent = jnp.where(on_left, me + half, me - half)
    quarter = half // 2
    peer = jnp.where(is_odd, me - 1, me + 1)

    def device(number):
        return (number // row_len, number % row_len)

    loads = [
        pltpu.make_async_copy(source, target, load_sem.at[at])
        for at, (source, target) in enumerate(
            (
                (rhs_hbm, rhs),
                (in_hbm, leaf_in),
                (rank_hbm, rank),
                (up_hbm, up),
                (cross_hbm, cross),
                (down_hbm, down),
                (diag_hbm, diag),
                (out_hbm, leaf_out),
            )
        )
    ]
    load_rhs, load_in, load_rank, load_up, load_cross, load_down, load_diag, load_out = loads
    for load in loads:
        load.start()

    barrier = pltpu.get_barrier_semaphore()

    def greet(number):
        pl.semaphore_signal(barrier, inc=1, device_id=device(number), device_id_type=MESH)

    greet(peer)

    @pl.when(sends_up)
    def _():
        greet(parent)

    @pl.when(is_upper)
    def _():
        greet(me - quarter)
        greet(me + quarter)

    def remote(source, target, at_send, at_recv, number):
        return pltpu.make_async_remote_copy(
            src_ref=source,
            dst_ref=target,
            send_sem=send_sem.at[at_send],
            recv_sem=recv_sem.at[at_recv],
            device_id=device(number),
            device_id_type=MESH,
        )

    left_part, right_part = pl.ds(0, width), pl.ds(width, width)
    narrow, narrow_right = pl.ds(0, leaf_width), pl.ds(width, leaf_width)

    load_rhs.wait()
    load_in.wait()
    load_rank.wait()
    leaf_keep = lax.broadcasted_iota(jnp.int32, (rows, leaf_width), 1) < rank[0, 0]
    node_keep = lax.broadcasted_iota(jnp.int32, (rows, width), 1) < rank[0, 1]
    projected = jnp.dot(rhs[...], leaf_in[...], preferred_element_type=F32)
    leaf_coef[...] = jnp.where(leaf_keep, projected, 0.0).astype(BF16)

    greeted = 1 + sends_up.astype(jnp.int32) + 2 * is_upper.astype(jnp.int32)
    pl.semaphore_wait(barrier, greeted)

    leaf_up = remote(leaf_coef, child.at[:, narrow], 0, 0, peer)
    up_left = remote(coef, child.at[:, left_part], 1, 0, parent)
    up_right = remote(coef, child.at[:, right_part], 1, 1, parent)
    down_left = remote(to_child.at[0], down_in, 2, 2, me - quarter)
    down_right = remote(to_child.at[1], down_in, 3, 2, me + quarter)
    leaf_left = remote(to_child.at[0, :, narrow], leaf_down, 2, 3, peer)

    def send_up(summed):
        coef[...] = jnp.where(node_keep, summed, 0.0).astype(BF16)

        @pl.when(on_left)
        def _():
            up_left.start()

        @pl.when(jnp.logical_not(on_left))
        def _():
            up_right.start()

    @pl.when(jnp.logical_not(is_odd))
    def _():
        leaf_up.start()

    @pl.when(is_odd)
    def _():
        load_up.wait()
        summed = jnp.dot(leaf_coef[...], up[1, 0, narrow, :], preferred_element_type=F32)
        leaf_up.wait_recv()
        summed += jnp.dot(child[:, narrow], up[0, 0, narrow, :], preferred_element_type=F32)
        send_up(summed)
        load_cross.wait()
        cross_sum[0, :, narrow] = jnp.dot(leaf_coef[...], cross[0, 0, narrow, narrow], preferred_element_type=F32)
        cross_sum[1, :, narrow] = jnp.dot(child[:, narrow], cross[1, 0, narrow, narrow], preferred_element_type=F32)

    @pl.when(is_upper)
    def _():
        load_up.wait()
        up_left.wait_recv()

        @pl.when(sends_up)
        def _():
            summed = jnp.dot(child[:, left_part], up[0, 0], preferred_element_type=F32)
            up_right.wait_recv()
            summed += jnp.dot(child[:, right_part], up[1, 0], preferred_element_type=F32)
            send_up(summed)
            load_cross.wait()
            cross_sum[0] = jnp.dot(child[:, right_part], cross[0, 0], preferred_element_type=F32)
            cross_sum[1] = jnp.dot(child[:, left_part], cross[1, 0], preferred_element_type=F32)

        @pl.when(is_root)
        def _():
            load_cross.wait()
            to_child[1] = jnp.dot(child[:, left_part], cross[1, 0], preferred_element_type=F32).astype(BF16)
            down_right.start()
            up_right.wait_recv()
            to_child[0] = jnp.dot(child[:, right_part], cross[0, 0], preferred_element_type=F32).astype(BF16)
            down_left.start()

    load_diag.wait()
    product[...] = jnp.dot(rhs[...], diag[...], preferred_element_type=F32)
    load_out.wait()
    load_down.wait()

    @pl.when(sends_up)
    def _():
        down_left.wait_recv()
        down_in[...] = jnp.where(node_keep, down_in[...], jnp.zeros_like(down_in))

    @pl.when(is_odd)
    def _():
        to_left = cross_sum[0, :, narrow] + jnp.dot(down_in[...], down[0, 0, :, narrow], preferred_element_type=F32)
        to_child[0, :, narrow] = to_left.astype(BF16)
        leaf_left.start()
        to_right = cross_sum[1, :, narrow] + jnp.dot(down_in[...], down[1, 0, :, narrow], preferred_element_type=F32)
        leaf_down[...] = to_right.astype(BF16)

    @pl.when(jnp.logical_and(is_upper, sends_up))
    def _():
        to_left = cross_sum[0] + jnp.dot(down_in[...], down[0, 0], preferred_element_type=F32)
        to_child[0] = to_left.astype(BF16)
        down_left.start()
        to_right = cross_sum[1] + jnp.dot(down_in[...], down[1, 0], preferred_element_type=F32)
        to_child[1] = to_right.astype(BF16)
        down_right.start()

    @pl.when(jnp.logical_not(is_odd))
    def _():
        leaf_left.wait_recv()

    kept = jnp.where(leaf_keep, leaf_down[...], jnp.zeros_like(leaf_down))
    product[...] += jnp.dot(kept, leaf_out[...], preferred_element_type=F32)

    @pl.when(is_leaf_only)
    def _():
        load_up.wait()
        load_cross.wait()

    @pl.when(is_root)
    def _():
        pass

    @pl.when(jnp.logical_not(is_odd))
    def _():
        leaf_up.wait_send()

    @pl.when(is_odd)
    def _():
        leaf_left.wait_send()

    @pl.when(sends_up)
    def _():
        up_left.wait_send()

    @pl.when(is_upper)
    def _():
        down_left.wait_send()
        down_right.wait_send()


def on_device(levels, row_len, rhs, diag_blocks, leaf_in, leaf_out, up_maps, cross_maps, down_maps, node_rank):
    rows, leaf = rhs.shape
    width, leaf_width = up_maps.shape[-1], leaf_in.shape[1]
    operands = (rhs, diag_blocks, leaf_in, leaf_out, up_maps, cross_maps, down_maps)
    return pl.pallas_call(
        functools.partial(kernel, row_len, levels),
        out_shape=jax.ShapeDtypeStruct((rows, leaf), F32),
        in_specs=[pl.BlockSpec(memory_space=pl.ANY)] * 8,
        out_specs=pl.BlockSpec(memory_space=pltpu.VMEM),
        scratch_shapes=[pltpu.VMEM(each.shape, each.dtype) for each in operands]
        + [
            pltpu.SMEM(node_rank.shape, node_rank.dtype),
            pltpu.VMEM((rows, leaf_width), BF16),
            pltpu.VMEM((rows, width), BF16),
            pltpu.VMEM((rows, 2 * width), BF16),
            pltpu.VMEM((2, rows, width), F32),
            pltpu.VMEM((2, rows, width), BF16),
            pltpu.VMEM((rows, width), BF16),
            pltpu.VMEM((rows, leaf_width), BF16),
            pltpu.SemaphoreType.DMA((8,)),
            pltpu.SemaphoreType.DMA((4,)),
            pltpu.SemaphoreType.DMA((4,)),
        ],
        compiler_params=pltpu.CompilerParams(
            collective_id=0, has_side_effects=True, vmem_limit_bytes=60 * 2**20
        ),
    )(*operands, node_rank)


def solution(mesh):
    row_len = mesh.shape["ty"]
    levels = (mesh.shape["tx"] * row_len).bit_length() - 1
    in_specs = (
        P(None, ("tx", "ty")),
        P(("tx", "ty"), None),
        P(("tx", "ty"), None),
        P(("tx", "ty"), None),
        P(None, ("tx", "ty"), None, None),
        P(None, ("tx", "ty"), None, None),
        P(None, ("tx", "ty"), None, None),
        P(("tx", "ty"), None),
    )
    return jax.shard_map(
        functools.partial(on_device, levels, row_len),
        mesh=mesh,
        in_specs=in_specs,
        out_specs=P(None, ("tx", "ty")),
        check_vma=False,
    )
```

```python
import functools

import jax
import jax.numpy as jnp
from jax import lax
from jax.experimental import pallas as pl
from jax.experimental.pallas import tpu as pltpu
from jax.sharding import PartitionSpec as P

MESH = pl.DeviceIdType.MESH
F32 = jnp.float32
BF16 = jnp.bfloat16
N_Z, N_CORE, N_X, N_Y = 16, 2, 4, 4


def kernel(
    rhs_hbm,
    diag_hbm,
    in_hbm,
    out_hbm,
    up_hbm,
    cross_hbm,
    down_hbm,
    rank_hbm,
    product,
    rhs,
    diag,
    leaf_in,
    leaf_out,
    up,
    cross,
    down,
    rank,
    leaf_coef,
    coef,
    child,
    cross_sum,
    path_coef,
    outgoing,
    map_a,
    map_b,
    map_c,
    map_d,
    leaf_map2,
    leaf_map1,
    cross_a,
    cross_b,
    leaf_cross2,
    leaf_cross1,
    above,
    leaf_above,
    parts7,
    parts8,
    load_sem,
    send_sem,
    recv_sem,
):
    rows, width = coef.shape
    leaf_width = leaf_coef.shape[1]
    tx, ty = lax.axis_index("tx"), lax.axis_index("ty")
    z, core = tx // N_CORE, tx % N_CORE
    x, y = ty // N_Y, ty % N_Y

    def at(z, core, x, y):
        return (z * N_CORE + core, x * N_Y + y)

    both = jnp.logical_and
    on_line = ty == 0
    on_top = both(on_line, core == 0)
    is_p1 = y % 2 == 1
    is_p2 = y == 2
    is_p3 = both(y == 0, x % 2 == 1)
    is_p4 = both(y == 0, x == 2)
    is_gate = both(on_line, core == 1)
    is_p6 = both(on_top, z % 2 == 1)
    is_p7 = both(on_top, z % 4 == 2)
    is_p8 = both(on_top, z % 8 == 4)
    is_p9 = both(on_top, z == 8)
    is_even = y % 2 == 0

    loads = [
        pltpu.make_async_copy(source, target, load_sem.at[n])
        for n, (source, target) in enumerate(
            (
                (rhs_hbm, rhs),
                (in_hbm, leaf_in),
                (rank_hbm, rank),
                (up_hbm, up),
                (cross_hbm, cross),
                (down_hbm, down),
                (diag_hbm, diag),
                (out_hbm, leaf_out),
            )
        )
    ]
    load_rhs, load_in, load_rank, load_up, load_cross, load_down, load_diag, load_out = loads
    for load in loads:
        load.start()

    x_odd = x // 2 * 2 + 1
    z_odd, z_seven, z_eight = z // 2 * 2 + 1, z // 4 * 4 + 2, z // 8 * 8 + 4
    z_far = (z + N_Z // 2) % N_Z
    z_far_half = z_far // 8 * 8
    leaf_peer = at(z, core, x, y + 1)
    left_leaf = at(z, core, x, y - 1)
    column = [at(z, core, x, k) for k in range(N_Y)]
    left_column = [at(z, core, x - 1, k) for k in range(N_Y)]
    my_p3 = at(z, core, x_odd, 0)
    p3s = [at(z, core, 1, 0), at(z, core, 3, 0)]
    p4 = at(z, core, 2, 0)
    gate = at(z, 1, 0, 0)
    p3s_of_gate = [at(z, c, k, 0) for c in range(N_CORE) for k in (1, 3)]
    p4s_of_gate = [at(z, c, 2, 0) for c in range(N_CORE)]
    p6, p7, p8 = at(z_odd, 0, 0, 0), at(z_seven, 0, 0, 0), at(z_eight, 0, 0, 0)
    gates_of_p6 = [at(z_odd - 1, 1, 0, 0), at(z_odd, 1, 0, 0)]
    gates_of_p7 = [at(z_seven - 2 + k, 1, 0, 0) for k in range(4)]
    p6s_of_p7 = [at(z_seven - 1, 0, 0, 0), at(z_seven + 1, 0, 0, 0)]
    p7s_of_p8 = [at(z_eight - 2, 0, 0, 0), at(z_eight + 2, 0, 0, 0)]
    far_same, far_other = at(z_far, 0, 0, 0), at(z_far_half + 8 - z_far % 8, 0, 0, 0)
    p9 = at(N_Z // 2, 0, 0, 0)
    p7s = [at(k, 0, 0, 0) for k in (2, 6, 10, 14)]

    barrier = pltpu.get_barrier_semaphore()

    def greet(condition, devices):
        @pl.when(condition)
        def _():
            for device in devices:
                pl.semaphore_signal(barrier, inc=1, device_id=device, device_id_type=MESH)

    greet(is_p1, [left_leaf, column[2], my_p3])
    greet(is_p2, [column[1], column[3], my_p3])
    greet(y == 0, [column[1], column[2]])
    greet(both(y == 0, x % 2 == 0), [my_p3])
    greet(is_p3, [at(z, core, x - 1, 2), p4, gate])
    greet(is_p4, p3s)
    greet(is_gate, [*p4s_of_gate, p6, p7])
    greet(is_p6, gates_of_p6)
    greet(is_p7, [*p6s_of_p7, *gates_of_p7, p8, far_same, far_other, p9])
    greet(is_p8, p7s_of_p8)
    sizes = (
        (is_even, 1),
        (y == 1, 2),
        (y == 3, 1),
        (is_p2, 3),
        (both(is_p2, x % 2 == 0), 1),
        (is_p3, 8),
        (is_p4, 3),
        (is_gate, 6),
        (is_p6, 3),
        (is_p7, 7),
        (is_p8, 2),
        (is_p9, 4),
    )
    greeted = sum(condition.astype(jnp.int32) * size for condition, size in sizes)

    def remote(source, target, send, recv, device):
        return pltpu.make_async_remote_copy(
            src_ref=source,
            dst_ref=target,
            send_sem=send_sem.at[send],
            recv_sem=recv_sem.at[recv],
            device_id=device,
            device_id_type=MESH,
        )

    left_part, right_part = pl.ds(0, width), pl.ds(width, width)
    narrow = pl.ds(0, leaf_width)

    leaf_up = remote(leaf_coef, child.at[:, narrow], 0, 0, leaf_peer)
    side = jnp.where(
        is_p1,
        y // 2,
        jnp.where(is_p2, x % 2, jnp.where(is_p3, x // 2, jnp.where(is_p4, core, jnp.where(is_gate, z % 2, jnp.where(is_p6, z // 2 % 2, z // 4 % 2))))),
    )
    steps = ((is_p1, column[2]), (is_p2, my_p3), (is_p3, p4), (is_p4, gate), (is_gate, p6), (is_p6, p7), (is_p7, p8))
    parent = tuple(sum(condition.astype(jnp.int32) * device[k] for condition, device in steps) for k in range(2))
    up_left = remote(coef, child.at[:, left_part], 1, 0, parent)
    up_right = remote(coef, child.at[:, right_part], 1, 1, parent)
    send_cross1 = [remote(cross_sum.at[0, :, narrow], leaf_cross1, 2, 2, left_leaf)]
    send_down1 = [remote(down.at[0, 0, :, narrow], leaf_map1, 3, 3, left_leaf)]
    sides2 = ((0, 0), (1, 0), (3, 1))
    send_cross2 = [remote(cross_sum.at[s], leaf_cross2, 2 + n, 4, column[k]) for n, (k, s) in enumerate(sides2)]
    send_down2 = [remote(down.at[s, 0], leaf_map2, 5 + n, 5, column[k]) for n, (k, s) in enumerate(sides2)]
    send_cross4 = [remote(cross_sum.at[s], cross_a, 2 + s, 11, p3s[s]) for s in range(2)]
    send_down4 = [remote(down.at[s, 0], map_d, 5 + s, 10, p3s[s]) for s in range(2)]
    send_cross6 = [remote(cross_sum.at[s], cross_b, 2 + s, 12, gates_of_p6[s]) for s in range(2)]
    send_up6 = [remote(up.at[s, 0], map_a, 4 + s, 7, gates_of_p6[s]) for s in range(2)]
    send_down6 = [remote(down.at[s, 0], map_c, 6 + s, 9, gates_of_p6[s]) for s in range(2)]
    send_cross7 = [remote(cross_sum.at[k // 2], cross_a, 2 + k, 11, gates_of_p7[k]) for k in range(4)]
    send_up7 = [remote(up.at[k // 2, 0], map_b, 6 + k, 8, gates_of_p7[k]) for k in range(4)]
    send_down7 = [remote(down.at[k // 2, 0], map_d, 10 + k, 10, gates_of_p7[k]) for k in range(4)]
    send_cross8 = [remote(cross_sum.at[s], cross_a, 2 + s, 11, p7s_of_p8[s]) for s in range(2)]
    send_up8 = [remote(up.at[s, 0], map_a, 4 + s, 7, p7s_of_p8[s]) for s in range(2)]
    send_down8 = [remote(down.at[s, 0], map_c, 6 + s, 9, p7s_of_p8[s]) for s in range(2)]
    send_cross9 = [remote(cross.at[1 - k // 2, 0], map_b, 2 + k, 8, p7s[k]) for k in range(4)]
    send_part7 = [remote(path_coef, parts7.at[k], 2, 14 + k, p7) for k in range(4)]
    send_part8 = [
        [remote(path_coef, parts8.at[k], 14, 18 + k, far_same), remote(path_coef, parts8.at[k], 15, 18 + k, far_other)]
        for k in range(2)
    ]
    send_above7 = [remote(outgoing.at[0], above, 16 + k, 13, gates_of_p7[k]) for k in (0, 3, 1, 2)]
    send_above4 = [remote(outgoing.at[k // 2], above, 3 + k, 13, p3s_of_gate[k]) for k in range(4)]
    send_above2_left = [remote(outgoing.at[0], leaf_above, 2 + k, 6, left_column[k]) for k in (2, 1, 3, 0)]
    send_above2_right = [remote(outgoing.at[1], leaf_above, 5 + k, 6, column[k]) for k in (2, 1, 3)]

    def start(copies):
        for copy in copies:
            copy.start()

    def dot(a, b):
        return jnp.dot(a, b, preferred_element_type=F32)

    load_rhs.wait()
    load_in.wait()
    load_rank.wait()
    leaf_rank, node_rank = rank[0, 0], rank[0, 1]
    leaf_keep = lax.broadcasted_iota(jnp.int32, (rows, leaf_width), 1) < leaf_rank
    node_keep = lax.broadcasted_iota(jnp.int32, (rows, width), 1) < node_rank
    leaf_coef[...] = jnp.where(leaf_keep, dot(rhs[...], leaf_in[...]), 0.0).astype(BF16)

    pl.semaphore_wait(barrier, greeted)

    def mask_up():
        keep = lax.broadcasted_iota(jnp.int32, (width, width), 1) < node_rank
        for s in range(2):
            up[s, 0] = jnp.where(keep, up[s, 0], jnp.zeros((width, width), BF16))

    def mask_down():
        keep = lax.broadcasted_iota(jnp.int32, (width, width), 0) < node_rank
        for s in range(2):
            down[s, 0] = jnp.where(keep, down[s, 0], jnp.zeros((width, width), BF16))

    def send_up(summed):
        coef[...] = jnp.where(node_keep, summed, 0.0).astype(BF16)

        @pl.when(side == 0)
        def _():
            up_left.start()

        @pl.when(side == 1)
        def _():
            up_right.start()

    def cross_terms():
        cross_sum[0] = dot(child[:, right_part], cross[0, 0])
        cross_sum[1] = dot(child[:, left_part], cross[1, 0])

    @pl.when(is_even)
    def _():
        leaf_up.start()

    @pl.when(is_p1)
    def _():
        load_up.wait()
        summed = dot(leaf_coef[...], up[1, 0, narrow, :])
        leaf_up.wait_recv()
        send_up(summed + dot(child[:, narrow], up[0, 0, narrow, :]))
        load_cross.wait()
        cross_sum[0, :, narrow] = dot(leaf_coef[...], cross[0, 0, narrow, narrow])
        leaf_cross1[...] = dot(child[:, narrow], cross[1, 0, narrow, narrow])
        start(send_cross1)
        load_down.wait()
        mask_down()
        start(send_down1)
        leaf_map1[...] = down[1, 0, :, narrow]

    def lift():
        up_left.wait_recv()
        summed = dot(child[:, left_part], up[0, 0])
        up_right.wait_recv()
        send_up(summed + dot(child[:, right_part], up[1, 0]))

    @pl.when(is_p2)
    def _():
        load_up.wait()
        lift()
        load_cross.wait()
        cross_terms()
        start(send_cross2)
        leaf_cross2[...] = cross_sum[1]
        load_down.wait()
        mask_down()
        start(send_down2)
        leaf_map2[...] = down[1, 0]

    @pl.when(is_p3)
    def _():
        load_up.wait()
        lift()
        load_cross.wait()
        cross_terms()
        load_down.wait()
        mask_down()

    @pl.when(is_p4)
    def _():
        load_up.wait()
        lift()
        load_cross.wait()
        cross_terms()
        start(send_cross4)
        load_down.wait()
        mask_down()
        start(send_down4)

    @pl.when(is_gate)
    def _():
        load_up.wait()
        load_cross.wait()
        load_down.wait()
        mask_down()
        lift()
        send_up6[0].wait_recv()
        path_coef[...] = dot(coef[...], map_a[...]).astype(BF16)
        send_up7[0].wait_recv()
        path_coef[...] = dot(path_coef[...], map_b[...]).astype(BF16)
        for k in range(4):

            @pl.when(z % 4 == k)
            def _():
                send_part7[k].start()

        cross_terms()

    @pl.when(is_p6)
    def _():
        load_up.wait()
        mask_up()
        start(send_up6)
        load_cross.wait()
        load_down.wait()
        mask_down()
        for copy in send_up6:
            copy.wait_send()
        start(send_down6)
        lift()
        cross_terms()
        start(send_cross6)

    @pl.when(is_p7)
    def _():
        load_up.wait()
        mask_up()
        start(send_up7)
        load_cross.wait()
        load_down.wait()
        mask_down()
        for copy in send_up7:
            copy.wait_send()
        start(send_down7)
        summed = jnp.zeros((rows, width), F32)
        for k in range(4):
            send_part7[k].wait_recv()
            summed += parts7[k].astype(F32)
        send_up(summed)
        send_up8[0].wait_recv()
        part = dot(coef[...], map_a[...]).astype(BF16)
        send_cross9[0].wait_recv()
        path_coef[...] = dot(part, map_b[...]).astype(BF16)
        for k in range(2):

            @pl.when(z // 4 % 2 == k)
            def _():
                start(send_part8[k])

        up_left.wait_recv()
        up_right.wait_recv()
        cross_terms()
        start(send_cross7)

    @pl.when(is_p8)
    def _():
        load_up.wait()
        mask_up()
        start(send_up8)
        load_cross.wait()
        load_down.wait()
        mask_down()
        for copy in send_up8:
            copy.wait_send()
        start(send_down8)
        up_left.wait_recv()
        up_right.wait_recv()
        cross_terms()
        start(send_cross8)

    @pl.when(both(on_top, z % 8 == 0))
    def _():
        load_up.wait()
        load_cross.wait()
        load_down.wait()

    @pl.when(is_p9)
    def _():
        start(send_cross9)

    load_diag.wait()
    product[...] = dot(rhs[...], diag[...])
    load_out.wait()

    @pl.when(is_p7)
    def _():
        send_down8[0].wait_recv()
        send_cross8[0].wait_recv()
        for k in range(2):
            send_part8[k][0].wait_recv()
        crossed = (parts8[0].astype(F32) + parts8[1].astype(F32)).astype(BF16)
        outgoing[0] = (cross_a[...] + dot(crossed, map_c[...])).astype(BF16)
        start(send_above7)

    @pl.when(is_gate)
    def _():
        send_down7[0].wait_recv()
        send_cross7[0].wait_recv()
        send_down6[0].wait_recv()
        send_cross6[0].wait_recv()
        send_above7[0].wait_recv()
        six = (cross_a[...] + dot(above[...], map_d[...])).astype(BF16)
        five = (cross_b[...] + dot(six, map_c[...])).astype(BF16)
        for s in range(2):
            outgoing[s] = (cross_sum[s] + dot(five, down[s, 0])).astype(BF16)
            start(send_above4[2 * s : 2 * s + 2])

    @pl.when(is_p3)
    def _():
        send_down4[0].wait_recv()
        send_cross4[0].wait_recv()
        send_above4[0].wait_recv()
        three = (cross_a[...] + dot(above[...], map_d[...])).astype(BF16)
        outgoing[0] = (cross_sum[0] + dot(three, down[0, 0])).astype(BF16)
        start(send_above2_left)
        outgoing[1] = (cross_sum[1] + dot(three, down[1, 0])).astype(BF16)
        start(send_above2_right)
        leaf_above[...] = outgoing[1]

    @pl.when(is_even)
    def _():
        send_cross1[0].wait_recv()
        send_down1[0].wait_recv()

    @pl.when(jnp.logical_not(is_p2))
    def _():
        send_cross2[0].wait_recv()
        send_down2[0].wait_recv()

    @pl.when(jnp.logical_not(is_p3))
    def _():
        send_above2_left[0].wait_recv()

    one = (leaf_cross2[...] + dot(leaf_above[...], leaf_map2[...])).astype(BF16)
    zero = (leaf_cross1[...] + dot(one, leaf_map1[...])).astype(BF16)
    zero = jnp.where(leaf_keep, zero, jnp.zeros_like(zero))
    product[...] += dot(zero, leaf_out[...])

    def sent(condition, copies):
        @pl.when(condition)
        def _():
            for copy in copies:
                copy.wait_send()

    sent(is_even, [leaf_up])
    sent(is_p1, [up_left, *send_cross1, *send_down1])
    sent(is_p2, [up_left, *send_cross2, *send_down2])
    sent(is_p3, [up_left, *send_above2_left, *send_above2_right])
    sent(is_p4, [up_left, *send_cross4, *send_down4])
    sent(is_gate, [up_left, send_part7[0], *send_above4])
    sent(is_p6, [up_left, *send_down6, *send_cross6])
    sent(is_p7, [up_left, *send_down7, *send_part8[0], *send_cross7, *send_above7])
    sent(is_p8, [*send_down8, *send_cross8])
    sent(is_p9, send_cross9)


def on_device(rhs, diag_blocks, leaf_in, leaf_out, up_maps, cross_maps, down_maps, node_rank):
    rows, leaf = rhs.shape
    width, leaf_width = up_maps.shape[-1], leaf_in.shape[1]
    operands = (rhs, diag_blocks, leaf_in, leaf_out, up_maps, cross_maps, down_maps)

    def vector(*lead, kind=BF16, columns=width):
        return pltpu.VMEM((*lead, rows, columns), kind)

    full_map = pltpu.VMEM((width, width), BF16)
    return pl.pallas_call(
        kernel,
        out_shape=jax.ShapeDtypeStruct((rows, leaf), F32),
        in_specs=[pl.BlockSpec(memory_space=pl.ANY)] * 8,
        out_specs=pl.BlockSpec(memory_space=pltpu.VMEM),
        scratch_shapes=[pltpu.VMEM(each.shape, each.dtype) for each in operands]
        + [
            pltpu.SMEM(node_rank.shape, node_rank.dtype),
            vector(columns=leaf_width),
            vector(),
            vector(columns=2 * width),
            vector(2, kind=F32),
            vector(),
            vector(2),
            full_map,
            full_map,
            full_map,
            full_map,
            full_map,
            pltpu.VMEM((width, leaf_width), BF16),
            vector(kind=F32),
            vector(kind=F32),
            vector(kind=F32),
            vector(kind=F32, columns=leaf_width),
            vector(),
            vector(),
            vector(4),
            vector(2),
            pltpu.SemaphoreType.DMA((8,)),
            pltpu.SemaphoreType.DMA((20,)),
            pltpu.SemaphoreType.DMA((20,)),
        ],
        compiler_params=pltpu.CompilerParams(
            collective_id=0, has_side_effects=True, vmem_limit_bytes=60 * 2**20
        ),
    )(*operands, node_rank)


def solution(mesh):
    assert mesh.shape["tx"] == N_Z * N_CORE and mesh.shape["ty"] == N_X * N_Y
    in_specs = (
        P(None, ("tx", "ty")),
        P(("tx", "ty"), None),
        P(("tx", "ty"), None),
        P(("tx", "ty"), None),
        P(None, ("tx", "ty"), None, None),
        P(None, ("tx", "ty"), None, None),
        P(None, ("tx", "ty"), None, None),
        P(("tx", "ty"), None),
    )
    return jax.shard_map(
        on_device, mesh=mesh, in_specs=in_specs, out_specs=P(None, ("tx", "ty")), check_vma=False
    )
```

```python
import functools

import jax
import jax.numpy as jnp
from jax import lax
from jax.experimental import pallas as pl
from jax.experimental.pallas import tpu as pltpu
from jax.sharding import PartitionSpec as P

MESH = pl.DeviceIdType.MESH
F32 = jnp.float32
BF16 = jnp.bfloat16
N_Z, N_CORE, N_X, N_Y = 16, 2, 4, 4


def kernel(
    rhs_hbm,
    diag_hbm,
    in_hbm,
    out_hbm,
    up_hbm,
    cross_hbm,
    down_hbm,
    rank_hbm,
    product,
    rhs,
    diag,
    leaf_in,
    leaf_out,
    up,
    cross,
    down,
    rank,
    leaf_coef,
    coef,
    child,
    cross_sum,
    path_coef,
    outgoing,
    map_a,
    map_b,
    map_c,
    map_d,
    leaf_map2,
    leaf_map1,
    cross_a,
    cross_b,
    leaf_cross2,
    leaf_cross1,
    above,
    leaf_above,
    parts7,
    parts8,
    load_sem,
    send_sem,
    recv_sem,
    go_sem,
):
    rows, width = coef.shape
    leaf_width = leaf_coef.shape[1]
    tx, ty = lax.axis_index("tx"), lax.axis_index("ty")
    z, core = tx // N_CORE, tx % N_CORE
    x, y = ty // N_Y, ty % N_Y

    def at(z, core, x, y):
        return (z * N_CORE + core, x * N_Y + y)

    both = jnp.logical_and
    on_line = ty == 0
    on_top = both(on_line, core == 0)
    is_p1 = y % 2 == 1
    is_p2 = y == 2
    is_p3 = both(y == 0, x % 2 == 1)
    is_p4 = both(y == 0, x == 2)
    is_gate = both(on_line, core == 1)
    is_p6 = both(on_top, z % 2 == 1)
    is_p7 = both(on_top, z % 4 == 2)
    is_p8 = both(on_top, z % 8 == 4)
    is_p9 = both(on_top, z == 8)
    is_even = y % 2 == 0

    loads = [
        pltpu.make_async_copy(source, target, load_sem.at[n])
        for n, (source, target) in enumerate(
            (
                (rhs_hbm, rhs),
                (in_hbm, leaf_in),
                (rank_hbm, rank),
                (up_hbm, up),
                (cross_hbm, cross),
                (down_hbm, down),
                (diag_hbm, diag),
                (out_hbm, leaf_out),
            )
        )
    ]
    load_rhs, load_in, load_rank, load_up, load_cross, load_down, load_diag, load_out = loads
    for load in loads[:3]:
        load.start()

    x_odd = x // 2 * 2 + 1
    z_odd, z_seven, z_eight = z // 2 * 2 + 1, z // 4 * 4 + 2, z // 8 * 8 + 4
    z_far = (z + N_Z // 2) % N_Z
    z_far_half = z_far // 8 * 8
    leaf_peer = at(z, core, x, y + 1)
    left_leaf = at(z, core, x, y - 1)
    column = [at(z, core, x, k) for k in range(N_Y)]
    left_column = [at(z, core, x - 1, k) for k in range(N_Y)]
    my_p3 = at(z, core, x_odd, 0)
    p3s = [at(z, core, 1, 0), at(z, core, 3, 0)]
    p4 = at(z, core, 2, 0)
    gate = at(z, 1, 0, 0)
    p3s_of_gate = [at(z, c, k, 0) for c in range(N_CORE) for k in (1, 3)]
    p4s_of_gate = [at(z, c, 2, 0) for c in range(N_CORE)]
    p6, p7, p8 = at(z_odd, 0, 0, 0), at(z_seven, 0, 0, 0), at(z_eight, 0, 0, 0)
    gates_of_p6 = [at(z_odd - 1, 1, 0, 0), at(z_odd, 1, 0, 0)]
    gates_of_p7 = [at(z_seven - 2 + k, 1, 0, 0) for k in range(4)]
    p6s_of_p7 = [at(z_seven - 1, 0, 0, 0), at(z_seven + 1, 0, 0, 0)]
    p7s_of_p8 = [at(z_eight - 2, 0, 0, 0), at(z_eight + 2, 0, 0, 0)]
    far_same, far_other = at(z_far, 0, 0, 0), at(z_far_half + 8 - z_far % 8, 0, 0, 0)
    p9 = at(N_Z // 2, 0, 0, 0)
    p7s = [at(k, 0, 0, 0) for k in (2, 6, 10, 14)]

    barrier = pltpu.get_barrier_semaphore()

    def greet(condition, devices):
        @pl.when(condition)
        def _():
            for device in devices:
                pl.semaphore_signal(barrier, inc=1, device_id=device, device_id_type=MESH)

    def collector(z, core, x):
        return at(z, core, x, 1)

    x_even = x % 2 == 0
    next_p3 = collector(z, core, x_odd)
    greet(is_p1, [left_leaf])
    greet(y == 1, [column[3]])
    greet(both(y == 1, x_even), [next_p3])
    greet(y == 3, [next_p3])
    greet(is_p2, [column[1], column[3], next_p3])
    greet(y == 0, [column[1], column[3]])
    greet(both(y == 0, x_even), [next_p3])
    greet(is_p3, [at(z, core, x - 1, 3), collector(z, core, 2), collector(z, 1, 0)])
    greet(is_p4, [collector(z, core, 1), collector(z, core, 3)])
    greet(is_gate, [collector(z, c, 2) for c in range(N_CORE)] + [collector(z_odd, 0, 0), collector(z_seven, 0, 0)])
    greet(both(is_gate, z % 4 == 0), [collector(z + 1, 1, 0)])
    greet(is_p6, [collector(z_odd - 1, 1, 0), collector(z_odd, 1, 0)])
    greet(
        is_p7,
        [collector(z_seven - 1, 0, 0), collector(z_seven + 1, 0, 0)]
        + [collector(z_seven - 2 + k, 1, 0) for k in range(4)]
        + [collector(z_eight, 0, 0), collector(N_Z // 2, 0, 0)],
    )
    greet(is_p8, [collector(z_eight - 2, 0, 0), collector(z_eight + 2, 0, 0)])
    sizes = (
        (is_even, 1),
        (y == 3, 3),
        (both(y == 3, x_even), 1),
        (y == 1, 2),
        (both(y == 1, x % 2 == 1), 7),
        (both(y == 1, x == 2), 3),
        (both(ty == 1, core == 1), 6),
        (both(both(ty == 1, core == 1), z % 4 == 1), 1),
        (both(both(ty == 1, core == 0), z % 2 == 1), 3),
        (both(both(ty == 1, core == 0), z % 4 == 2), 5),
        (both(both(ty == 1, core == 0), z % 8 == 4), 2),
        (both(both(ty == 1, core == 0), z == 8), 4),
    )
    greeted = sum(condition.astype(jnp.int32) * size for condition, size in sizes)
    for load in loads[3:]:
        load.start()

    def remote(source, target, send, recv, device):
        return pltpu.make_async_remote_copy(
            src_ref=source,
            dst_ref=target,
            send_sem=send_sem.at[send],
            recv_sem=recv_sem.at[recv],
            device_id=device,
            device_id_type=MESH,
        )

    left_part, right_part = pl.ds(0, width), pl.ds(width, width)
    narrow = pl.ds(0, leaf_width)

    leaf_up = remote(leaf_coef, child.at[:, narrow], 0, 0, leaf_peer)
    side = jnp.where(
        is_p1,
        y // 2,
        jnp.where(is_p2, x % 2, jnp.where(is_p3, x // 2, jnp.where(is_p4, core, jnp.where(is_gate, z % 2, jnp.where(is_p6, z // 2 % 2, z // 4 % 2))))),
    )
    steps = ((is_p1, column[2]), (is_p2, my_p3), (is_p3, p4), (is_p4, gate), (is_gate, p6), (is_p6, p7), (is_p7, p8))
    parent = tuple(sum(condition.astype(jnp.int32) * device[k] for condition, device in steps) for k in range(2))
    up_left = remote(coef, child.at[:, left_part], 1, 0, parent)
    up_right = remote(coef, child.at[:, right_part], 1, 1, parent)
    send_cross1 = [remote(cross_sum.at[0, :, narrow], leaf_cross1, 2, 2, left_leaf)]
    send_down1 = [remote(down.at[0, 0, :, narrow], leaf_map1, 3, 3, left_leaf)]
    sides2 = ((0, 0), (1, 0), (3, 1))
    send_cross2 = [remote(cross_sum.at[s], leaf_cross2, 2 + n, 4, column[k]) for n, (k, s) in enumerate(sides2)]
    send_down2 = [remote(down.at[s, 0], leaf_map2, 5 + n, 5, column[k]) for n, (k, s) in enumerate(sides2)]
    send_cross4 = [remote(cross_sum.at[s], cross_a, 2 + s, 11, p3s[s]) for s in range(2)]
    send_down4 = [remote(down.at[s, 0], map_d, 5 + s, 10, p3s[s]) for s in range(2)]
    send_cross6 = [remote(cross_sum.at[s], cross_b, 2 + s, 12, gates_of_p6[s]) for s in range(2)]
    send_up6 = [remote(up.at[s, 0], map_a, 4 + s, 7, gates_of_p6[s]) for s in range(2)]
    send_down6 = [remote(down.at[s, 0], map_c, 6 + s, 9, gates_of_p6[s]) for s in range(2)]
    send_cross7 = [remote(cross_sum.at[k // 2], cross_a, 2 + k, 11, gates_of_p7[k]) for k in range(4)]
    send_up7 = [remote(up.at[k // 2, 0], map_b, 6 + k, 8, gates_of_p7[k]) for k in range(4)]
    send_down7 = [remote(down.at[k // 2, 0], map_d, 10 + k, 10, gates_of_p7[k]) for k in range(4)]
    pass_up7 = remote(map_b, map_b, 7, 8, at(z - 1, 1, 0, 0))
    pass_down7 = remote(map_d, map_d, 8, 10, at(z - 1, 1, 0, 0))
    send_cross8 = [remote(cross_sum.at[s], cross_a, 2 + s, 11, p7s_of_p8[s]) for s in range(2)]
    send_up8 = [remote(up.at[s, 0], map_a, 4 + s, 7, p7s_of_p8[s]) for s in range(2)]
    send_down8 = [remote(down.at[s, 0], map_c, 6 + s, 9, p7s_of_p8[s]) for s in range(2)]
    send_cross9 = [remote(cross.at[1 - k // 2, 0], map_b, 2 + k, 8, p7s[k]) for k in range(4)]
    send_part7 = [remote(path_coef, parts7.at[k], 2, 14 + k, p7) for k in range(4)]
    send_part8 = [
        [remote(path_coef, parts8.at[k], 14, 18 + k, far_same), remote(path_coef, parts8.at[k], 15, 18 + k, far_other)]
        for k in range(2)
    ]
    send_above7 = [remote(outgoing.at[0], above, 16 + k, 13, gates_of_p7[k]) for k in (0, 3, 1, 2)]
    send_above4 = [remote(outgoing.at[k // 2], above, 3 + k, 13, p3s_of_gate[k]) for k in range(4)]
    send_above2_left = [remote(outgoing.at[0], leaf_above, 2 + k, 6, left_column[k]) for k in (2, 1, 3, 0)]
    send_above2_right = [remote(outgoing.at[1], leaf_above, 5 + k, 6, column[k]) for k in (2, 1, 3)]

    def start(copies):
        for copy in copies:
            copy.start()

    def dot(a, b):
        return jnp.dot(a, b, preferred_element_type=F32)

    load_rhs.wait()
    load_in.wait()
    load_rank.wait()
    leaf_rank, node_rank = rank[0, 0], rank[0, 1]
    leaf_keep = lax.broadcasted_iota(jnp.int32, (rows, leaf_width), 1) < leaf_rank
    node_keep = lax.broadcasted_iota(jnp.int32, (rows, width), 1) < node_rank
    leaf_coef[...] = jnp.where(leaf_keep, dot(rhs[...], leaf_in[...]), 0.0).astype(BF16)

    pl.semaphore_wait(barrier, greeted)

    @pl.when(is_p1)
    def _():
        pl.semaphore_signal(go_sem, inc=1, device_id=left_leaf, device_id_type=MESH)

    def mask_up():
        keep = lax.broadcasted_iota(jnp.int32, (width, width), 1) < node_rank
        for s in range(2):
            up[s, 0] = jnp.where(keep, up[s, 0], jnp.zeros((width, width), BF16))

    def mask_down():
        keep = lax.broadcasted_iota(jnp.int32, (width, width), 0) < node_rank
        for s in range(2):
            down[s, 0] = jnp.where(keep, down[s, 0], jnp.zeros((width, width), BF16))

    def send_up(summed, waits=False):
        coef[...] = jnp.where(node_keep, summed, 0.0).astype(BF16)
        if waits:
            pl.semaphore_wait(go_sem, 1)

        @pl.when(side == 0)
        def _():
            up_left.start()

        @pl.when(side == 1)
        def _():
            up_right.start()

    def cross_terms():
        cross_sum[0] = dot(child[:, right_part], cross[0, 0])
        cross_sum[1] = dot(child[:, left_part], cross[1, 0])

    @pl.when(is_even)
    def _():
        leaf_up.start()

    @pl.when(on_line)
    def _():
        pl.semaphore_wait(go_sem, 1)

    @pl.when(is_p1)
    def _():
        load_up.wait()
        summed = dot(leaf_coef[...], up[1, 0, narrow, :])
        leaf_up.wait_recv()
        send_up(summed + dot(child[:, narrow], up[0, 0, narrow, :]))
        load_cross.wait()
        cross_sum[0, :, narrow] = dot(leaf_coef[...], cross[0, 0, narrow, narrow])
        leaf_cross1[...] = dot(child[:, narrow], cross[1, 0, narrow, narrow])
        start(send_cross1)
        load_down.wait()
        mask_down()
        start(send_down1)
        leaf_map1[...] = down[1, 0, :, narrow]

    def lift(waits=True):
        up_left.wait_recv()
        summed = dot(child[:, left_part], up[0, 0])
        up_right.wait_recv()
        send_up(summed + dot(child[:, right_part], up[1, 0]), waits)

    @pl.when(is_p2)
    def _():
        load_up.wait()
        lift()
        load_cross.wait()
        cross_terms()
        start(send_cross2)
        leaf_cross2[...] = cross_sum[1]
        load_down.wait()
        mask_down()
        start(send_down2)
        leaf_map2[...] = down[1, 0]

    @pl.when(is_p3)
    def _():
        load_up.wait()
        lift()
        load_cross.wait()
        cross_terms()
        load_down.wait()
        mask_down()

    @pl.when(is_p4)
    def _():
        load_up.wait()
        lift()
        load_cross.wait()
        cross_terms()
        start(send_cross4)
        load_down.wait()
        mask_down()
        start(send_down4)

    @pl.when(is_gate)
    def _():
        load_up.wait()
        load_cross.wait()
        load_down.wait()
        mask_down()
        send_up7[0].wait_recv()

        @pl.when(z % 4 == 1)
        def _():
            pass_up7.start()

        lift(waits=False)
        send_up6[0].wait_recv()
        path_coef[...] = dot(coef[...], map_a[...]).astype(BF16)
        path_coef[...] = dot(path_coef[...], map_b[...]).astype(BF16)
        for k in range(4):

            @pl.when(z % 4 == k)
            def _():
                send_part7[k].start()

        cross_terms()
        send_down7[0].wait_recv()

        @pl.when(z % 4 == 1)
        def _():
            pass_down7.start()

    @pl.when(is_p6)
    def _():
        load_up.wait()
        mask_up()
        start(send_up6)
        load_cross.wait()
        load_down.wait()
        mask_down()
        for copy in send_up6:
            copy.wait_send()
        start(send_down6)
        lift(waits=False)
        cross_terms()
        start(send_cross6)

    @pl.when(is_p7)
    def _():
        load_up.wait()
        mask_up()
        start(send_up7[1:])
        load_cross.wait()
        load_down.wait()
        mask_down()
        for copy in send_up7[1:]:
            copy.wait_send()
        start(send_down7[1:])
        summed = jnp.zeros((rows, width), F32)
        for k in range(4):
            send_part7[k].wait_recv()
            summed += parts7[k].astype(F32)
        send_up(summed)
        send_up8[0].wait_recv()
        part = dot(coef[...], map_a[...]).astype(BF16)
        send_cross9[0].wait_recv()
        path_coef[...] = dot(part, map_b[...]).astype(BF16)
        for k in range(2):

            @pl.when(z // 4 % 2 == k)
            def _():
                start(send_part8[k])

        up_left.wait_recv()
        up_right.wait_recv()
        cross_terms()
        start(send_cross7)

    @pl.when(is_p8)
    def _():
        load_up.wait()
        mask_up()
        start(send_up8)
        load_cross.wait()
        load_down.wait()
        mask_down()
        for copy in send_up8:
            copy.wait_send()
        start(send_down8)
        up_left.wait_recv()
        up_right.wait_recv()
        cross_terms()
        start(send_cross8)

    @pl.when(both(on_top, z % 8 == 0))
    def _():
        load_up.wait()
        load_cross.wait()
        load_down.wait()

    @pl.when(is_p9)
    def _():
        start(send_cross9)

    load_diag.wait()
    product[...] = dot(rhs[...], diag[...])
    load_out.wait()

    @pl.when(is_p7)
    def _():
        send_down8[0].wait_recv()
        send_cross8[0].wait_recv()
        for k in range(2):
            send_part8[k][0].wait_recv()
        crossed = (parts8[0].astype(F32) + parts8[1].astype(F32)).astype(BF16)
        outgoing[0] = (cross_a[...] + dot(crossed, map_c[...])).astype(BF16)
        start(send_above7)

    @pl.when(is_gate)
    def _():
        send_cross7[0].wait_recv()
        send_down6[0].wait_recv()
        send_cross6[0].wait_recv()
        send_above7[0].wait_recv()
        six = (cross_a[...] + dot(above[...], map_d[...])).astype(BF16)
        five = (cross_b[...] + dot(six, map_c[...])).astype(BF16)
        for s in range(2):
            outgoing[s] = (cross_sum[s] + dot(five, down[s, 0])).astype(BF16)
            start(send_above4[2 * s : 2 * s + 2])

    @pl.when(is_p3)
    def _():
        send_down4[0].wait_recv()
        send_cross4[0].wait_recv()
        send_above4[0].wait_recv()
        three = (cross_a[...] + dot(above[...], map_d[...])).astype(BF16)
        outgoing[0] = (cross_sum[0] + dot(three, down[0, 0])).astype(BF16)
        start(send_above2_left)
        outgoing[1] = (cross_sum[1] + dot(three, down[1, 0])).astype(BF16)
        start(send_above2_right)
        leaf_above[...] = outgoing[1]

    @pl.when(is_even)
    def _():
        send_cross1[0].wait_recv()
        send_down1[0].wait_recv()

    @pl.when(jnp.logical_not(is_p2))
    def _():
        send_cross2[0].wait_recv()
        send_down2[0].wait_recv()

    @pl.when(jnp.logical_not(is_p3))
    def _():
        send_above2_left[0].wait_recv()

    one = (leaf_cross2[...] + dot(leaf_above[...], leaf_map2[...])).astype(BF16)
    zero = (leaf_cross1[...] + dot(one, leaf_map1[...])).astype(BF16)
    zero = jnp.where(leaf_keep, zero, jnp.zeros_like(zero))
    product[...] += dot(zero, leaf_out[...])

    def sent(condition, copies):
        @pl.when(condition)
        def _():
            for copy in copies:
                copy.wait_send()

    sent(is_even, [leaf_up])
    sent(is_p1, [up_left, *send_cross1, *send_down1])
    sent(is_p2, [up_left, *send_cross2, *send_down2])
    sent(is_p3, [up_left, *send_above2_left, *send_above2_right])
    sent(is_p4, [up_left, *send_cross4, *send_down4])
    sent(is_gate, [up_left, send_part7[0], *send_above4])
    sent(both(is_gate, z % 4 == 1), [pass_up7, pass_down7])
    sent(is_p6, [up_left, *send_down6, *send_cross6])
    sent(is_p7, [up_left, *send_down7[1:], *send_part8[0], *send_cross7, *send_above7])
    sent(is_p8, [*send_down8, *send_cross8])
    sent(is_p9, send_cross9)


def on_device(rhs, diag_blocks, leaf_in, leaf_out, up_maps, cross_maps, down_maps, node_rank):
    rows, leaf = rhs.shape
    width, leaf_width = up_maps.shape[-1], leaf_in.shape[1]
    operands = (rhs, diag_blocks, leaf_in, leaf_out, up_maps, cross_maps, down_maps)

    def vector(*lead, kind=BF16, columns=width):
        return pltpu.VMEM((*lead, rows, columns), kind)

    full_map = pltpu.VMEM((width, width), BF16)
    return pl.pallas_call(
        kernel,
        out_shape=jax.ShapeDtypeStruct((rows, leaf), F32),
        in_specs=[pl.BlockSpec(memory_space=pl.ANY)] * 8,
        out_specs=pl.BlockSpec(memory_space=pltpu.VMEM),
        scratch_shapes=[pltpu.VMEM(each.shape, each.dtype) for each in operands]
        + [
            pltpu.SMEM(node_rank.shape, node_rank.dtype),
            vector(columns=leaf_width),
            vector(),
            vector(columns=2 * width),
            vector(2, kind=F32),
            vector(),
            vector(2),
            full_map,
            full_map,
            full_map,
            full_map,
            full_map,
            pltpu.VMEM((width, leaf_width), BF16),
            vector(kind=F32),
            vector(kind=F32),
            vector(kind=F32),
            vector(kind=F32, columns=leaf_width),
            vector(),
            vector(),
            vector(4),
            vector(2),
            pltpu.SemaphoreType.DMA((8,)),
            pltpu.SemaphoreType.DMA((20,)),
            pltpu.SemaphoreType.DMA((20,)),
            pltpu.SemaphoreType.REGULAR,
        ],
        compiler_params=pltpu.CompilerParams(
            collective_id=0, has_side_effects=True, vmem_limit_bytes=60 * 2**20
        ),
    )(*operands, node_rank)


def solution(mesh):
    assert mesh.shape["tx"] == N_Z * N_CORE and mesh.shape["ty"] == N_X * N_Y
    in_specs = (
        P(None, ("tx", "ty")),
        P(("tx", "ty"), None),
        P(("tx", "ty"), None),
        P(("tx", "ty"), None),
        P(None, ("tx", "ty"), None, None),
        P(None, ("tx", "ty"), None, None),
        P(None, ("tx", "ty"), None, None),
        P(("tx", "ty"), None),
    )
    return jax.shard_map(
        on_device, mesh=mesh, in_specs=in_specs, out_specs=P(None, ("tx", "ty")), check_vma=False
    )
```

```python
import functools

import jax
import jax.numpy as jnp
from jax import lax
from jax.experimental import pallas as pl
from jax.experimental.pallas import tpu as pltpu
from jax.sharding import PartitionSpec as P

MESH = pl.DeviceIdType.MESH
F32 = jnp.float32
BF16 = jnp.bfloat16
N_Z, N_CORE, N_X, N_Y = 16, 2, 4, 4


def kernel(
    rhs_hbm,
    diag_hbm,
    in_hbm,
    out_hbm,
    up_hbm,
    cross_hbm,
    down_hbm,
    rank_hbm,
    product,
    rhs,
    diag,
    leaf_in,
    leaf_out,
    up,
    cross,
    down,
    rank,
    leaf_coef,
    coef,
    child,
    cross_sum,
    path_coef,
    outgoing,
    map_a,
    map_b,
    map_c,
    map_d,
    leaf_map2,
    leaf_map1,
    cross_a,
    cross_b,
    cross_c,
    leaf_cross2,
    leaf_cross1,
    above,
    leaf_above,
    parts6,
    parts8,
    load_sem,
    send_sem,
    recv_sem,
    go_sem,
):
    rows, width = coef.shape
    leaf_width = leaf_coef.shape[1]
    tx, ty = lax.axis_index("tx"), lax.axis_index("ty")
    z, core = tx // N_CORE, tx % N_CORE
    x, y = ty // N_Y, ty % N_Y

    def at(z, core, x, y):
        return (z * N_CORE + core, x * N_Y + y)

    both = jnp.logical_and
    on_line = ty == 0
    on_top = both(on_line, core == 0)
    is_p1 = y % 2 == 1
    is_p2 = y == 2
    is_p3 = both(y == 0, x % 2 == 1)
    is_p4 = both(y == 0, x == 2)
    is_gate = both(on_line, core == 1)
    is_p6 = both(on_top, z % 2 == 1)
    is_p7 = both(on_top, z % 4 == 2)
    is_p8 = both(on_top, z % 8 == 4)
    is_p9 = both(on_top, z == 8)
    is_even = y % 2 == 0
    is_first = both(is_gate, z < 4)
    is_left_p8 = both(on_top, z == 4)
    is_right_p8 = both(on_top, z == 12)
    is_right_p7 = both(is_p7, z >= 8)
    is_second_p7 = both(on_top, z == 6)

    loads = [
        pltpu.make_async_copy(source, target, load_sem.at[n])
        for n, (source, target) in enumerate(
            (
                (rhs_hbm, rhs),
                (in_hbm, leaf_in),
                (rank_hbm, rank),
                (up_hbm, up),
                (cross_hbm, cross),
                (down_hbm, down),
                (diag_hbm, diag),
                (out_hbm, leaf_out),
            )
        )
    ]
    load_rhs, load_in, load_rank, load_up, load_cross, load_down, load_diag, load_out = loads
    for load in loads[:3]:
        load.start()

    x_odd = x // 2 * 2 + 1
    z_odd, z_seven, z_eight = z // 2 * 2 + 1, z // 4 * 4 + 2, z // 8 * 8 + 4
    leaf_peer = at(z, core, x, y + 1)
    left_leaf = at(z, core, x, y - 1)
    column = [at(z, core, x, k) for k in range(N_Y)]
    left_column = [at(z, core, x - 1, k) for k in range(N_Y)]
    my_p3 = at(z, core, x_odd, 0)
    p3s = [at(z, core, 1, 0), at(z, core, 3, 0)]
    p4 = at(z, core, 2, 0)
    gate = at(z, 1, 0, 0)
    p3s_of_gate = [at(z, c, k, 0) for c in range(N_CORE) for k in (1, 3)]
    p4s_of_gate = [at(z, c, 2, 0) for c in range(N_CORE)]
    p6, p7, p8 = at(z_odd, 0, 0, 0), at(z_seven, 0, 0, 0), at(z_eight, 0, 0, 0)
    gates_of_p6 = [at(z_odd - 1, 1, 0, 0), at(z_odd, 1, 0, 0)]
    gates_of_p7 = [at(z_seven - 2 + k, 1, 0, 0) for k in range(4)]
    p7s_of_p8 = [at(z_eight - 2, 0, 0, 0), at(z_eight + 2, 0, 0, 0)]
    first_gates = [at(k, 1, 0, 0) for k in range(4)]
    second_p7, left_p8 = at(6, 0, 0, 0), at(4, 0, 0, 0)
    right_p7s = [at(k, 0, 0, 0) for k in (10, 14)]

    barrier = pltpu.get_barrier_semaphore()

    def greet(condition, devices):
        @pl.when(condition)
        def _():
            for device in devices:
                pl.semaphore_signal(barrier, inc=1, device_id=device, device_id_type=MESH)

    def collector(z, core, x):
        return at(z, core, x, 1)

    x_even = x % 2 == 0
    next_p3 = collector(z, core, x_odd)
    greet(is_p1, [left_leaf])
    greet(y == 1, [column[3]])
    greet(both(y == 1, x_even), [next_p3])
    greet(y == 3, [next_p3])
    greet(is_p2, [column[1], column[3], next_p3])
    greet(y == 0, [column[1], column[3]])
    greet(both(y == 0, x_even), [next_p3])
    greet(is_p3, [at(z, core, x - 1, 3), collector(z, core, 2), collector(z, 1, 0)])
    greet(is_p4, [collector(z, core, 1), collector(z, core, 3)])
    greet(is_gate, [collector(z, c, 2) for c in range(N_CORE)] + [collector(z_odd, 0, 0), collector(z_seven, 0, 0)])
    greet(both(is_gate, z % 4 == 0), [collector(z + 1, 1, 0)])
    greet(is_first, [collector(4, 0, 0), collector(8, 0, 0)])
    greet(is_p6, [collector(z_odd - 1, 1, 0), collector(z_odd, 1, 0)])
    greet(is_p7, [collector(z_seven - 2 + k, 1, 0) for k in range(4)])
    greet(both(is_p7, z > 2), [collector(z_eight, 0, 0), collector(8, 0, 0)])
    greet(is_p8, [collector(z_eight - 2, 0, 0), collector(z_eight + 2, 0, 0)])
    greet(is_left_p8, [collector(8, 0, 0)])
    sizes = (
        (is_even, 1),
        (y == 3, 3),
        (both(y == 3, x_even), 1),
        (y == 1, 2),
        (both(y == 1, x % 2 == 1), 7),
        (both(y == 1, x == 2), 3),
        (both(ty == 1, core == 1), 6),
        (both(both(ty == 1, core == 1), z % 4 == 1), 1),
        (both(both(ty == 1, core == 0), z % 2 == 1), 2),
        (both(both(ty == 1, core == 0), z % 4 == 2), 5),
        (both(both(ty == 1, core == 0), z == 4), 5),
        (both(both(ty == 1, core == 0), z == 12), 2),
        (both(both(ty == 1, core == 0), z == 8), 8),
    )
    greeted = sum(condition.astype(jnp.int32) * size for condition, size in sizes)
    for load in loads[3:]:
        load.start()

    def remote(source, target, send, recv, device):
        return pltpu.make_async_remote_copy(
            src_ref=source,
            dst_ref=target,
            send_sem=send_sem.at[send],
            recv_sem=recv_sem.at[recv],
            device_id=device,
            device_id_type=MESH,
        )

    left_part, right_part = pl.ds(0, width), pl.ds(width, width)
    narrow = pl.ds(0, leaf_width)

    leaf_up = remote(leaf_coef, child.at[:, narrow], 0, 0, leaf_peer)
    side = jnp.where(
        is_p1,
        y // 2,
        jnp.where(is_p2, x % 2, jnp.where(is_p3, x // 2, jnp.where(is_p4, core, jnp.where(is_gate, z % 2, z // 4 % 2)))),
    )
    steps = ((is_p1, column[2]), (is_p2, my_p3), (is_p3, p4), (is_p4, gate), (is_gate, p6), (is_p7, p8))
    parent = tuple(sum(condition.astype(jnp.int32) * device[k] for condition, device in steps) for k in range(2))
    up_left = remote(coef, child.at[:, left_part], 1, 0, parent)
    up_right = remote(coef, child.at[:, right_part], 1, 1, parent)
    send_cross1 = [remote(cross_sum.at[0, :, narrow], leaf_cross1, 2, 2, left_leaf)]
    send_down1 = [remote(down.at[0, 0, :, narrow], leaf_map1, 3, 3, left_leaf)]
    sides2 = ((0, 0), (1, 0), (3, 1))
    send_cross2 = [remote(cross_sum.at[s], leaf_cross2, 2 + n, 4, column[k]) for n, (k, s) in enumerate(sides2)]
    send_down2 = [remote(down.at[s, 0], leaf_map2, 5 + n, 5, column[k]) for n, (k, s) in enumerate(sides2)]
    send_cross4 = [remote(cross_sum.at[s], cross_a, 2 + s, 11, p3s[s]) for s in range(2)]
    send_down4 = [remote(down.at[s, 0], map_d, 5 + s, 10, p3s[s]) for s in range(2)]
    send_cross6 = [remote(cross_sum.at[s], cross_b, 2 + s, 12, gates_of_p6[s]) for s in range(2)]
    send_up6 = [remote(up.at[s, 0], map_a, 4 + s, 7, gates_of_p6[s]) for s in range(2)]
    send_down6 = [remote(down.at[s, 0], map_c, 6 + s, 9, gates_of_p6[s]) for s in range(2)]
    send_cross7 = [remote(cross_sum.at[k // 2], cross_a, 2 + k, 11, gates_of_p7[k]) for k in range(4)]
    send_down7 = [remote(down.at[k // 2, 0], map_d, 10 + k, 10, gates_of_p7[k]) for k in range(4)]
    pass_down7 = remote(map_d, map_d, 7, 10, at(z - 1, 1, 0, 0))
    send_cross8 = [remote(cross_sum.at[s], cross_a, 2 + s, 11, p7s_of_p8[s]) for s in range(2)]
    send_cross8_first = [remote(cross_sum.at[0], cross_c, 10 + k, 20, first_gates[k]) for k in range(4)]
    send_up8 = [remote(up.at[s, 0], map_a, 4 + s, 7, p7s_of_p8[s]) for s in range(2)]
    send_down8 = [remote(down.at[s, 0], map_c, 6 + s, 9, p7s_of_p8[s]) for s in range(2)]
    send_down8_first = [remote(down.at[0, 0], map_b, 14 + k, 8, first_gates[k]) for k in range(4)]
    pass_down8 = remote(map_b, map_b, 8, 8, at(z - 1, 1, 0, 0))
    send_cross9 = [remote(cross.at[0, 0], map_b, 2 + k, 8, right_p7s[k]) for k in range(2)]
    send_cross9 += [remote(cross.at[1, 0], map_b, 4, 8, left_p8)]
    send_part6 = [remote(path_coef, parts6.at[k], 2, 14 + k, p7) for k in range(4)]
    send_part8 = [
        [remote(path_coef, parts8.at[k], 6 + n, 18 + k, device) for n, device in enumerate((*first_gates, second_p7))]
        for k in range(2)
    ]
    send_part8_right = [remote(path_coef, parts8.at[0], 8 + k, 18, right_p7s[k]) for k in range(2)]
    send_above7 = [remote(outgoing.at[0], above, 16 + k, 13, gates_of_p7[k]) for k in (0, 3, 1, 2)]
    send_above4 = [remote(outgoing.at[k // 2], above, 3 + k, 13, p3s_of_gate[k]) for k in range(4)]
    send_above2_left = [remote(outgoing.at[0], leaf_above, 2 + k, 6, left_column[k]) for k in (2, 1, 3, 0)]
    send_above2_right = [remote(outgoing.at[1], leaf_above, 5 + k, 6, column[k]) for k in (2, 1, 3)]

    def start(copies):
        for copy in copies:
            copy.start()

    def dot(a, b):
        return jnp.dot(a, b, preferred_element_type=F32)

    load_rhs.wait()
    load_in.wait()
    load_rank.wait()
    leaf_rank, node_rank = rank[0, 0], rank[0, 1]
    leaf_keep = lax.broadcasted_iota(jnp.int32, (rows, leaf_width), 1) < leaf_rank
    node_keep = lax.broadcasted_iota(jnp.int32, (rows, width), 1) < node_rank
    leaf_coef[...] = jnp.where(leaf_keep, dot(rhs[...], leaf_in[...]), 0.0).astype(BF16)

    pl.semaphore_wait(barrier, greeted)

    @pl.when(is_p1)
    def _():
        pl.semaphore_signal(go_sem, inc=1, device_id=left_leaf, device_id_type=MESH)

    def mask_up():
        keep = lax.broadcasted_iota(jnp.int32, (width, width), 1) < node_rank
        for s in range(2):
            up[s, 0] = jnp.where(keep, up[s, 0], jnp.zeros((width, width), BF16))

    def mask_down():
        keep = lax.broadcasted_iota(jnp.int32, (width, width), 0) < node_rank
        for s in range(2):
            down[s, 0] = jnp.where(keep, down[s, 0], jnp.zeros((width, width), BF16))

    def send_up(summed, waits=False):
        coef[...] = jnp.where(node_keep, summed, 0.0).astype(BF16)
        if waits:
            pl.semaphore_wait(go_sem, 1)

        @pl.when(side == 0)
        def _():
            up_left.start()

        @pl.when(side == 1)
        def _():
            up_right.start()

    def cross_terms():
        cross_sum[0] = dot(child[:, right_part], cross[0, 0])
        cross_sum[1] = dot(child[:, left_part], cross[1, 0])

    @pl.when(is_even)
    def _():
        leaf_up.start()

    @pl.when(on_line)
    def _():
        pl.semaphore_wait(go_sem, 1)

    @pl.when(is_p1)
    def _():
        load_up.wait()
        summed = dot(leaf_coef[...], up[1, 0, narrow, :])
        leaf_up.wait_recv()
        send_up(summed + dot(child[:, narrow], up[0, 0, narrow, :]))
        load_cross.wait()
        cross_sum[0, :, narrow] = dot(leaf_coef[...], cross[0, 0, narrow, narrow])
        leaf_cross1[...] = dot(child[:, narrow], cross[1, 0, narrow, narrow])
        start(send_cross1)
        load_down.wait()
        mask_down()
        start(send_down1)
        leaf_map1[...] = down[1, 0, :, narrow]

    def lift(waits=True):
        up_left.wait_recv()
        summed = dot(child[:, left_part], up[0, 0])
        up_right.wait_recv()
        send_up(summed + dot(child[:, right_part], up[1, 0]), waits)

    @pl.when(is_p2)
    def _():
        load_up.wait()
        lift()
        load_cross.wait()
        cross_terms()
        start(send_cross2)
        leaf_cross2[...] = cross_sum[1]
        load_down.wait()
        mask_down()
        start(send_down2)
        leaf_map2[...] = down[1, 0]

    @pl.when(is_p3)
    def _():
        load_up.wait()
        lift()
        load_cross.wait()
        cross_terms()
        load_down.wait()
        mask_down()

    @pl.when(is_p4)
    def _():
        load_up.wait()
        lift()
        load_cross.wait()
        cross_terms()
        start(send_cross4)
        load_down.wait()
        mask_down()
        start(send_down4)

    @pl.when(is_gate)
    def _():
        load_up.wait()
        load_cross.wait()
        load_down.wait()
        mask_down()

        @pl.when(z % 4 == 1)
        def _():
            send_down7[0].wait_recv()
            pass_down7.start()

        lift(waits=False)
        send_up6[0].wait_recv()
        path_coef[...] = dot(coef[...], map_a[...]).astype(BF16)
        for k in range(4):

            @pl.when(z % 4 == k)
            def _():
                send_part6[k].start()

        cross_terms()

        @pl.when(z == 1)
        def _():
            send_down8_first[0].wait_recv()
            pass_down8.start()

    @pl.when(is_p6)
    def _():
        load_up.wait()
        mask_up()
        start(send_up6)
        load_cross.wait()
        load_down.wait()
        mask_down()
        for copy in send_up6:
            copy.wait_send()
        start(send_down6)
        up_left.wait_recv()
        up_right.wait_recv()
        cross_terms()
        start(send_cross6)

    @pl.when(is_p7)
    def _():
        load_down.wait()
        mask_down()
        start(send_down7[1:])
        load_up.wait()
        load_cross.wait()
        for s in range(2):
            for k in (2 * s, 2 * s + 1):
                send_part6[k].wait_recv()
            six = parts6[2 * s].astype(F32) + parts6[2 * s + 1].astype(F32)
            child[:, (left_part, right_part)[s]] = six.astype(BF16)
        send_up(dot(child[:, left_part], up[0, 0]) + dot(child[:, right_part], up[1, 0]))

        @pl.when(is_right_p7)
        def _():
            send_up8[0].wait_recv()
            eight = dot(coef[...], map_a[...]).astype(BF16)
            send_cross9[0].wait_recv()
            path_coef[...] = dot(eight, map_b[...]).astype(BF16)
            for k in range(2):

                @pl.when(z // 4 % 2 == k)
                def _():
                    start(send_part8[k])

        cross_terms()
        start(send_cross7)

    @pl.when(is_p8)
    def _():
        load_up.wait()
        load_cross.wait()
        load_down.wait()
        mask_down()
        send_cross1[0].wait_recv()
        send_down1[0].wait_recv()

        @pl.when(is_right_p8)
        def _():
            mask_up()
            start(send_up8)
            for copy in send_up8:
                copy.wait_send()
            start(send_down8)
            up_left.wait_recv()
            up_right.wait_recv()
            cross_terms()
            start(send_cross8)

        @pl.when(is_left_p8)
        def _():
            send_down8[1].start()
            for copy in send_down8_first[1:]:
                copy.start()
                copy.wait_send()
            up_left.wait_recv()
            eight = dot(child[:, left_part], up[0, 0])
            up_right.wait_recv()
            cross_terms()
            start(send_cross8_first)
            send_cross8[1].start()
            eight += dot(child[:, right_part], up[1, 0])
            coef[...] = jnp.where(node_keep, eight, 0.0).astype(BF16)
            send_cross9[2].wait_recv()
            path_coef[...] = dot(coef[...], map_b[...]).astype(BF16)
            start(send_part8_right)

    @pl.when(both(on_top, z % 8 == 0))
    def _():
        load_up.wait()
        load_cross.wait()
        load_down.wait()

    @pl.when(is_p9)
    def _():
        start(send_cross9)

    load_diag.wait()
    product[...] = dot(rhs[...], diag[...])
    load_out.wait()

    @pl.when(both(is_p7, z > 2))
    def _():
        send_down8[0].wait_recv()
        send_cross8[0].wait_recv()
        send_part8[0][0].wait_recv()

        @pl.when(is_second_p7)
        def _():
            send_part8[1][0].wait_recv()
            crossed = parts8[0].astype(F32) + parts8[1].astype(F32)
            parts8[0] = crossed.astype(BF16)

        outgoing[0] = (cross_a[...] + dot(parts8[0], map_c[...])).astype(BF16)
        start(send_above7)

    @pl.when(is_gate)
    def _():
        @pl.when(z % 4 != 1)
        def _():
            send_down7[0].wait_recv()

        send_cross7[0].wait_recv()
        send_down6[0].wait_recv()
        send_cross6[0].wait_recv()

        @pl.when(both(z < 4, z != 1))
        def _():
            send_down8_first[0].wait_recv()

        @pl.when(z < 4)
        def _():
            send_cross8_first[0].wait_recv()
            for k in range(2):
                send_part8[k][0].wait_recv()
            crossed = (parts8[0].astype(F32) + parts8[1].astype(F32)).astype(BF16)
            above[...] = (cross_c[...] + dot(crossed, map_b[...])).astype(BF16)

        @pl.when(z >= 4)
        def _():
            send_above7[0].wait_recv()

        six = (cross_a[...] + dot(above[...], map_d[...])).astype(BF16)
        five = (cross_b[...] + dot(six, map_c[...])).astype(BF16)
        for s in range(2):
            outgoing[s] = (cross_sum[s] + dot(five, down[s, 0])).astype(BF16)
            start(send_above4[2 * s : 2 * s + 2])

    @pl.when(is_p3)
    def _():
        send_down4[0].wait_recv()
        send_cross4[0].wait_recv()
        send_above4[0].wait_recv()
        three = (cross_a[...] + dot(above[...], map_d[...])).astype(BF16)
        outgoing[0] = (cross_sum[0] + dot(three, down[0, 0])).astype(BF16)
        start(send_above2_left)
        outgoing[1] = (cross_sum[1] + dot(three, down[1, 0])).astype(BF16)
        start(send_above2_right)
        leaf_above[...] = outgoing[1]

    @pl.when(both(is_even, jnp.logical_not(is_p8)))
    def _():
        send_cross1[0].wait_recv()
        send_down1[0].wait_recv()

    @pl.when(jnp.logical_not(is_p2))
    def _():
        send_cross2[0].wait_recv()
        send_down2[0].wait_recv()

    @pl.when(jnp.logical_not(is_p3))
    def _():
        send_above2_left[0].wait_recv()

    one = (leaf_cross2[...] + dot(leaf_above[...], leaf_map2[...])).astype(BF16)
    zero = (leaf_cross1[...] + dot(one, leaf_map1[...])).astype(BF16)
    zero = jnp.where(leaf_keep, zero, jnp.zeros_like(zero))
    product[...] += dot(zero, leaf_out[...])

    def sent(condition, copies):
        @pl.when(condition)
        def _():
            for copy in copies:
                copy.wait_send()

    sent(is_even, [leaf_up])
    sent(is_p1, [up_left, *send_cross1, *send_down1])
    sent(is_p2, [up_left, *send_cross2, *send_down2])
    sent(is_p3, [up_left, *send_above2_left, *send_above2_right])
    sent(is_p4, [up_left, *send_cross4, *send_down4])
    sent(is_gate, [up_left, send_part6[0], *send_above4])
    sent(both(is_gate, z % 4 == 1), [pass_down7])
    sent(both(is_gate, z == 1), [pass_down8])
    sent(is_p6, [*send_down6, *send_cross6])
    sent(is_p7, [up_left, *send_down7[1:], *send_cross7])
    sent(both(is_p7, z > 2), send_above7)
    sent(is_right_p7, send_part8[0])
    sent(is_right_p8, [*send_down8, *send_cross8])
    sent(is_left_p8, [send_down8[1], *send_cross8_first, send_cross8[1], *send_part8_right])
    sent(is_p9, send_cross9)


def on_device(rhs, diag_blocks, leaf_in, leaf_out, up_maps, cross_maps, down_maps, node_rank):
    rows, leaf = rhs.shape
    width, leaf_width = up_maps.shape[-1], leaf_in.shape[1]
    operands = (rhs, diag_blocks, leaf_in, leaf_out, up_maps, cross_maps, down_maps)

    def vector(*lead, kind=BF16, columns=width):
        return pltpu.VMEM((*lead, rows, columns), kind)

    full_map = pltpu.VMEM((width, width), BF16)
    return pl.pallas_call(
        kernel,
        out_shape=jax.ShapeDtypeStruct((rows, leaf), F32),
        in_specs=[pl.BlockSpec(memory_space=pl.ANY)] * 8,
        out_specs=pl.BlockSpec(memory_space=pltpu.VMEM),
        scratch_shapes=[pltpu.VMEM(each.shape, each.dtype) for each in operands]
        + [
            pltpu.SMEM(node_rank.shape, node_rank.dtype),
            vector(columns=leaf_width),
            vector(),
            vector(columns=2 * width),
            vector(2, kind=F32),
            vector(),
            vector(2),
            full_map,
            full_map,
            full_map,
            full_map,
            full_map,
            pltpu.VMEM((width, leaf_width), BF16),
            vector(kind=F32),
            vector(kind=F32),
            vector(kind=F32),
            vector(kind=F32),
            vector(kind=F32, columns=leaf_width),
            vector(),
            vector(),
            vector(4),
            vector(2),
            pltpu.SemaphoreType.DMA((8,)),
            pltpu.SemaphoreType.DMA((20,)),
            pltpu.SemaphoreType.DMA((21,)),
            pltpu.SemaphoreType.REGULAR,
        ],
        compiler_params=pltpu.CompilerParams(
            collective_id=0, has_side_effects=True, vmem_limit_bytes=60 * 2**20
        ),
    )(*operands, node_rank)


def solution(mesh):
    assert mesh.shape["tx"] == N_Z * N_CORE and mesh.shape["ty"] == N_X * N_Y
    in_specs = (
        P(None, ("tx", "ty")),
        P(("tx", "ty"), None),
        P(("tx", "ty"), None),
        P(("tx", "ty"), None),
        P(None, ("tx", "ty"), None, None),
        P(None, ("tx", "ty"), None, None),
        P(None, ("tx", "ty"), None, None),
        P(("tx", "ty"), None),
    )
    return jax.shard_map(
        on_device, mesh=mesh, in_specs=in_specs, out_specs=P(None, ("tx", "ty")), check_vma=False
    )
```

```python
import functools

import jax
import jax.numpy as jnp
from jax import lax
from jax.experimental import pallas as pl
from jax.experimental.pallas import tpu as pltpu
from jax.sharding import PartitionSpec as P

MESH = pl.DeviceIdType.MESH
F32 = jnp.float32
BF16 = jnp.bfloat16
N_Z, N_CORE, N_X, N_Y = 16, 2, 4, 4


def kernel(
    rhs_hbm,
    diag_hbm,
    in_hbm,
    out_hbm,
    up_hbm,
    cross_hbm,
    down_hbm,
    rank_hbm,
    product,
    rhs,
    diag,
    leaf_in,
    leaf_out,
    up,
    cross,
    down,
    rank,
    leaf_coef,
    coef,
    child,
    cross_sum,
    path_coef,
    outgoing,
    map_a,
    map_b,
    map_c,
    map_d,
    leaf_map2,
    leaf_map1,
    cross_a,
    cross_b,
    cross_c,
    leaf_cross2,
    leaf_cross1,
    above,
    leaf_above,
    parts,
    parts8,
    load_sem,
    send_sem,
    recv_sem,
    go_sem,
):
    rows, width = coef.shape
    leaf_width = leaf_coef.shape[1]
    tx, ty = lax.axis_index("tx"), lax.axis_index("ty")
    z, core = tx // N_CORE, tx % N_CORE
    x, y = ty // N_Y, ty % N_Y

    def at(z, core, x, y):
        return (z * N_CORE + core, x * N_Y + y)

    both = jnp.logical_and
    on_line = ty == 0
    on_top = both(on_line, core == 0)
    is_p1 = y % 2 == 1
    is_p2 = y == 2
    is_p3 = both(y == 0, x % 2 == 1)
    is_p4 = both(y == 0, x == 2)
    is_gate = both(on_line, core == 1)
    is_p6 = both(on_top, z % 2 == 1)
    is_p7 = both(on_top, z % 4 == 2)
    is_p8 = both(on_top, z % 8 == 4)
    is_p9 = both(on_top, z == 8)
    is_even = y % 2 == 0
    is_first = both(is_gate, z < 4)
    is_left_p8 = both(on_top, z == 4)
    is_right_p8 = both(on_top, z == 12)
    is_third_p7 = both(on_top, z == 10)
    is_second_p7 = both(on_top, z == 6)

    loads = [
        pltpu.make_async_copy(source, target, load_sem.at[n])
        for n, (source, target) in enumerate(
            (
                (rhs_hbm, rhs),
                (in_hbm, leaf_in),
                (rank_hbm, rank),
                (up_hbm, up),
                (cross_hbm, cross),
                (down_hbm, down),
                (diag_hbm, diag),
                (out_hbm, leaf_out),
            )
        )
    ]
    load_rhs, load_in, load_rank, load_up, load_cross, load_down, load_diag, load_out = loads
    for load in loads[:3]:
        load.start()

    x_odd = x // 2 * 2 + 1
    z_odd, z_seven, z_eight = z // 2 * 2 + 1, z // 4 * 4 + 2, z // 8 * 8 + 4
    leaf_peer = at(z, core, x, y + 1)
    left_leaf = at(z, core, x, y - 1)
    column = [at(z, core, x, k) for k in range(N_Y)]
    left_column = [at(z, core, x - 1, k) for k in range(N_Y)]
    my_p3 = at(z, core, x_odd, 0)
    p3s = [at(z, core, 1, 0), at(z, core, 3, 0)]
    p4 = at(z, core, 2, 0)
    gate = at(z, 1, 0, 0)
    p3s_of_gate = [at(z, c, k, 0) for c in range(N_CORE) for k in (1, 3)]
    p4s_of_gate = [at(z, c, 2, 0) for c in range(N_CORE)]
    p6, p7, p8 = at(z_odd, 0, 0, 0), at(z_seven, 0, 0, 0), at(z_eight, 0, 0, 0)
    gates_of_p6 = [at(z_odd - 1, 1, 0, 0), at(z_odd, 1, 0, 0)]
    gates_of_p7 = [at(z_seven - 2 + k, 1, 0, 0) for k in range(4)]
    p7s_of_p8 = [at(z_eight - 2, 0, 0, 0), at(z_eight + 2, 0, 0, 0)]
    first_gates = [at(k, 1, 0, 0) for k in range(4)]
    second_p7, left_p8 = at(6, 0, 0, 0), at(4, 0, 0, 0)
    right_p7s = [at(k, 0, 0, 0) for k in (10, 14)]

    barrier = pltpu.get_barrier_semaphore()

    def greet(condition, devices):
        @pl.when(condition)
        def _():
            for device in devices:
                pl.semaphore_signal(barrier, inc=1, device_id=device, device_id_type=MESH)

    def collector(z, core, x):
        return at(z, core, x, 1)

    x_even = x % 2 == 0
    next_p3 = collector(z, core, x_odd)
    greet(is_p1, [left_leaf])
    greet(y == 1, [column[3]])
    greet(both(y == 1, x_even), [next_p3])
    greet(y == 3, [next_p3])
    greet(is_p2, [column[1], column[3], next_p3])
    greet(y == 0, [column[1], column[3]])
    greet(both(y == 0, x_even), [next_p3])
    greet(is_p3, [at(z, core, x - 1, 3), collector(z, core, 2), collector(z, 1, 0)])
    greet(is_p4, [collector(z, core, 1), collector(z, core, 3)])
    greet(is_gate, [collector(z, 0, 1), collector(z, 0, 3), collector(z, 1, 2)] + [collector(z_odd, 0, 0), collector(z_seven, 0, 0)])
    greet(both(is_gate, z % 4 == 0), [collector(z + 1, 1, 0)])
    greet(is_first, [collector(4, 0, 0), collector(8, 0, 0)])
    greet(is_p6, [collector(z_odd - 1, 1, 0), collector(z_odd, 1, 0)])
    greet(is_p7, [collector(z_seven - 2 + k, 1, 0) for k in range(4)])
    greet(both(is_p7, z > 2), [collector(z_eight, 0, 0), collector(8, 0, 0)])
    greet(is_p8, [collector(z_eight - 2, 0, 0), collector(z_eight + 2, 0, 0)])
    greet(is_p8, [collector(8, 0, 0)])
    sizes = (
        (is_even, 1),
        (y == 3, 3),
        (both(y == 3, x_even), 1),
        (y == 1, 2),
        (both(y == 1, x % 2 == 1), 7),
        (both(both(y == 1, x % 2 == 1), core == 0), 1),
        (both(y == 1, x == 2), 2 + core),
        (both(ty == 1, core == 1), 6),
        (both(both(ty == 1, core == 1), z % 4 == 1), 1),
        (both(both(ty == 1, core == 0), z % 2 == 1), 2),
        (both(both(ty == 1, core == 0), z % 4 == 2), 5),
        (both(both(ty == 1, core == 0), z == 4), 5),
        (both(both(ty == 1, core == 0), z == 12), 2),
        (both(both(ty == 1, core == 0), z == 8), 9),
    )
    greeted = sum(condition.astype(jnp.int32) * size for condition, size in sizes)
    for load in loads[3:]:
        load.start()

    def remote(source, target, send, recv, device):
        return pltpu.make_async_remote_copy(
            src_ref=source,
            dst_ref=target,
            send_sem=send_sem.at[send],
            recv_sem=recv_sem.at[recv],
            device_id=device,
            device_id_type=MESH,
        )

    left_part, right_part = pl.ds(0, width), pl.ds(width, width)
    narrow = pl.ds(0, leaf_width)

    leaf_up = remote(leaf_coef, child.at[:, narrow], 0, 0, leaf_peer)
    side = jnp.where(
        is_p1,
        y // 2,
        jnp.where(is_p2, x % 2, jnp.where(is_p3, x // 2, jnp.where(is_p4, core, jnp.where(is_gate, z % 2, z // 4 % 2)))),
    )
    steps = ((is_p1, column[2]), (is_p2, my_p3), (is_p3, p4), (is_p4, gate), (is_gate, p6), (is_p7, p8))
    parent = tuple(sum(condition.astype(jnp.int32) * device[k] for condition, device in steps) for k in range(2))
    up_left = remote(coef, child.at[:, left_part], 1, 0, parent)
    up_right = remote(coef, child.at[:, right_part], 1, 1, parent)
    send_cross1 = [remote(cross_sum.at[0, :, narrow], leaf_cross1, 2, 2, left_leaf)]
    send_down1 = [remote(down.at[0, 0, :, narrow], leaf_map1, 3, 3, left_leaf)]
    sides2 = ((0, 0), (1, 0), (3, 1))
    send_cross2 = [remote(cross_sum.at[s], leaf_cross2, 2 + n, 4, column[k]) for n, (k, s) in enumerate(sides2)]
    send_down2 = [remote(down.at[s, 0], leaf_map2, 5 + n, 5, column[k]) for n, (k, s) in enumerate(sides2)]
    send_cross4 = [remote(cross_sum.at[s], cross_a, 2 + s, 11, p3s[s]) for s in range(2)]
    send_up4 = [remote(up.at[s, 0], map_a, 7 + s, 7, p3s[s]) for s in range(2)]
    send_part4 = [remote(path_coef, parts.at[k], 9, 14 + k, gate) for k in range(2)]
    send_down4 = [remote(down.at[s, 0], map_d, 5 + s, 10, p3s[s]) for s in range(2)]
    send_cross6 = [remote(cross_sum.at[s], cross_b, 2 + s, 12, gates_of_p6[s]) for s in range(2)]
    send_up6 = [remote(up.at[s, 0], map_a, 4 + s, 7, gates_of_p6[s]) for s in range(2)]
    send_down6 = [remote(down.at[s, 0], map_c, 6 + s, 9, gates_of_p6[s]) for s in range(2)]
    send_cross7 = [remote(cross_sum.at[k // 2], cross_a, 2 + k, 11, gates_of_p7[k]) for k in range(4)]
    send_down7 = [remote(down.at[k // 2, 0], map_d, 10 + k, 10, gates_of_p7[k]) for k in range(4)]
    pass_down7 = remote(map_d, map_d, 7, 10, at(z - 1, 1, 0, 0))
    send_cross8 = [remote(cross_sum.at[s], cross_a, 2 + s, 11, p7s_of_p8[s]) for s in range(2)]
    send_cross8_first = [remote(cross_sum.at[0], cross_c, 10 + k, 20, first_gates[k]) for k in range(4)]
    send_up8 = remote(up.at[0, 0], map_a, 4, 7, p7s_of_p8[0])
    send_down8 = [remote(down.at[s, 0], map_c, 6 + s, 9, p7s_of_p8[s]) for s in range(2)]
    halves = [pl.ds(k * (width // 2), width // 2) for k in range(2)]
    send_down8_half = [remote(down.at[0, 0, half], map_c.at[half], 6 + 5 * k, 9, p7s_of_p8[0]) for k, half in enumerate(halves)]
    send_down8_first = [remote(down.at[0, 0], map_b, 14 + k, 8, first_gates[k]) for k in range(4)]
    pass_down8 = remote(map_b, map_b, 8, 8, at(z - 1, 1, 0, 0))
    send_cross9 = [remote(cross.at[0, 0], map_b, 2 + k, 8, at((10, 12)[k], 0, 0, 0)) for k in range(2)]
    send_cross9 += [remote(cross.at[1, 0], map_b, 4, 8, left_p8)]
    send_part6 = [remote(path_coef, parts.at[k], 2, 14 + k, p7) for k in range(4)]
    send_part8 = [
        [remote(path_coef, parts8.at[k], 12 + n, 18 + k, device) for n, device in enumerate((*first_gates, second_p7))]
        for k in range(2)
    ]
    send_part8_right = [remote(path_coef, parts8.at[0], 8 + k, 18, right_p7s[k]) for k in range(2)]
    send_above7 = [remote(outgoing.at[0], above, 16 + k, 13, gates_of_p7[k]) for k in (0, 3, 1, 2)]
    send_above4 = [remote(outgoing.at[k // 2], above, 3 + k, 13, p3s_of_gate[k]) for k in range(4)]
    send_above2_left = [remote(outgoing.at[0], leaf_above, 2 + k, 6, left_column[k]) for k in (2, 1, 3, 0)]
    send_above2_right = [remote(outgoing.at[1], leaf_above, 5 + k, 6, column[k]) for k in (2, 1, 3)]

    def start(copies):
        for copy in copies:
            copy.start()

    def dot(a, b):
        return jnp.dot(a, b, preferred_element_type=F32)

    load_rhs.wait()
    load_in.wait()
    load_rank.wait()
    leaf_rank, node_rank = rank[0, 0], rank[0, 1]
    leaf_keep = lax.broadcasted_iota(jnp.int32, (rows, leaf_width), 1) < leaf_rank
    node_keep = lax.broadcasted_iota(jnp.int32, (rows, width), 1) < node_rank
    leaf_coef[...] = jnp.where(leaf_keep, dot(rhs[...], leaf_in[...]), 0.0).astype(BF16)

    pl.semaphore_wait(barrier, greeted)

    @pl.when(is_p1)
    def _():
        pl.semaphore_signal(go_sem, inc=1, device_id=left_leaf, device_id_type=MESH)

    def mask_up():
        keep = lax.broadcasted_iota(jnp.int32, (width, width), 1) < node_rank
        for s in range(2):
            up[s, 0] = jnp.where(keep, up[s, 0], jnp.zeros((width, width), BF16))

    def mask_down():
        keep = lax.broadcasted_iota(jnp.int32, (width, width), 0) < node_rank
        for s in range(2):
            down[s, 0] = jnp.where(keep, down[s, 0], jnp.zeros((width, width), BF16))

    def send_up(summed, waits=False):
        coef[...] = jnp.where(node_keep, summed, 0.0).astype(BF16)
        if waits:
            pl.semaphore_wait(go_sem, 1)

        @pl.when(side == 0)
        def _():
            up_left.start()

        @pl.when(side == 1)
        def _():
            up_right.start()

    def cross_terms():
        cross_sum[0] = dot(child[:, right_part], cross[0, 0])
        cross_sum[1] = dot(child[:, left_part], cross[1, 0])

    @pl.when(is_even)
    def _():
        leaf_up.start()

    @pl.when(on_line)
    def _():
        pl.semaphore_wait(go_sem, 1)

    @pl.when(is_p1)
    def _():
        load_up.wait()
        summed = dot(leaf_coef[...], up[1, 0, narrow, :])
        leaf_up.wait_recv()
        send_up(summed + dot(child[:, narrow], up[0, 0, narrow, :]))
        load_cross.wait()
        cross_sum[0, :, narrow] = dot(leaf_coef[...], cross[0, 0, narrow, narrow])
        leaf_cross1[...] = dot(child[:, narrow], cross[1, 0, narrow, narrow])
        start(send_cross1)
        load_down.wait()
        mask_down()
        start(send_down1)
        leaf_map1[...] = down[1, 0, :, narrow]

    def lift(waits=True):
        up_left.wait_recv()
        summed = dot(child[:, left_part], up[0, 0])
        up_right.wait_recv()
        send_up(summed + dot(child[:, right_part], up[1, 0]), waits)

    @pl.when(is_p2)
    def _():
        load_up.wait()
        lift()
        load_cross.wait()
        cross_terms()
        start(send_cross2)
        leaf_cross2[...] = cross_sum[1]
        load_down.wait()
        mask_down()
        start(send_down2)
        leaf_map2[...] = down[1, 0]

    @pl.when(is_p3)
    def _():
        load_up.wait()
        lift()

        @pl.when(core == 0)
        def _():
            send_up4[0].wait_recv()
            path_coef[...] = dot(coef[...], map_a[...]).astype(BF16)
            for k in range(2):

                @pl.when(x // 2 == k)
                def _():
                    send_part4[k].start()

        load_cross.wait()
        cross_terms()
        load_down.wait()
        mask_down()

    @pl.when(is_p4)
    def _():
        load_up.wait()
        mask_up()
        pl.semaphore_wait(go_sem, 1)

        @pl.when(core == 0)
        def _():
            start(send_up4)
            up_left.wait_recv()
            up_right.wait_recv()

        @pl.when(core == 1)
        def _():
            lift(waits=False)

        load_cross.wait()
        cross_terms()
        start(send_cross4)
        load_down.wait()
        mask_down()
        start(send_down4)

    @pl.when(is_gate)
    def _():
        load_up.wait()
        load_cross.wait()
        load_down.wait()
        mask_down()

        @pl.when(z % 4 == 1)
        def _():
            send_down7[0].wait_recv()
            pass_down7.start()

        for copy in send_part4:
            copy.wait_recv()
        child[:, left_part] = (parts[0].astype(F32) + parts[1].astype(F32)).astype(BF16)
        up_right.wait_recv()
        send_up(dot(child[:, left_part], up[0, 0]) + dot(child[:, right_part], up[1, 0]))
        send_up6[0].wait_recv()
        path_coef[...] = dot(coef[...], map_a[...]).astype(BF16)
        for k in range(4):

            @pl.when(z % 4 == k)
            def _():
                send_part6[k].start()

        cross_terms()

        @pl.when(z == 1)
        def _():
            send_down8_first[0].wait_recv()
            pass_down8.start()

    @pl.when(is_p6)
    def _():
        load_up.wait()
        mask_up()
        start(send_up6)
        load_cross.wait()
        load_down.wait()
        mask_down()
        for copy in send_up6:
            copy.wait_send()
        start(send_down6)
        up_left.wait_recv()
        up_right.wait_recv()
        cross_terms()
        start(send_cross6)

    @pl.when(is_p7)
    def _():
        load_down.wait()
        mask_down()
        start(send_down7[1:])
        load_up.wait()
        load_cross.wait()

        @pl.when(is_third_p7)
        def _():
            send_up8.wait_recv()
            send_cross9[0].wait_recv()
            map_a[...] = dot(map_a[...], map_b[...]).astype(BF16)

        for s in range(2):
            for k in (2 * s, 2 * s + 1):
                send_part6[k].wait_recv()
            six = parts[2 * s].astype(F32) + parts[2 * s + 1].astype(F32)
            child[:, (left_part, right_part)[s]] = six.astype(BF16)
        send_up(dot(child[:, left_part], up[0, 0]) + dot(child[:, right_part], up[1, 0]))

        @pl.when(is_third_p7)
        def _():
            path_coef[...] = dot(coef[...], map_a[...]).astype(BF16)
            start(send_part8[0])

        cross_terms()
        start(send_cross7)

    @pl.when(is_p8)
    def _():
        load_up.wait()
        load_cross.wait()
        load_down.wait()
        mask_down()
        @pl.when(is_right_p8)
        def _():
            send_down8[1].start()
            mask_up()

        send_cross1[0].wait_recv()

        @pl.when(is_right_p8)
        def _():
            send_down1[0].wait_recv()
            send_up8.start()
            send_up8.wait_send()
            send_down8_half[0].start()
            send_cross9[1].wait_recv()
            map_a[...] = dot(up[1, 0], map_b[...]).astype(BF16)
            up_right.wait_recv()
            path_coef[...] = dot(child[:, right_part], map_a[...]).astype(BF16)
            start(send_part8[1])
            send_down8_half[1].start()
            up_left.wait_recv()
            cross_terms()
            start(send_cross8)

        @pl.when(is_left_p8)
        def _():
            send_down8[1].start()
            send_down8_first[1].start()
            send_down1[0].wait_recv()
            send_down8_first[1].wait_send()
            start(send_down8_first[2:])
            up_left.wait_recv()
            eight = dot(child[:, left_part], up[0, 0])
            up_right.wait_recv()
            cross_terms()
            start(send_cross8_first)
            send_cross8[1].start()
            eight += dot(child[:, right_part], up[1, 0])
            coef[...] = jnp.where(node_keep, eight, 0.0).astype(BF16)
            send_cross9[2].wait_recv()
            path_coef[...] = dot(coef[...], map_b[...]).astype(BF16)
            start(send_part8_right)

    @pl.when(both(on_top, z % 8 == 0))
    def _():
        load_up.wait()
        load_cross.wait()
        load_down.wait()

    @pl.when(is_p9)
    def _():
        start(send_cross9)

    load_diag.wait()
    product[...] = dot(rhs[...], diag[...])
    load_out.wait()

    @pl.when(both(is_p7, z > 2))
    def _():
        send_down8[0].wait_recv()
        send_cross8[0].wait_recv()
        send_part8[0][0].wait_recv()

        @pl.when(is_second_p7)
        def _():
            send_part8[1][0].wait_recv()
            crossed = parts8[0].astype(F32) + parts8[1].astype(F32)
            parts8[0] = crossed.astype(BF16)

        outgoing[0] = (cross_a[...] + dot(parts8[0], map_c[...])).astype(BF16)
        start(send_above7)

    @pl.when(is_gate)
    def _():
        @pl.when(z % 4 != 1)
        def _():
            send_down7[0].wait_recv()

        @pl.when(z % 4 == 1)
        def _():
            pass_down7.wait_send()

        send_down6[0].wait_recv()
        map_d[...] = dot(map_d[...], map_c[...]).astype(BF16)

        @pl.when(both(z < 4, z != 1))
        def _():
            send_down8_first[0].wait_recv()

        @pl.when(z == 1)
        def _():
            pass_down8.wait_send()

        @pl.when(z < 4)
        def _():
            map_b[...] = dot(map_b[...], map_d[...]).astype(BF16)

        send_cross7[0].wait_recv()
        send_cross6[0].wait_recv()
        cross_b[...] += dot(cross_a[...].astype(BF16), map_c[...])

        @pl.when(z < 4)
        def _():
            send_cross8_first[0].wait_recv()
            cross_b[...] += dot(cross_c[...].astype(BF16), map_d[...])
            for k in range(2):
                send_part8[k][0].wait_recv()
            crossed = (parts8[0].astype(F32) + parts8[1].astype(F32)).astype(BF16)
            above[...] = (cross_b[...] + dot(crossed, map_b[...])).astype(BF16)

        @pl.when(z >= 4)
        def _():
            send_above7[0].wait_recv()
            above[...] = (cross_b[...] + dot(above[...], map_d[...])).astype(BF16)

        for s in range(2):
            outgoing[s] = (cross_sum[s] + dot(above[...], down[s, 0])).astype(BF16)
            start(send_above4[2 * s : 2 * s + 2])

    @pl.when(is_p3)
    def _():
        send_down4[0].wait_recv()
        send_cross4[0].wait_recv()
        for s in range(2):
            cross_sum[s] += dot(cross_a[...].astype(BF16), down[s, 0])
            down[s, 0] = dot(map_d[...], down[s, 0]).astype(BF16)
        send_above4[0].wait_recv()
        outgoing[0] = (cross_sum[0] + dot(above[...], down[0, 0])).astype(BF16)
        start(send_above2_left)
        outgoing[1] = (cross_sum[1] + dot(above[...], down[1, 0])).astype(BF16)
        start(send_above2_right)
        leaf_above[...] = outgoing[1]

    @pl.when(both(is_even, jnp.logical_not(is_p8)))
    def _():
        send_cross1[0].wait_recv()
        send_down1[0].wait_recv()

    @pl.when(jnp.logical_not(is_p2))
    def _():
        send_cross2[0].wait_recv()
        send_down2[0].wait_recv()

    zero = dot(leaf_cross2[...].astype(BF16), leaf_map1[...]) + leaf_cross1[...]
    zero = jnp.where(leaf_keep, zero, 0.0).astype(BF16)
    product[...] += dot(zero, leaf_out[...])
    map_keep = lax.broadcasted_iota(jnp.int32, (width, leaf_width), 1) < leaf_rank
    leaf_map1[...] = jnp.where(map_keep, dot(leaf_map2[...], leaf_map1[...]), 0.0).astype(BF16)
    leaf_map2[...] = dot(leaf_map1[...], leaf_out[...]).astype(BF16)

    @pl.when(jnp.logical_not(is_p3))
    def _():
        send_above2_left[0].wait_recv()

    product[...] += dot(leaf_above[...], leaf_map2[...])

    def sent(condition, copies):
        @pl.when(condition)
        def _():
            for copy in copies:
                copy.wait_send()

    sent(is_even, [leaf_up])
    sent(is_p1, [up_left, *send_cross1, *send_down1])
    sent(is_p2, [up_left, *send_cross2, *send_down2])
    sent(both(is_p3, core == 0), [send_part4[0]])
    sent(is_p3, [up_left, *send_above2_left, *send_above2_right])
    sent(both(is_p4, core == 0), send_up4)
    sent(both(is_p4, core == 1), [up_left])
    sent(is_p4, [*send_cross4, *send_down4])
    sent(is_gate, [up_left, send_part6[0], *send_above4])
    sent(is_p6, [*send_down6, *send_cross6])
    sent(is_p7, [up_left, *send_down7[1:], *send_cross7])
    sent(both(is_p7, z > 2), send_above7)
    sent(is_third_p7, send_part8[0])
    sent(is_right_p8, [send_down8[1], *send_down8_half, *send_part8[1], *send_cross8])
    sent(is_left_p8, [send_down8[1], *send_down8_first[2:], *send_cross8_first, send_cross8[1], *send_part8_right])
    sent(is_p9, send_cross9)


def on_device(rhs, diag_blocks, leaf_in, leaf_out, up_maps, cross_maps, down_maps, node_rank):
    rows, leaf = rhs.shape
    width, leaf_width = up_maps.shape[-1], leaf_in.shape[1]
    operands = (rhs, diag_blocks, leaf_in, leaf_out, up_maps, cross_maps, down_maps)

    def vector(*lead, kind=BF16, columns=width):
        return pltpu.VMEM((*lead, rows, columns), kind)

    full_map = pltpu.VMEM((width, width), BF16)
    return pl.pallas_call(
        kernel,
        out_shape=jax.ShapeDtypeStruct((rows, leaf), F32),
        in_specs=[pl.BlockSpec(memory_space=pl.ANY)] * 8,
        out_specs=pl.BlockSpec(memory_space=pltpu.VMEM),
        scratch_shapes=[pltpu.VMEM(each.shape, each.dtype) for each in operands]
        + [
            pltpu.SMEM(node_rank.shape, node_rank.dtype),
            vector(columns=leaf_width),
            vector(),
            vector(columns=2 * width),
            vector(2, kind=F32),
            vector(),
            vector(2),
            full_map,
            full_map,
            full_map,
            full_map,
            full_map,
            pltpu.VMEM((width, leaf_width), BF16),
            vector(kind=F32),
            vector(kind=F32),
            vector(kind=F32),
            vector(kind=F32),
            vector(kind=F32, columns=leaf_width),
            vector(),
            vector(),
            vector(4),
            vector(2),
            pltpu.SemaphoreType.DMA((8,)),
            pltpu.SemaphoreType.DMA((20,)),
            pltpu.SemaphoreType.DMA((21,)),
            pltpu.SemaphoreType.REGULAR,
        ],
        compiler_params=pltpu.CompilerParams(
            collective_id=0, has_side_effects=True, vmem_limit_bytes=60 * 2**20
        ),
    )(*operands, node_rank)


def solution(mesh):
    assert mesh.shape["tx"] == N_Z * N_CORE and mesh.shape["ty"] == N_X * N_Y
    in_specs = (
        P(None, ("tx", "ty")),
        P(("tx", "ty"), None),
        P(("tx", "ty"), None),
        P(("tx", "ty"), None),
        P(None, ("tx", "ty"), None, None),
        P(None, ("tx", "ty"), None, None),
        P(None, ("tx", "ty"), None, None),
        P(("tx", "ty"), None),
    )
    return jax.shard_map(
        on_device, mesh=mesh, in_specs=in_specs, out_specs=P(None, ("tx", "ty")), check_vma=False
    )
```

```python
import functools

import jax
import jax.numpy as jnp
from jax import lax
from jax.experimental import pallas as pl
from jax.experimental.pallas import tpu as pltpu
from jax.sharding import PartitionSpec as P

MESH = pl.DeviceIdType.MESH
F32 = jnp.float32
BF16 = jnp.bfloat16
N_Z, N_CORE, N_X, N_Y = 16, 2, 4, 4


def kernel(
    rhs_hbm,
    diag_hbm,
    in_hbm,
    out_hbm,
    up_hbm,
    cross_hbm,
    down_hbm,
    rank_hbm,
    product,
    rhs,
    diag,
    leaf_in,
    leaf_out,
    up,
    cross,
    down,
    rank,
    leaf_coef,
    coef,
    child,
    cross_sum,
    path_coef,
    outgoing,
    map_a,
    map_b,
    map_c,
    map_d,
    map_e,
    map_f,
    top_up,
    top_cross,
    top_child,
    top_coef,
    top_sum,
    top_out,
    far_out,
    gate_up,
    leaf_map2,
    leaf_map1,
    cross_a,
    cross_b,
    cross_c,
    leaf_cross2,
    leaf_cross1,
    above,
    leaf_above,
    parts4,
    parts6,
    parts8,
    load_sem,
    send_sem,
    recv_sem,
    go_sem,
    late_sem,
):
    rows, width = coef.shape
    leaf_width = leaf_coef.shape[1]
    tx, ty = lax.axis_index("tx"), lax.axis_index("ty")
    z, core = tx // N_CORE, tx % N_CORE
    x, y = ty // N_Y, ty % N_Y

    def at(z, core, x, y):
        return (z * N_CORE + core, x * N_Y + y)

    both = jnp.logical_and
    on_line = ty == 0
    on_top = both(on_line, core == 0)
    is_p1 = y % 2 == 1
    is_p2 = y == 2
    is_p3 = both(y == 0, x % 2 == 1)
    is_p4 = both(y == 0, x == 2)
    is_gate = both(on_line, core == 1)
    is_p6 = both(on_top, z % 2 == 1)
    is_p7 = both(on_top, z % 4 == 2)
    is_p8 = both(on_top, z % 8 == 4)
    is_p9 = both(on_top, z == 8)
    is_even = y % 2 == 0
    is_hub = both(is_gate, z % 4 == 2)
    is_late_hub = both(is_hub, z > 2)
    is_far_hub = both(is_hub, z >= 8)
    is_left_center = both(is_gate, z == 4)
    is_right_center = both(is_gate, z == 12)
    is_left_p8 = both(on_top, z == 4)
    is_right_p8 = both(on_top, z == 12)

    loads = [
        pltpu.make_async_copy(source, target, load_sem.at[n])
        for n, (source, target) in enumerate(
            (
                (rhs_hbm, rhs),
                (in_hbm, leaf_in),
                (rank_hbm, rank),
                (up_hbm, up),
                (cross_hbm, cross),
                (down_hbm, down),
                (diag_hbm, diag),
                (out_hbm, leaf_out),
            )
        )
    ]
    load_rhs, load_in, load_rank, load_up, load_cross, load_down, load_diag, load_out = loads
    for load in loads[:3]:
        load.start()

    x_odd = x // 2 * 2 + 1
    z_odd, z_seven, z_eight = z // 2 * 2 + 1, z // 4 * 4 + 2, z // 8 * 8 + 4
    leaf_peer = at(z, core, x, y + 1)
    left_leaf = at(z, core, x, y - 1)
    column = [at(z, core, x, k) for k in range(N_Y)]
    left_column = [at(z, core, x - 1, k) for k in range(N_Y)]
    my_p3 = at(z, core, x_odd, 0)
    p3s = [at(z, core, 1, 0), at(z, core, 3, 0)]
    p4 = at(z, core, 2, 0)
    gate = at(z, 1, 0, 0)
    p3s_of_gate = [at(z, c, k, 0) for c in range(N_CORE) for k in (1, 3)]
    p4s_of_gate = [at(z, c, 2, 0) for c in range(N_CORE)]
    p6, p7, p8 = at(z_odd, 0, 0, 0), at(z_seven, 0, 0, 0), at(z_eight, 0, 0, 0)
    gates_of_p6 = [at(z_odd - 1, 1, 0, 0), at(z_odd, 1, 0, 0)]
    gates_of_p7 = [at(z_seven - 2 + k, 1, 0, 0) for k in range(4)]
    hub, center = at(z_seven, 1, 0, 0), at(z_eight, 1, 0, 0)
    hubs_of_center = [at(z_eight - 2, 1, 0, 0), at(z_eight + 2, 1, 0, 0)]
    first_gates = [at(k, 1, 0, 0) for k in range(4)]
    second_hub, third_hub, fourth_hub = at(6, 1, 0, 0), at(10, 1, 0, 0), at(14, 1, 0, 0)

    barrier = pltpu.get_barrier_semaphore()

    def greet(condition, devices):
        @pl.when(condition)
        def _():
            for device in devices:
                pl.semaphore_signal(barrier, inc=1, device_id=device, device_id_type=MESH)

    def collector(z, core, x):
        return at(z, core, x, 1)

    x_even = x % 2 == 0
    next_p3 = collector(z, core, x_odd)
    greet(is_p1, [left_leaf])
    greet(y == 1, [column[3]])
    greet(both(y == 1, x_even), [next_p3])
    greet(y == 3, [next_p3])
    greet(is_p2, [column[1], column[3], next_p3])
    greet(y == 0, [column[1], column[3]])
    greet(both(y == 0, x_even), [next_p3])
    greet(is_p3, [at(z, core, x - 1, 3), collector(z, core, 2), collector(z, 1, 0)])
    greet(is_p4, [collector(z, core, 1), collector(z, core, 3)])
    greet(is_gate, [collector(z, 0, 1), collector(z, 0, 3), collector(z, 1, 2)] + [collector(z_odd, 0, 0), collector(z_seven, 0, 0)])
    greet(both(is_gate, z % 4 == 0), [collector(z + 1, 1, 0)])
    greet(both(is_gate, z < 4), [collector(4, 0, 0), collector(8, 0, 0), collector(4, 1, 0)])
    greet(both(both(is_gate, z >= 4), z % 4 != 2), [collector(z_seven, 1, 0)])
    greet(is_hub, [collector(z_seven - 2 + k, 1, 0) for k in (0, 1, 3)])
    greet(is_late_hub, [collector(z_eight, 0, 0), collector(z_eight, 1, 0)])
    greet(both(is_late_hub, z < 12), [collector(8, 0, 0)])
    greet(both(is_late_hub, z > 12), [collector(4, 1, 0), collector(8, 1, 0)])
    greet(is_p9, [collector(8, 1, 0)])
    greet(
        both(is_gate, z % 8 == 4),
        [collector(z_eight - 2, 1, 0), collector(z_eight + 2, 1, 0), collector(z, 0, 0)],
    )
    greet(is_left_center, [collector(8, 0, 0)])
    greet(is_p6, [collector(z_odd - 1, 1, 0), collector(z_odd, 1, 0)])
    greet(is_p7, [collector(z, 1, 0)])
    greet(is_right_p8, [collector(z, 1, 0)])
    sizes = (
        (is_even, 1),
        (y == 3, 3),
        (both(y == 3, x_even), 1),
        (y == 1, 2),
        (both(y == 1, x % 2 == 1), 7),
        (both(both(y == 1, x % 2 == 1), core == 0), 1),
        (both(y == 1, x == 2), 2 + core),
        (both(ty == 1, core == 1), 5),
        (both(both(ty == 1, core == 1), z % 4 != 2), 1),
        (both(both(ty == 1, core == 1), z % 4 == 1), 1),
        (both(both(ty == 1, core == 1), z % 4 == 2), 2),
        (both(both(ty == 1, core == 1), both(z % 4 == 2, z > 2)), 3),
        (both(both(ty == 1, core == 1), z == 4), 6),
        (both(both(ty == 1, core == 1), z == 12), 3),
        (both(both(ty == 1, core == 1), z == 8), 2),
        (both(both(ty == 1, core == 0), z % 2 == 1), 2),
        (both(both(ty == 1, core == 0), z % 4 == 2), 4),
        (both(both(ty == 1, core == 0), z == 4), 6),
        (both(both(ty == 1, core == 0), z == 12), 3),
        (both(both(ty == 1, core == 0), z == 8), 7),
    )
    greeted = sum(condition.astype(jnp.int32) * size for condition, size in sizes)
    for load in loads[3:]:
        load.start()

    def remote(source, target, send, recv, device):
        return pltpu.make_async_remote_copy(
            src_ref=source,
            dst_ref=target,
            send_sem=send_sem.at[send],
            recv_sem=recv_sem.at[recv],
            device_id=device,
            device_id_type=MESH,
        )

    left_part, right_part = pl.ds(0, width), pl.ds(width, width)
    narrow = pl.ds(0, leaf_width)

    leaf_up = remote(leaf_coef, child.at[:, narrow], 0, 0, leaf_peer)
    side = jnp.where(
        is_p1,
        y // 2,
        jnp.where(is_p2, x % 2, jnp.where(is_p3, x // 2, jnp.where(is_p4, core, z % 2))),
    )
    steps = ((is_p1, column[2]), (is_p2, my_p3), (is_p3, p4), (is_p4, gate), (is_gate, p6))
    parent = tuple(sum(condition.astype(jnp.int32) * device[k] for condition, device in steps) for k in range(2))
    up_left = remote(coef, child.at[:, left_part], 1, 0, parent)
    up_right = remote(coef, child.at[:, right_part], 1, 1, parent)
    send_cross1 = [remote(cross_sum.at[0, :, narrow], leaf_cross1, 2, 2, left_leaf)]
    send_down1 = [remote(down.at[0, 0, :, narrow], leaf_map1, 3, 3, left_leaf)]
    sides2 = ((0, 0), (1, 0), (3, 1))
    send_cross2 = [remote(cross_sum.at[s], leaf_cross2, 2 + n, 4, column[k]) for n, (k, s) in enumerate(sides2)]
    send_down2 = [remote(down.at[s, 0], leaf_map2, 5 + n, 5, column[k]) for n, (k, s) in enumerate(sides2)]
    send_cross4 = [remote(cross_sum.at[s], cross_a, 2 + s, 11, p3s[s]) for s in range(2)]
    send_up4 = [remote(up.at[s, 0], map_a, 7 + s, 7, p3s[s]) for s in range(2)]
    send_part4 = [remote(path_coef, parts4.at[k], 9, 21 + k, gate) for k in range(2)]
    send_down4 = [remote(down.at[s, 0], map_d, 5 + s, 10, p3s[s]) for s in range(2)]
    send_cross6 = [remote(cross_sum.at[s], cross_b, 2 + s, 12, gates_of_p6[s]) for s in range(2)]
    send_up6 = [remote(up.at[s, 0], map_a, 4 + s, 7, gates_of_p6[s]) for s in range(2)]
    send_down6 = [remote(down.at[s, 0], map_c, 6 + s, 9, gates_of_p6[s]) for s in range(2)]
    halves = [pl.ds(k * (width // 2), width // 2) for k in range(2)]
    send_down6_half = [remote(down.at[0, 0, half], map_c.at[half], (6, 8)[k], 9, gates_of_p6[0]) for k, half in enumerate(halves)]
    send_cross7 = [remote(cross_sum.at[k // 2], cross_a, 2 + k, 11, gates_of_p7[k]) for k in range(4)]
    send_down7 = [remote(down.at[k // 2, 0], map_d, 10 + k, 10, gates_of_p7[k]) for k in range(4)]
    pass_down7 = remote(map_d, map_d, 7, 10, at(z - 1, 1, 0, 0))
    send_cross8 = [remote(top_sum.at[s], cross_c, 16 + s, 20, hubs_of_center[s]) for s in range(2)]
    send_cross8_first = [remote(top_sum.at[0], cross_c, 18 + k, 20, first_gates[k]) for k in range(4)]
    send_top_up7 = remote(up, top_up, 6, 23, hub)
    send_top_up8 = remote(up, top_up, 4, 23, center)
    send_top_cross = remote(cross, top_cross, 8, 24, center)
    send_up8 = [remote(up.at[s, 0], map_e, 4 + s, 27, hubs_of_center[s]) for s in range(2)]
    send_down8 = [remote(down.at[s, 0], map_b, 6 + s, 8, hubs_of_center[s]) for s in range(2)]
    send_down8_first = [remote(down.at[0, 0], map_b, 14 + k, 8, first_gates[k]) for k in range(4)]
    pass_down8 = remote(map_b, map_b, 8, 8, at(z - 1, 1, 0, 0))
    send_cross9 = [remote(cross.at[0, 0], map_f, 2, 28, third_hub), remote(cross.at[0, 0], map_f, 3, 28, fourth_hub)]
    send_cross9 += [remote(cross.at[1, 0], map_f, 4, 28, at(4, 1, 0, 0))]
    send_part6 = [remote(path_coef, parts6.at[k], 2, 14 + k, hub) for k in range(4)]
    send_child7 = remote(top_child, child, 9, 0, p7)
    send_coef7 = [remote(top_coef, top_child.at[:, part], 10, 25 + k, center) for k, part in enumerate((left_part, right_part))]
    send_part8 = [
        [remote(far_out, parts8.at[k], 11 + n, 18 + k, device) for n, device in enumerate((*first_gates, second_hub))]
        for k in range(2)
    ]
    send_part8_right = [remote(far_out, parts8.at[0], 11 + k, 18, (third_hub, fourth_hub)[k]) for k in range(2)]
    send_above7 = [remote(top_out, above, 16 + n, 13, gates_of_p7[k]) for n, k in enumerate((0, 3, 1))]
    send_above4 = [remote(outgoing.at[k // 2], above, 3 + k, 13, p3s_of_gate[k]) for k in range(4)]
    send_above2_left = [remote(outgoing.at[0], leaf_above, 2 + k, 6, left_column[k]) for k in (2, 1, 3, 0)]
    send_above2_right = [remote(outgoing.at[1], leaf_above, 5 + k, 6, column[k]) for k in (2, 1, 3)]

    def start(copies):
        for copy in copies:
            copy.start()

    def dot(a, b):
        return jnp.dot(a, b, preferred_element_type=F32)

    load_rhs.wait()
    load_in.wait()
    load_rank.wait()
    leaf_rank, node_rank = rank[0, 0], rank[0, 1]
    leaf_keep = lax.broadcasted_iota(jnp.int32, (rows, leaf_width), 1) < leaf_rank
    node_keep = lax.broadcasted_iota(jnp.int32, (rows, width), 1) < node_rank
    leaf_coef[...] = jnp.where(leaf_keep, dot(rhs[...], leaf_in[...]), 0.0).astype(BF16)

    pl.semaphore_wait(barrier, greeted)

    @pl.when(is_p1)
    def _():
        pl.semaphore_signal(go_sem, inc=1, device_id=left_leaf, device_id_type=MESH)

    @pl.when(both(both(ty == 1, core == 1), z == 8))
    def _():
        pl.semaphore_signal(late_sem, inc=1, device_id=at(8, 0, 0, 0), device_id_type=MESH)

    def mask_up():
        keep = lax.broadcasted_iota(jnp.int32, (width, width), 1) < node_rank
        for s in range(2):
            up[s, 0] = jnp.where(keep, up[s, 0], jnp.zeros((width, width), BF16))

    def mask_down():
        keep = lax.broadcasted_iota(jnp.int32, (width, width), 0) < node_rank
        for s in range(2):
            down[s, 0] = jnp.where(keep, down[s, 0], jnp.zeros((width, width), BF16))

    def send_up(summed, waits=False):
        coef[...] = jnp.where(node_keep, summed, 0.0).astype(BF16)
        if waits:
            pl.semaphore_wait(go_sem, 1)

        @pl.when(side == 0)
        def _():
            up_left.start()

        @pl.when(side == 1)
        def _():
            up_right.start()

    def cross_terms():
        cross_sum[0] = dot(child[:, right_part], cross[0, 0])
        cross_sum[1] = dot(child[:, left_part], cross[1, 0])

    @pl.when(is_even)
    def _():
        leaf_up.start()

    @pl.when(on_line)
    def _():
        pl.semaphore_wait(go_sem, 1)

    @pl.when(is_p1)
    def _():
        load_up.wait()
        summed = dot(leaf_coef[...], up[1, 0, narrow, :])
        leaf_up.wait_recv()
        send_up(summed + dot(child[:, narrow], up[0, 0, narrow, :]))
        load_cross.wait()
        cross_sum[0, :, narrow] = dot(leaf_coef[...], cross[0, 0, narrow, narrow])
        leaf_cross1[...] = dot(child[:, narrow], cross[1, 0, narrow, narrow])
        start(send_cross1)
        load_down.wait()
        mask_down()
        start(send_down1)
        leaf_map1[...] = down[1, 0, :, narrow]

    def lift(waits=True):
        up_left.wait_recv()
        summed = dot(child[:, left_part], up[0, 0])
        up_right.wait_recv()
        send_up(summed + dot(child[:, right_part], up[1, 0]), waits)

    @pl.when(is_p2)
    def _():
        load_up.wait()
        lift()
        load_cross.wait()
        cross_terms()
        start(send_cross2)
        leaf_cross2[...] = cross_sum[1]
        load_down.wait()
        mask_down()
        start(send_down2)
        leaf_map2[...] = down[1, 0]

    @pl.when(is_p3)
    def _():
        load_up.wait()
        lift()

        @pl.when(core == 0)
        def _():
            send_up4[0].wait_recv()
            path_coef[...] = dot(coef[...], map_a[...]).astype(BF16)
            for k in range(2):

                @pl.when(x // 2 == k)
                def _():
                    send_part4[k].start()

        load_cross.wait()
        cross_terms()
        load_down.wait()
        mask_down()

    @pl.when(is_p4)
    def _():
        load_up.wait()
        mask_up()
        pl.semaphore_wait(go_sem, 1)

        @pl.when(core == 0)
        def _():
            start(send_up4)
            up_left.wait_recv()
            up_right.wait_recv()

        @pl.when(core == 1)
        def _():
            lift(waits=False)

        load_cross.wait()
        cross_terms()
        start(send_cross4)
        load_down.wait()
        mask_down()
        start(send_down4)

    @pl.when(is_gate)
    def _():
        load_up.wait()
        load_cross.wait()
        load_down.wait()
        mask_down()

        @pl.when(z % 4 == 1)
        def _():
            send_down7[0].wait_recv()
            pass_down7.start()

        map_keep = lax.broadcasted_iota(jnp.int32, (width, width), 1) < node_rank
        send_up6[0].wait_recv()
        for s in range(2):
            ahead = dot(jnp.where(map_keep, up[s, 0], jnp.zeros((width, width), BF16)), map_a[...])
            gate_up[s] = ahead.astype(BF16)
        for copy in send_part4:
            copy.wait_recv()
        child[:, left_part] = (parts4[0].astype(F32) + parts4[1].astype(F32)).astype(BF16)
        up_right.wait_recv()
        six = dot(child[:, left_part], gate_up[0]) + dot(child[:, right_part], gate_up[1])
        path_coef[...] = six.astype(BF16)
        for k in (0, 1, 3):

            @pl.when(z % 4 == k)
            def _():
                send_part6[k].start()

        send_up(dot(child[:, left_part], up[0, 0]) + dot(child[:, right_part], up[1, 0]))

        @pl.when(is_hub)
        def _():
            parts6[2] = path_coef[...]
            send_top_up7.wait_recv()

            @pl.when(is_far_hub)
            def _():
                send_up8[0].wait_recv()
                send_cross9[0].wait_recv()
                map_e[...] = dot(map_e[...], map_f[...]).astype(BF16)

            for k in (0, 1, 3):
                send_part6[k].wait_recv()
            for k, part in enumerate((left_part, right_part)):
                six = parts6[2 * k].astype(F32) + parts6[2 * k + 1].astype(F32)
                top_child[:, part] = six.astype(BF16)
            seven = dot(top_child[:, left_part], top_up[0, 0]) + dot(top_child[:, right_part], top_up[1, 0])
            top_coef[...] = seven.astype(BF16)
            for k in range(2):

                @pl.when(z // 4 % 2 == k)
                def _():
                    send_coef7[k].start()

            @pl.when(is_far_hub)
            def _():
                far_out[...] = dot(top_coef[...], map_e[...]).astype(BF16)
                for k in range(2):

                    @pl.when(z == 10 + 4 * k)
                    def _():
                        start(send_part8[k])

            send_child7.start()

        def center_cross_terms():
            send_top_cross.wait_recv()
            top_sum[0] = dot(top_child[:, right_part], top_cross[0, 0]).astype(BF16)
            top_sum[1] = dot(top_child[:, left_part], top_cross[1, 0]).astype(BF16)

        @pl.when(is_left_center)
        def _():
            send_top_up8.wait_recv()
            send_coef7[0].wait_recv()
            send_coef7[1].wait_recv()
            center_cross_terms()
            start(send_cross8_first)
            send_cross8[1].start()
            eight = dot(top_child[:, left_part], top_up[0, 0]) + dot(top_child[:, right_part], top_up[1, 0])
            top_coef[...] = eight.astype(BF16)
            send_cross9[2].wait_recv()
            far_out[...] = dot(top_coef[...], map_f[...]).astype(BF16)
            start(send_part8_right)

        @pl.when(is_right_center)
        def _():
            pl.semaphore_signal(late_sem, inc=1, device_id=p8, device_id_type=MESH)
            send_coef7[1].wait_recv()
            send_coef7[0].wait_recv()
            center_cross_terms()
            start(send_cross8)

        cross_terms()

        @pl.when(z == 1)
        def _():
            send_down8_first[0].wait_recv()
            pass_down8.start()

    @pl.when(is_p6)
    def _():
        load_up.wait()
        mask_up()
        start(send_up6)
        load_cross.wait()
        load_down.wait()
        mask_down()
        for copy in send_up6:
            copy.wait_send()
        send_down6[1].start()

        @pl.when(z % 4 == 1)
        def _():
            send_down6[0].start()

        @pl.when(both(z % 4 == 3, z != 7))
        def _():
            send_down6_half[0].start()

        up_right.wait_recv()

        @pl.when(both(z % 4 == 3, z != 7))
        def _():
            send_down6_half[1].start()

        @pl.when(z == 7)
        def _():
            send_down6[0].start()

        up_left.wait_recv()
        cross_terms()
        start(send_cross6)

    @pl.when(is_p7)
    def _():
        load_up.wait()
        mask_up()
        send_top_up7.start()
        load_down.wait()
        mask_down()
        start(send_down7[1:])
        load_cross.wait()
        send_child7.wait_recv()
        cross_terms()
        start(send_cross7)

    @pl.when(is_p8)
    def _():
        load_up.wait()
        mask_up()
        load_cross.wait()
        send_top_cross.start()
        load_down.wait()
        mask_down()

        @pl.when(is_left_p8)
        def _():
            send_down8[1].start()

        @pl.when(is_right_p8)
        def _():
            send_up8[1].start()

        send_cross1[0].wait_recv()

        @pl.when(is_right_p8)
        def _():
            send_down1[0].wait_recv()
            send_up8[0].start()
            pl.semaphore_wait(late_sem, 1)
            start(send_down8)

        @pl.when(is_left_p8)
        def _():
            send_top_up8.start()
            send_down8_first[1].start()
            send_down1[0].wait_recv()
            for k, after in ((1, 3), (3, 2)):
                send_down8_first[k].wait_send()
                send_down8_first[after].start()

    @pl.when(both(on_top, z % 8 == 0))
    def _():
        load_up.wait()
        load_cross.wait()
        load_down.wait()

    @pl.when(is_p9)
    def _():
        send_cross9[0].start()
        send_cross9[2].start()
        pl.semaphore_wait(late_sem, 1)
        send_cross9[1].start()

    load_diag.wait()
    product[...] = dot(rhs[...], diag[...])
    load_out.wait()

    @pl.when(is_gate)
    def _():
        @pl.when(z % 4 != 1)
        def _():
            send_down7[0].wait_recv()

        @pl.when(z % 4 == 1)
        def _():
            pass_down7.wait_send()

        send_down6[0].wait_recv()
        map_d[...] = dot(map_d[...], map_c[...]).astype(BF16)

        @pl.when(both(z < 4, z != 1))
        def _():
            send_down8_first[0].wait_recv()

        @pl.when(z == 1)
        def _():
            pass_down8.wait_send()

        @pl.when(z < 4)
        def _():
            map_b[...] = dot(map_b[...], map_d[...]).astype(BF16)

        send_cross7[0].wait_recv()
        send_cross6[0].wait_recv()
        cross_b[...] += dot(cross_a[...].astype(BF16), map_c[...])

        @pl.when(z < 4)
        def _():
            send_cross8_first[0].wait_recv()
            cross_b[...] += dot(cross_c[...], map_d[...])
            for k in range(2):
                send_part8[k][0].wait_recv()
            crossed = (parts8[0].astype(F32) + parts8[1].astype(F32)).astype(BF16)
            above[...] = (cross_b[...] + dot(crossed, map_b[...])).astype(BF16)

        @pl.when(is_late_hub)
        def _():
            send_down8[0].wait_recv()
            send_cross8[0].wait_recv()
            send_part8[0][0].wait_recv()

            @pl.when(z == 6)
            def _():
                send_part8[1][0].wait_recv()
                crossed = parts8[0].astype(F32) + parts8[1].astype(F32)
                parts8[0] = crossed.astype(BF16)

            top_out[...] = (cross_c[...].astype(F32) + dot(parts8[0], map_b[...])).astype(BF16)
            start(send_above7)
            above[...] = top_out[...]

        @pl.when(both(z >= 4, z % 4 != 2))
        def _():
            send_above7[0].wait_recv()

        @pl.when(z >= 4)
        def _():
            above[...] = (cross_b[...] + dot(above[...], map_d[...])).astype(BF16)

        for s in range(2):
            outgoing[s] = (cross_sum[s] + dot(above[...], down[s, 0])).astype(BF16)
            start(send_above4[2 * s : 2 * s + 2])

    @pl.when(is_p3)
    def _():
        send_down4[0].wait_recv()
        send_cross4[0].wait_recv()
        for s in range(2):
            cross_sum[s] += dot(cross_a[...].astype(BF16), down[s, 0])
            down[s, 0] = dot(map_d[...], down[s, 0]).astype(BF16)
        send_above4[0].wait_recv()
        outgoing[0] = (cross_sum[0] + dot(above[...], down[0, 0])).astype(BF16)

        @pl.when(core == 0)
        def _():
            start(send_above2_left)

        @pl.when(core == 1)
        def _():
            start([send_above2_left[3], *send_above2_left[:3]])

        outgoing[1] = (cross_sum[1] + dot(above[...], down[1, 0])).astype(BF16)
        start(send_above2_right)
        leaf_above[...] = outgoing[1]

    @pl.when(both(is_even, jnp.logical_not(is_p8)))
    def _():
        send_cross1[0].wait_recv()
        send_down1[0].wait_recv()

    @pl.when(jnp.logical_not(is_p2))
    def _():
        send_cross2[0].wait_recv()
        send_down2[0].wait_recv()

    zero = dot(leaf_cross2[...].astype(BF16), leaf_map1[...]) + leaf_cross1[...]
    zero = jnp.where(leaf_keep, zero, 0.0).astype(BF16)
    product[...] += dot(zero, leaf_out[...])
    map_keep = lax.broadcasted_iota(jnp.int32, (width, leaf_width), 1) < leaf_rank
    leaf_map1[...] = jnp.where(map_keep, dot(leaf_map2[...], leaf_map1[...]), 0.0).astype(BF16)
    leaf_map2[...] = dot(leaf_map1[...], leaf_out[...]).astype(BF16)

    @pl.when(jnp.logical_not(is_p3))
    def _():
        send_above2_left[0].wait_recv()

    product[...] += dot(leaf_above[...], leaf_map2[...])

    def sent(condition, copies):
        @pl.when(condition)
        def _():
            for copy in copies:
                copy.wait_send()

    sent(is_even, [leaf_up])
    sent(is_p1, [up_left, *send_cross1, *send_down1])
    sent(is_p2, [up_left, *send_cross2, *send_down2])
    sent(both(is_p3, core == 0), [send_part4[0]])
    sent(is_p3, [up_left, *send_above2_left, *send_above2_right])
    sent(both(is_p4, core == 0), send_up4)
    sent(both(is_p4, core == 1), [up_left])
    sent(is_p4, [*send_cross4, *send_down4])
    sent(is_gate, [up_left, *send_above4])
    sent(both(is_gate, z % 4 != 2), [send_part6[0]])
    sent(is_hub, [send_coef7[0], send_child7])
    sent(is_late_hub, send_above7)
    sent(is_far_hub, send_part8[0])
    sent(is_left_center, [*send_cross8_first, send_cross8[1], *send_part8_right])
    sent(is_right_center, send_cross8)
    sent(is_p6, [send_down6[1], *send_cross6])
    sent(both(is_p6, both(z % 4 == 3, z != 7)), send_down6_half)
    sent(both(is_p6, jnp.logical_not(both(z % 4 == 3, z != 7))), [send_down6[0]])
    sent(is_p7, [send_top_up7, *send_down7[1:], *send_cross7])
    sent(is_p8, [send_top_cross, send_down8[1]])
    sent(is_left_p8, [send_top_up8, send_down8_first[2]])
    sent(is_right_p8, [*send_up8, send_down8[0]])
    sent(is_p9, send_cross9)


def on_device(rhs, diag_blocks, leaf_in, leaf_out, up_maps, cross_maps, down_maps, node_rank):
    rows, leaf = rhs.shape
    width, leaf_width = up_maps.shape[-1], leaf_in.shape[1]
    operands = (rhs, diag_blocks, leaf_in, leaf_out, up_maps, cross_maps, down_maps)

    def vector(*lead, kind=BF16, columns=width):
        return pltpu.VMEM((*lead, rows, columns), kind)

    full_map = pltpu.VMEM((width, width), BF16)
    return pl.pallas_call(
        kernel,
        out_shape=jax.ShapeDtypeStruct((rows, leaf), F32),
        in_specs=[pl.BlockSpec(memory_space=pl.ANY)] * 8,
        out_specs=pl.BlockSpec(memory_space=pltpu.VMEM),
        scratch_shapes=[pltpu.VMEM(each.shape, each.dtype) for each in operands]
        + [
            pltpu.SMEM(node_rank.shape, node_rank.dtype),
            vector(columns=leaf_width),
            vector(),
            vector(columns=2 * width),
            vector(2, kind=F32),
            vector(),
            vector(2),
            full_map,
            full_map,
            full_map,
            full_map,
            full_map,
            full_map,
            pltpu.VMEM(up_maps.shape, BF16),
            pltpu.VMEM(cross_maps.shape, BF16),
            vector(columns=2 * width),
            vector(),
            vector(2),
            vector(),
            vector(),
            pltpu.VMEM((2, width, width), BF16),
            full_map,
            pltpu.VMEM((width, leaf_width), BF16),
            vector(kind=F32),
            vector(kind=F32),
            vector(),
            vector(kind=F32),
            vector(kind=F32, columns=leaf_width),
            vector(),
            vector(),
            vector(2),
            vector(4),
            vector(2),
            pltpu.SemaphoreType.DMA((8,)),
            pltpu.SemaphoreType.DMA((22,)),
            pltpu.SemaphoreType.DMA((29,)),
            pltpu.SemaphoreType.REGULAR,
            pltpu.SemaphoreType.REGULAR,
        ],
        compiler_params=pltpu.CompilerParams(
            collective_id=0, has_side_effects=True, vmem_limit_bytes=60 * 2**20
        ),
    )(*operands, node_rank)


def solution(mesh):
    assert mesh.shape["tx"] == N_Z * N_CORE and mesh.shape["ty"] == N_X * N_Y
    in_specs = (
        P(None, ("tx", "ty")),
        P(("tx", "ty"), None),
        P(("tx", "ty"), None),
        P(("tx", "ty"), None),
        P(None, ("tx", "ty"), None, None),
        P(None, ("tx", "ty"), None, None),
        P(None, ("tx", "ty"), None, None),
        P(("tx", "ty"), None),
    )
    return jax.shard_map(
        on_device, mesh=mesh, in_specs=in_specs, out_specs=P(None, ("tx", "ty")), check_vma=False
    )
```

```python
import functools

import jax
import jax.numpy as jnp
from jax import lax
from jax.experimental import pallas as pl
from jax.experimental.pallas import tpu as pltpu
from jax.sharding import PartitionSpec as P

MESH = pl.DeviceIdType.MESH
F32 = jnp.float32
BF16 = jnp.bfloat16
N_Z, N_CORE, N_X, N_Y = 16, 2, 4, 4


def kernel(
    rhs_hbm,
    diag_hbm,
    in_hbm,
    out_hbm,
    up_hbm,
    cross_hbm,
    down_hbm,
    rank_hbm,
    product,
    rhs,
    diag,
    leaf_in,
    leaf_out,
    up,
    cross,
    down,
    rank,
    leaf_coef,
    coef,
    child,
    cross_sum,
    path_coef,
    outgoing,
    map_a,
    map_b,
    map_c,
    map_d,
    map_e,
    map_f,
    top_up,
    top_cross,
    top_child,
    top_coef,
    top_sum,
    top_out,
    far_out,
    gate_up,
    head_map,
    head_base,
    head_out,
    leaf_map2,
    leaf_map1,
    cross_a,
    cross_b,
    cross_c,
    leaf_cross2,
    leaf_cross1,
    above,
    leaf_above,
    parts4,
    parts6,
    parts8,
    load_sem,
    send_sem,
    recv_sem,
    go_sem,
    late_sem,
):
    rows, width = coef.shape
    leaf_width = leaf_coef.shape[1]
    tx, ty = lax.axis_index("tx"), lax.axis_index("ty")
    z, core = tx // N_CORE, tx % N_CORE
    x, y = ty // N_Y, ty % N_Y

    def at(z, core, x, y):
        return (z * N_CORE + core, x * N_Y + y)

    both = jnp.logical_and
    on_line = ty == 0
    on_top = both(on_line, core == 0)
    is_p1 = y % 2 == 1
    is_p2 = y == 2
    is_p3 = both(y == 0, x % 2 == 1)
    is_p4 = both(y == 0, x == 2)
    is_gate = both(on_line, core == 1)
    is_p6 = both(on_top, z % 2 == 1)
    is_p7 = both(on_top, z % 4 == 2)
    is_p8 = both(on_top, z % 8 == 4)
    is_p9 = both(on_top, z == 8)
    is_even = y % 2 == 0
    is_head = both(y == 0, x % 2 == 0)
    is_hub = both(is_gate, z % 4 == 2)
    is_late_hub = both(is_hub, z > 2)
    is_far_hub = both(is_hub, z >= 8)
    is_left_center = both(is_gate, z == 4)
    is_right_center = both(is_gate, z == 12)
    is_left_p8 = both(on_top, z == 4)
    is_right_p8 = both(on_top, z == 12)

    loads = [
        pltpu.make_async_copy(source, target, load_sem.at[n])
        for n, (source, target) in enumerate(
            (
                (rhs_hbm, rhs),
                (in_hbm, leaf_in),
                (rank_hbm, rank),
                (up_hbm, up),
                (cross_hbm, cross),
                (down_hbm, down),
                (diag_hbm, diag),
                (out_hbm, leaf_out),
            )
        )
    ]
    load_rhs, load_in, load_rank, load_up, load_cross, load_down, load_diag, load_out = loads
    for load in loads[:3]:
        load.start()

    x_odd = x // 2 * 2 + 1
    z_odd, z_seven, z_eight = z // 2 * 2 + 1, z // 4 * 4 + 2, z // 8 * 8 + 4
    leaf_peer = at(z, core, x, y + 1)
    left_leaf = at(z, core, x, y - 1)
    column = [at(z, core, x, k) for k in range(N_Y)]
    my_p3 = at(z, core, x_odd, 0)
    p3s = [at(z, core, 1, 0), at(z, core, 3, 0)]
    p4 = at(z, core, 2, 0)
    gate = at(z, 1, 0, 0)
    p3s_of_gate = [at(z, c, k, 0) for c in range(N_CORE) for k in (1, 3)]
    p4s_of_gate = [at(z, c, 2, 0) for c in range(N_CORE)]
    p6, p7, p8 = at(z_odd, 0, 0, 0), at(z_seven, 0, 0, 0), at(z_eight, 0, 0, 0)
    gates_of_p6 = [at(z_odd - 1, 1, 0, 0), at(z_odd, 1, 0, 0)]
    gates_of_p7 = [at(z_seven - 2 + k, 1, 0, 0) for k in range(4)]
    hub, center = at(z_seven, 1, 0, 0), at(z_eight, 1, 0, 0)
    hubs_of_center = [at(z_eight - 2, 1, 0, 0), at(z_eight + 2, 1, 0, 0)]
    first_gates = [at(k, 1, 0, 0) for k in range(6)]
    second_hub, third_hub, fourth_hub = at(6, 1, 0, 0), at(10, 1, 0, 0), at(14, 1, 0, 0)

    barrier = pltpu.get_barrier_semaphore()

    def greet(condition, devices):
        @pl.when(condition)
        def _():
            for device in devices:
                pl.semaphore_signal(barrier, inc=1, device_id=device, device_id_type=MESH)

    def collector(z, core, x):
        return at(z, core, x, 1)

    x_even = x % 2 == 0
    next_p3 = collector(z, core, x_odd)
    greet(is_p1, [left_leaf])
    greet(y == 1, [column[3]])
    greet(y == 3, [collector(z, core, x)])
    greet(is_p2, [column[1], column[3]])
    greet(both(is_p2, x % 2 == 1), [column[1]])
    greet(on_top, [collector(z, 1, 0)])
    greet(y == 0, [column[1], column[3]])
    greet(both(y == 0, x_even), [next_p3])
    greet(is_p3, [at(z, core, x - 1, 3), collector(z, core, 2), collector(z, 1, 0)])
    greet(is_p4, [collector(z, core, 1), collector(z, core, 3), collector(z, 1, 0)])
    greet(is_gate, [collector(z, 0, 1), collector(z, 0, 3), collector(z, 1, 2)] + [collector(z_odd, 0, 0), collector(z_seven, 0, 0)])
    greet(both(is_gate, z % 4 == 0), [collector(z + 1, 1, 0)])
    greet(both(is_gate, both(z < 6, z != 4)), [collector(4, 0, 0), collector(8, 0, 0), collector(4, 1, 0)])
    greet(both(both(is_gate, z > 6), z % 4 != 2), [collector(z_seven, 1, 0)])
    greet(is_hub, [collector(z_seven - 2 + k, 1, 0) for k in (0, 1, 3)])
    greet(is_late_hub, [collector(z_eight, 0, 0), collector(z_eight, 1, 0)])
    greet(both(is_late_hub, z < 12), [collector(8, 0, 0)])
    greet(both(is_late_hub, z > 12), [collector(4, 1, 0), collector(8, 1, 0)])
    greet(is_p9, [collector(8, 1, 0)])
    greet(
        both(is_gate, z % 8 == 4),
        [collector(z_eight - 2, 1, 0), collector(z_eight + 2, 1, 0), collector(z, 0, 0)],
    )
    greet(is_left_center, [collector(8, 0, 0)])
    greet(is_p6, [collector(z_odd - 1, 1, 0), collector(z_odd, 1, 0)])
    greet(is_p7, [collector(z, 1, 0)])
    greet(is_right_p8, [collector(z, 1, 0)])
    sizes = (
        (is_even, 1),
        (y == 3, 3),
        (both(y == 3, x_even), 1),
        (y == 1, 2),
        (both(y == 1, x_even), 1),
        (both(y == 1, x % 2 == 1), 4),
        (both(both(y == 1, x % 2 == 1), core == 0), 1),
        (both(y == 1, x == 2), 2 + core),
        (both(ty == 1, core == 1), 8),
        (both(both(ty == 1, core == 1), z % 4 != 2), 1),
        (both(both(ty == 1, core == 1), z % 4 == 1), 1),
        (both(both(ty == 1, core == 1), z % 4 == 2), 2),
        (both(both(ty == 1, core == 1), z == 6), 1),
        (both(both(ty == 1, core == 1), both(z % 4 == 2, z > 6)), 3),
        (both(both(ty == 1, core == 1), z == 4), 7),
        (both(both(ty == 1, core == 1), z == 12), 3),
        (both(both(ty == 1, core == 1), z == 8), 2),
        (both(both(ty == 1, core == 0), z % 2 == 1), 2),
        (both(both(ty == 1, core == 0), z % 4 == 2), 4),
        (both(both(ty == 1, core == 0), z == 4), 7),
        (both(both(ty == 1, core == 0), z == 12), 3),
        (both(both(ty == 1, core == 0), z == 8), 8),
    )
    greeted = sum(condition.astype(jnp.int32) * size for condition, size in sizes)
    for load in loads[3:]:
        load.start()

    def remote(source, target, send, recv, device):
        return pltpu.make_async_remote_copy(
            src_ref=source,
            dst_ref=target,
            send_sem=send_sem.at[send],
            recv_sem=recv_sem.at[recv],
            device_id=device,
            device_id_type=MESH,
        )

    left_part, right_part = pl.ds(0, width), pl.ds(width, width)
    narrow = pl.ds(0, leaf_width)

    leaf_up = remote(leaf_coef, child.at[:, narrow], 0, 0, leaf_peer)
    side = jnp.where(
        is_p1,
        y // 2,
        jnp.where(is_p2, x % 2, jnp.where(is_p3, x // 2, jnp.where(is_p4, core, z % 2))),
    )
    steps = ((is_p1, column[2]), (is_p2, my_p3), (is_p3, p4), (is_p4, gate), (is_gate, p6))
    parent = tuple(sum(condition.astype(jnp.int32) * device[k] for condition, device in steps) for k in range(2))
    up_left = remote(coef, child.at[:, left_part], 1, 0, parent)
    up_right = remote(coef, child.at[:, right_part], 1, 1, parent)
    send_cross1 = [remote(cross_sum.at[0, :, narrow], leaf_cross1, 2, 2, left_leaf)]
    send_down1 = [remote(down.at[0, 0, :, narrow], leaf_map1, 3, 3, left_leaf)]
    sides2 = ((0, 0), (1, 0), (3, 1))
    send_cross2 = [remote(cross_sum.at[s], leaf_cross2, 2 + n, 4, column[k]) for n, (k, s) in enumerate(sides2)]
    send_down2 = [remote(down.at[s, 0], leaf_map2, 5 + n, 5, column[k]) for n, (k, s) in enumerate(sides2)]
    send_cross4 = [remote(cross_sum.at[s], cross_a, 2 + s, 11, p3s[s]) for s in range(2)]
    send_up4 = [remote(up.at[s, 0], map_a, 7 + s, 7, p3s[s]) for s in range(2)]
    send_part4 = [remote(path_coef, parts4.at[k], 9, 21 + k, gate) for k in range(2)]
    send_down4 = [remote(down.at[s, 0], map_d, 5 + s, 10, p3s[s]) for s in range(2)]
    send_cross6 = [remote(cross_sum.at[s], cross_b, 2 + s, 12, gates_of_p6[s]) for s in range(2)]
    send_up6 = [remote(up.at[s, 0], map_a, 4 + s, 7, gates_of_p6[s]) for s in range(2)]
    send_down6 = [remote(down.at[s, 0], map_c, 6 + s, 9, gates_of_p6[s]) for s in range(2)]
    halves = [pl.ds(k * (width // 2), width // 2) for k in range(2)]
    send_down6_half = [remote(down.at[0, 0, half], map_c.at[half], (6, 8)[k], 9, gates_of_p6[0]) for k, half in enumerate(halves)]
    send_cross7 = [remote(cross_sum.at[k // 2], cross_a, 2 + k, 11, gates_of_p7[k]) for k in range(4)]
    send_down7 = [remote(down.at[k // 2, 0], map_d, 10 + k, 10, gates_of_p7[k]) for k in range(4)]
    pass_down7 = remote(map_d, map_d, 22, 10, at(z - 1, 1, 0, 0))
    send_cross8 = [remote(top_sum.at[s], cross_c, 16 + s, 20, hubs_of_center[s]) for s in range(2)]
    send_cross8_first = [remote(top_sum.at[0], cross_c, 18 + k, 20, first_gates[k]) for k in range(4)]
    send_cross8_first += [remote(top_sum.at[1], cross_c, 13, 20, first_gates[5])]
    send_top_up7 = remote(up, top_up, 6, 23, hub)
    send_top_up8 = remote(up, top_up, 4, 23, center)
    send_top_cross = remote(cross, top_cross, 8, 24, center)
    send_up8 = [remote(up.at[s, 0], map_e, 4 + s, 27, hubs_of_center[s]) for s in range(2)]
    send_down8 = [remote(down.at[s, 0], map_b, 6 + s, 8, hubs_of_center[s]) for s in range(2)]
    send_down8_first = [remote(down.at[k // 4, 0], map_b, 14 + k, 8, first_gates[k]) for k in range(6)]
    pass_down8 = remote(map_b, map_b, 8, 8, at(z - 1, 1, 0, 0))
    send_cross9 = [remote(cross.at[0, 0], map_f, 2, 28, third_hub), remote(cross.at[0, 0], map_f, 3, 28, fourth_hub)]
    send_cross9 += [remote(cross.at[1, 0], map_f, 4, 28, at(4, 1, 0, 0))]
    send_part6 = [remote(path_coef, parts6.at[k], 2, 14 + k, hub) for k in range(4)]
    send_child7 = remote(top_child, child, 9, 0, p7)
    send_coef7 = [remote(top_coef, top_child.at[:, part], 10, 25 + k, center) for k, part in enumerate((left_part, right_part))]
    send_part8 = [
        [remote(far_out, parts8.at[k], 11 + n, 18 + k, device) for n, device in enumerate((*first_gates, second_hub))]
        for k in range(2)
    ]
    send_part8_right = [remote(far_out, parts8.at[0], 11 + k, 18, (third_hub, fourth_hub)[k]) for k in range(2)]
    send_above7 = [remote(top_out, above, 18 + n, 13, gates_of_p7[k]) for n, k in enumerate((3, 0, 1))]
    others = [at(z, 0, 2, 0), p3s_of_gate[1], at(z, 0, 0, 0), p3s_of_gate[0], at(z, 1, 2, 0), p3s_of_gate[3], p3s_of_gate[2]]
    above4_sems = (3, 4, 5, 6, 7, 23, 24)
    send_above4 = [remote(outgoing.at[n // 4], above, above4_sems[n], 13, device) for n, device in enumerate(others)]
    head = at(z, core, x - 1, 0)
    send_head_map = remote(head_map, head_map, 2, 29, head)
    send_head_base = remote(cross_sum.at[0], head_base, 3, 30, head)
    send_above2 = [remote(head_out, leaf_above, 24 + k, 6, column[k]) for k in (3, 2, 1)]
    send_above2_right = [remote(outgoing.at[1], leaf_above, 5 + k, 6, column[k]) for k in (3, 2, 1)]

    def start(copies):
        for copy in copies:
            copy.start()

    def dot(a, b):
        return jnp.dot(a, b, preferred_element_type=F32)

    load_rhs.wait()
    load_in.wait()
    load_rank.wait()
    leaf_rank, node_rank = rank[0, 0], rank[0, 1]
    leaf_keep = lax.broadcasted_iota(jnp.int32, (rows, leaf_width), 1) < leaf_rank
    node_keep = lax.broadcasted_iota(jnp.int32, (rows, width), 1) < node_rank
    leaf_coef[...] = jnp.where(leaf_keep, dot(rhs[...], leaf_in[...]), 0.0).astype(BF16)

    pl.semaphore_wait(barrier, greeted)

    @pl.when(is_p1)
    def _():
        pl.semaphore_signal(go_sem, inc=1, device_id=left_leaf, device_id_type=MESH)

    @pl.when(both(both(ty == 1, core == 1), z == 8))
    def _():
        pl.semaphore_signal(late_sem, inc=1, device_id=at(8, 0, 0, 0), device_id_type=MESH)

    def mask_up():
        keep = lax.broadcasted_iota(jnp.int32, (width, width), 1) < node_rank
        for s in range(2):
            up[s, 0] = jnp.where(keep, up[s, 0], jnp.zeros((width, width), BF16))

    def mask_down():
        keep = lax.broadcasted_iota(jnp.int32, (width, width), 0) < node_rank
        for s in range(2):
            down[s, 0] = jnp.where(keep, down[s, 0], jnp.zeros((width, width), BF16))

    def send_up(summed, waits=False):
        coef[...] = jnp.where(node_keep, summed, 0.0).astype(BF16)
        if waits:
            pl.semaphore_wait(go_sem, 1)

        @pl.when(side == 0)
        def _():
            up_left.start()

        @pl.when(side == 1)
        def _():
            up_right.start()

    def cross_terms():
        cross_sum[0] = dot(child[:, right_part], cross[0, 0])
        cross_sum[1] = dot(child[:, left_part], cross[1, 0])

    @pl.when(is_even)
    def _():
        leaf_up.start()

    @pl.when(on_line)
    def _():
        pl.semaphore_wait(go_sem, 1)

    @pl.when(is_p1)
    def _():
        load_up.wait()
        summed = dot(leaf_coef[...], up[1, 0, narrow, :])
        leaf_up.wait_recv()
        send_up(summed + dot(child[:, narrow], up[0, 0, narrow, :]))
        load_cross.wait()
        cross_sum[0, :, narrow] = dot(leaf_coef[...], cross[0, 0, narrow, narrow])
        leaf_cross1[...] = dot(child[:, narrow], cross[1, 0, narrow, narrow])
        start(send_cross1)
        load_down.wait()
        mask_down()
        start(send_down1)
        leaf_map1[...] = down[1, 0, :, narrow]

    def lift(waits=True):
        up_left.wait_recv()
        summed = dot(child[:, left_part], up[0, 0])
        up_right.wait_recv()
        send_up(summed + dot(child[:, right_part], up[1, 0]), waits)

    @pl.when(is_p2)
    def _():
        load_up.wait()
        lift()
        load_cross.wait()
        cross_terms()
        start(send_cross2)
        leaf_cross2[...] = cross_sum[1]
        load_down.wait()
        mask_down()
        start(send_down2)
        leaf_map2[...] = down[1, 0]

    @pl.when(is_p3)
    def _():
        load_up.wait()
        lift()

        @pl.when(core == 0)
        def _():
            send_up4[0].wait_recv()
            path_coef[...] = dot(coef[...], map_a[...]).astype(BF16)
            for k in range(2):

                @pl.when(x // 2 == k)
                def _():
                    send_part4[k].start()

        load_cross.wait()
        cross_terms()
        load_down.wait()
        mask_down()

    @pl.when(is_p4)
    def _():
        load_up.wait()
        mask_up()
        pl.semaphore_wait(go_sem, 1)

        @pl.when(core == 0)
        def _():
            start(send_up4)
            load_down.wait()
            mask_down()
            start(send_down4)
            up_left.wait_recv()
            up_right.wait_recv()

        @pl.when(core == 1)
        def _():
            lift(waits=False)

        load_cross.wait()
        cross_terms()
        start(send_cross4)

        @pl.when(core == 1)
        def _():
            load_down.wait()
            mask_down()
            start(send_down4)

    @pl.when(is_gate)
    def _():
        load_up.wait()
        load_cross.wait()
        load_down.wait()
        mask_down()

        @pl.when(z % 4 == 1)
        def _():
            send_down7[0].wait_recv()
            pass_down7.start()

        map_keep = lax.broadcasted_iota(jnp.int32, (width, width), 1) < node_rank
        send_up6[0].wait_recv()
        for s in range(2):
            ahead = dot(jnp.where(map_keep, up[s, 0], jnp.zeros((width, width), BF16)), map_a[...])
            gate_up[s] = ahead.astype(BF16)
        for copy in send_part4:
            copy.wait_recv()
        child[:, left_part] = (parts4[0].astype(F32) + parts4[1].astype(F32)).astype(BF16)
        up_right.wait_recv()
        six = dot(child[:, left_part], gate_up[0]) + dot(child[:, right_part], gate_up[1])
        path_coef[...] = six.astype(BF16)
        for k in (0, 1, 3):

            @pl.when(z % 4 == k)
            def _():
                send_part6[k].start()

        send_up(dot(child[:, left_part], up[0, 0]) + dot(child[:, right_part], up[1, 0]))

        @pl.when(is_hub)
        def _():
            parts6[2] = path_coef[...]
            send_top_up7.wait_recv()

            @pl.when(is_far_hub)
            def _():
                send_up8[0].wait_recv()
                send_cross9[0].wait_recv()
                map_e[...] = dot(map_e[...], map_f[...]).astype(BF16)

            for k in (0, 1, 3):
                send_part6[k].wait_recv()
            for k, part in enumerate((left_part, right_part)):
                six = parts6[2 * k].astype(F32) + parts6[2 * k + 1].astype(F32)
                top_child[:, part] = six.astype(BF16)
            seven = dot(top_child[:, left_part], top_up[0, 0]) + dot(top_child[:, right_part], top_up[1, 0])
            top_coef[...] = seven.astype(BF16)
            for k in range(2):

                @pl.when(z // 4 % 2 == k)
                def _():
                    send_coef7[k].start()

            @pl.when(is_far_hub)
            def _():
                far_out[...] = dot(top_coef[...], map_e[...]).astype(BF16)
                for k in range(2):

                    @pl.when(z == 10 + 4 * k)
                    def _():
                        start(send_part8[k])

            send_child7.start()

        def center_cross_terms():
            send_top_cross.wait_recv()
            top_sum[0] = dot(top_child[:, right_part], top_cross[0, 0]).astype(BF16)
            top_sum[1] = dot(top_child[:, left_part], top_cross[1, 0]).astype(BF16)

        @pl.when(is_left_center)
        def _():
            send_top_up8.wait_recv()
            send_coef7[0].wait_recv()
            send_coef7[1].wait_recv()
            center_cross_terms()
            start(send_cross8_first)
            send_cross8[1].start()
            cross_c[...] = top_sum[1]
            eight = dot(top_child[:, left_part], top_up[0, 0]) + dot(top_child[:, right_part], top_up[1, 0])
            top_coef[...] = eight.astype(BF16)
            send_cross9[2].wait_recv()
            far_out[...] = dot(top_coef[...], map_f[...]).astype(BF16)
            start(send_part8_right)

        @pl.when(is_right_center)
        def _():
            pl.semaphore_signal(late_sem, inc=1, device_id=p8, device_id_type=MESH)
            send_coef7[1].wait_recv()
            send_coef7[0].wait_recv()
            center_cross_terms()
            start(send_cross8)

        cross_terms()

        @pl.when(z == 1)
        def _():
            send_down8_first[0].wait_recv()
            pass_down8.start()

    @pl.when(is_p6)
    def _():
        load_up.wait()
        mask_up()
        start(send_up6)
        load_cross.wait()
        load_down.wait()
        mask_down()
        for copy in send_up6:
            copy.wait_send()
        send_down6[1].start()

        @pl.when(z % 4 == 1)
        def _():
            send_down6[0].start()

        @pl.when(both(z % 4 == 3, z != 7))
        def _():
            send_down6_half[0].start()

        up_right.wait_recv()

        @pl.when(both(z % 4 == 3, z != 7))
        def _():
            send_down6_half[1].start()

        @pl.when(z == 7)
        def _():
            send_down6[0].start()

        up_left.wait_recv()
        cross_terms()
        start(send_cross6)

    @pl.when(is_p7)
    def _():
        load_up.wait()
        mask_up()
        send_top_up7.start()
        load_down.wait()
        mask_down()
        start(send_down7[1:])
        load_cross.wait()
        send_child7.wait_recv()
        cross_terms()
        start(send_cross7)

    @pl.when(is_p8)
    def _():
        load_up.wait()
        mask_up()
        load_cross.wait()
        send_top_cross.start()
        load_down.wait()
        mask_down()

        @pl.when(is_left_p8)
        def _():
            send_down8[1].start()
            start(send_down8_first[4:])

        @pl.when(is_right_p8)
        def _():
            send_up8[1].start()

        send_cross1[0].wait_recv()

        @pl.when(is_right_p8)
        def _():
            send_down1[0].wait_recv()
            send_up8[0].start()
            pl.semaphore_wait(late_sem, 1)
            start(send_down8)

        @pl.when(is_left_p8)
        def _():
            send_top_up8.start()
            send_down8_first[1].start()
            send_down1[0].wait_recv()
            for k, after in ((1, 3), (3, 2)):
                send_down8_first[k].wait_send()
                send_down8_first[after].start()

    @pl.when(both(on_top, z % 8 == 0))
    def _():
        load_up.wait()
        load_cross.wait()
        load_down.wait()

    @pl.when(is_p9)
    def _():
        send_cross9[0].start()
        send_cross9[2].start()
        pl.semaphore_wait(late_sem, 1)
        send_cross9[1].start()

    load_diag.wait()
    product[...] = dot(rhs[...], diag[...])
    load_out.wait()

    @pl.when(is_gate)
    def _():
        @pl.when(z % 4 != 1)
        def _():
            send_down7[0].wait_recv()

        @pl.when(z % 4 == 1)
        def _():
            pass_down7.wait_send()

        send_down6[0].wait_recv()
        map_d[...] = dot(map_d[...], map_c[...]).astype(BF16)

        @pl.when(both(z < 6, z != 1))
        def _():
            send_down8_first[0].wait_recv()

        @pl.when(z == 1)
        def _():
            pass_down8.wait_send()

        @pl.when(z < 6)
        def _():
            map_b[...] = dot(map_b[...], map_d[...]).astype(BF16)

        send_cross7[0].wait_recv()
        send_cross6[0].wait_recv()
        cross_b[...] += dot(cross_a[...].astype(BF16), map_c[...])

        @pl.when(z < 6)
        def _():
            @pl.when(z != 4)
            def _():
                send_cross8_first[0].wait_recv()

            cross_b[...] += dot(cross_c[...], map_d[...])
            for k in range(2):
                send_part8[k][0].wait_recv()
            crossed = (parts8[0].astype(F32) + parts8[1].astype(F32)).astype(BF16)
            above[...] = (cross_b[...] + dot(crossed, map_b[...])).astype(BF16)

        @pl.when(is_late_hub)
        def _():
            send_down8[0].wait_recv()
            send_cross8[0].wait_recv()
            send_part8[0][0].wait_recv()

            @pl.when(z == 6)
            def _():
                send_part8[1][0].wait_recv()
                crossed = parts8[0].astype(F32) + parts8[1].astype(F32)
                parts8[0] = crossed.astype(BF16)

            top_out[...] = (cross_c[...].astype(F32) + dot(parts8[0], map_b[...])).astype(BF16)
            send_above7[0].start()

            @pl.when(z > 6)
            def _():
                start(send_above7[1:])

            above[...] = top_out[...]

        @pl.when(both(z > 6, z % 4 != 2))
        def _():
            send_above7[0].wait_recv()

        @pl.when(z >= 6)
        def _():
            above[...] = (cross_b[...] + dot(above[...], map_d[...])).astype(BF16)

        for s in range(2):
            outgoing[s] = (cross_sum[s] + dot(above[...], down[s, 0])).astype(BF16)
            start(send_above4[4 * s : 4 * s + 4])

    @pl.when(is_p3)
    def _():
        send_down4[0].wait_recv()
        head_map[...] = dot(map_d[...], down[0, 0]).astype(BF16)
        send_head_map.start()
        send_cross4[0].wait_recv()
        cross_four = cross_a[...].astype(BF16)
        cross_sum[0] += dot(cross_four, down[0, 0])
        send_head_base.start()
        cross_sum[1] += dot(cross_four, down[1, 0])
        down[1, 0] = dot(map_d[...], down[1, 0]).astype(BF16)
        send_above4[0].wait_recv()
        outgoing[1] = (cross_sum[1] + dot(above[...], down[1, 0])).astype(BF16)
        start(send_above2_right)
        leaf_above[...] = outgoing[1]

    @pl.when(is_head)
    def _():
        send_head_map.wait_recv()
        send_head_base.wait_recv()

        @pl.when(is_gate)
        def _():
            head_out[...] = (head_base[...] + dot(outgoing[1], head_map[...])).astype(BF16)

        @pl.when(jnp.logical_not(is_gate))
        def _():
            send_above4[0].wait_recv()
            head_out[...] = (head_base[...] + dot(above[...], head_map[...])).astype(BF16)

        start(send_above2)
        leaf_above[...] = head_out[...]

    @pl.when(both(is_even, jnp.logical_not(is_p8)))
    def _():
        send_cross1[0].wait_recv()
        send_down1[0].wait_recv()

    @pl.when(jnp.logical_not(is_p2))
    def _():
        send_cross2[0].wait_recv()
        send_down2[0].wait_recv()

    zero = dot(leaf_cross2[...].astype(BF16), leaf_map1[...]) + leaf_cross1[...]
    zero = jnp.where(leaf_keep, zero, 0.0).astype(BF16)
    product[...] += dot(zero, leaf_out[...])
    map_keep = lax.broadcasted_iota(jnp.int32, (width, leaf_width), 1) < leaf_rank
    leaf_map1[...] = jnp.where(map_keep, dot(leaf_map2[...], leaf_map1[...]), 0.0).astype(BF16)
    leaf_map2[...] = dot(leaf_map1[...], leaf_out[...]).astype(BF16)

    @pl.when(y > 0)
    def _():
        send_above2[0].wait_recv()

    product[...] += dot(leaf_above[...], leaf_map2[...])

    def sent(condition, copies):
        @pl.when(condition)
        def _():
            for copy in copies:
                copy.wait_send()

    sent(is_even, [leaf_up])
    sent(is_p1, [up_left, *send_cross1, *send_down1])
    sent(is_p2, [up_left, *send_cross2, *send_down2])
    sent(both(is_p3, core == 0), [send_part4[0]])
    sent(is_p3, [up_left, send_head_map, send_head_base, *send_above2_right])
    sent(is_head, send_above2)
    sent(both(is_p4, core == 0), send_up4)
    sent(both(is_p4, core == 1), [up_left])
    sent(is_p4, [*send_cross4, *send_down4])
    sent(is_gate, [up_left, *send_above4])
    sent(both(is_gate, z % 4 != 2), [send_part6[0]])
    sent(is_hub, [send_coef7[0], send_child7])
    sent(is_late_hub, send_above7[:1])
    sent(is_far_hub, send_above7[1:])
    sent(is_far_hub, send_part8[0])
    sent(is_left_center, [*send_cross8_first, send_cross8[1], *send_part8_right])
    sent(is_right_center, send_cross8)
    sent(is_p6, [send_down6[1], *send_cross6])
    sent(both(is_p6, both(z % 4 == 3, z != 7)), send_down6_half)
    sent(both(is_p6, jnp.logical_not(both(z % 4 == 3, z != 7))), [send_down6[0]])
    sent(is_p7, [send_top_up7, *send_down7[1:], *send_cross7])
    sent(is_p8, [send_top_cross, send_down8[1]])
    sent(is_left_p8, [send_top_up8, send_down8_first[2], *send_down8_first[4:]])
    sent(is_right_p8, [*send_up8, send_down8[0]])
    sent(is_p9, send_cross9)


def on_device(rhs, diag_blocks, leaf_in, leaf_out, up_maps, cross_maps, down_maps, node_rank):
    rows, leaf = rhs.shape
    width, leaf_width = up_maps.shape[-1], leaf_in.shape[1]
    operands = (rhs, diag_blocks, leaf_in, leaf_out, up_maps, cross_maps, down_maps)

    def vector(*lead, kind=BF16, columns=width):
        return pltpu.VMEM((*lead, rows, columns), kind)

    full_map = pltpu.VMEM((width, width), BF16)
    return pl.pallas_call(
        kernel,
        out_shape=jax.ShapeDtypeStruct((rows, leaf), F32),
        in_specs=[pl.BlockSpec(memory_space=pl.ANY)] * 8,
        out_specs=pl.BlockSpec(memory_space=pltpu.VMEM),
        scratch_shapes=[pltpu.VMEM(each.shape, each.dtype) for each in operands]
        + [
            pltpu.SMEM(node_rank.shape, node_rank.dtype),
            vector(columns=leaf_width),
            vector(),
            vector(columns=2 * width),
            vector(2, kind=F32),
            vector(),
            vector(2),
            full_map,
            full_map,
            full_map,
            full_map,
            full_map,
            full_map,
            pltpu.VMEM(up_maps.shape, BF16),
            pltpu.VMEM(cross_maps.shape, BF16),
            vector(columns=2 * width),
            vector(),
            vector(2),
            vector(),
            vector(),
            pltpu.VMEM((2, width, width), BF16),
            full_map,
            vector(kind=F32),
            vector(),
            full_map,
            pltpu.VMEM((width, leaf_width), BF16),
            vector(kind=F32),
            vector(kind=F32),
            vector(),
            vector(kind=F32),
            vector(kind=F32, columns=leaf_width),
            vector(),
            vector(),
            vector(2),
            vector(4),
            vector(2),
            pltpu.SemaphoreType.DMA((8,)),
            pltpu.SemaphoreType.DMA((28,)),
            pltpu.SemaphoreType.DMA((31,)),
            pltpu.SemaphoreType.REGULAR,
            pltpu.SemaphoreType.REGULAR,
        ],
        compiler_params=pltpu.CompilerParams(
            collective_id=0, has_side_effects=True, vmem_limit_bytes=60 * 2**20
        ),
    )(*operands, node_rank)


def solution(mesh):
    assert mesh.shape["tx"] == N_Z * N_CORE and mesh.shape["ty"] == N_X * N_Y
    in_specs = (
        P(None, ("tx", "ty")),
        P(("tx", "ty"), None),
        P(("tx", "ty"), None),
        P(("tx", "ty"), None),
        P(None, ("tx", "ty"), None, None),
        P(None, ("tx", "ty"), None, None),
        P(None, ("tx", "ty"), None, None),
        P(("tx", "ty"), None),
    )
    return jax.shard_map(
        on_device, mesh=mesh, in_specs=in_specs, out_specs=P(None, ("tx", "ty")), check_vma=False
    )
```

```python
import functools

import jax
import jax.numpy as jnp
from jax import lax
from jax.experimental import pallas as pl
from jax.experimental.pallas import tpu as pltpu
from jax.sharding import PartitionSpec as P

MESH = pl.DeviceIdType.MESH
F32 = jnp.float32
BF16 = jnp.bfloat16
N_Z, N_CORE, N_X, N_Y = 16, 2, 4, 4


def kernel(
    rhs_hbm,
    diag_hbm,
    in_hbm,
    out_hbm,
    up_hbm,
    cross_hbm,
    down_hbm,
    rank_hbm,
    product,
    rhs,
    diag,
    leaf_in,
    leaf_out,
    up,
    cross,
    down,
    rank,
    leaf_coef,
    coef,
    child,
    cross_sum,
    path_coef,
    outgoing,
    map_a,
    map_b,
    map_c,
    map_d,
    map_e,
    map_f,
    top_up,
    top_cross,
    top_child,
    top_coef,
    top_sum,
    top_out,
    far_out,
    gate_maps,
    head_map,
    head_base,
    head_out,
    leaf_map2,
    leaf_map1,
    cross_a,
    cross_b,
    cross_c,
    leaf_cross2,
    leaf_cross1,
    above,
    leaf_above,
    parts4,
    parts6,
    parts8,
    load_sem,
    send_sem,
    recv_sem,
    go_sem,
    late_sem,
):
    rows, width = coef.shape
    leaf_width = leaf_coef.shape[1]
    loads = [
        pltpu.make_async_copy(source, target, load_sem.at[n])
        for n, (source, target) in enumerate(
            (
                (rhs_hbm, rhs),
                (in_hbm, leaf_in),
                (rank_hbm, rank),
                (up_hbm, up),
                (cross_hbm, cross),
                (down_hbm, down),
                (diag_hbm, diag),
                (out_hbm, leaf_out),
            )
        )
    ]
    load_rhs, load_in, load_rank, load_up, load_cross, load_down, load_diag, load_out = loads
    quarter = in_hbm.shape[0] // 4
    for n in range(4):
        part = pl.ds(n * quarter, quarter)
        pltpu.make_async_copy(in_hbm.at[part], leaf_in.at[part], load_sem.at[1]).start()
    load_rhs.start()
    load_rank.start()

    tx, ty = lax.axis_index("tx"), lax.axis_index("ty")
    z, core = tx // N_CORE, tx % N_CORE
    x, y = ty // N_Y, ty % N_Y

    def at(z, core, x, y):
        return (z * N_CORE + core, x * N_Y + y)

    both = jnp.logical_and
    on_line = ty == 0
    on_top = both(on_line, core == 0)
    is_p1 = y % 2 == 1
    is_p2 = y == 2
    is_p3 = both(y == 0, x % 2 == 1)
    is_p4 = both(y == 0, x == 2)
    is_gate = both(on_line, core == 1)
    is_p6 = both(on_top, z % 2 == 1)
    is_p7 = both(on_top, z % 4 == 2)
    is_p8 = both(on_top, z % 8 == 4)
    is_p9 = both(on_top, z == 8)
    is_even = y % 2 == 0
    is_head = both(y == 0, x % 2 == 0)
    is_hub = both(is_gate, z % 4 == 2)
    is_late_hub = both(is_hub, z > 2)
    is_far_hub = both(is_hub, z >= 8)
    is_left_center = both(is_gate, z == 4)
    is_right_center = both(is_gate, z == 12)
    is_left_p8 = both(on_top, z == 4)
    is_right_p8 = both(on_top, z == 12)

    x_odd = x // 2 * 2 + 1
    z_odd, z_seven, z_eight = z // 2 * 2 + 1, z // 4 * 4 + 2, z // 8 * 8 + 4
    leaf_peer = at(z, core, x, y + 1)
    left_leaf = at(z, core, x, y - 1)
    column = [at(z, core, x, k) for k in range(N_Y)]
    my_p3 = at(z, core, x_odd, 0)
    p3s = [at(z, core, 1, 0), at(z, core, 3, 0)]
    p4 = at(z, core, 2, 0)
    gate = at(z, 1, 0, 0)
    p3s_of_gate = [at(z, c, k, 0) for c in range(N_CORE) for k in (1, 3)]
    p4s_of_gate = [at(z, c, 2, 0) for c in range(N_CORE)]
    p6, p7, p8 = at(z_odd, 0, 0, 0), at(z_seven, 0, 0, 0), at(z_eight, 0, 0, 0)
    gates_of_p6 = [at(z_odd - 1, 1, 0, 0), at(z_odd, 1, 0, 0)]
    gates_of_p7 = [at(z_seven - 2 + k, 1, 0, 0) for k in range(4)]
    hub, center = at(z_seven, 1, 0, 0), at(z_eight, 1, 0, 0)
    hubs_of_center = [at(z_eight - 2, 1, 0, 0), at(z_eight + 2, 1, 0, 0)]
    first_gates = [at(k, 1, 0, 0) for k in range(6)]
    second_hub, third_hub, fourth_hub = at(6, 1, 0, 0), at(10, 1, 0, 0), at(14, 1, 0, 0)

    barrier = pltpu.get_barrier_semaphore()

    def greet(condition, devices):
        @pl.when(condition)
        def _():
            for device in devices:
                pl.semaphore_signal(barrier, inc=1, device_id=device, device_id_type=MESH)

    def collector(z, core, x):
        return at(z, core, x, 1)

    x_even = x % 2 == 0
    next_p3 = collector(z, core, x_odd)
    greet(is_p1, [left_leaf])
    greet(y == 1, [column[3]])
    greet(y == 3, [collector(z, core, x)])
    greet(is_p2, [column[1], column[3]])
    greet(both(is_p2, x % 2 == 1), [column[1]])
    greet(on_top, [collector(z, 1, 0)])
    greet(y == 0, [column[1], column[3]])
    greet(both(y == 0, x_even), [next_p3])
    greet(is_p3, [at(z, core, x - 1, 3), collector(z, core, 2), collector(z, 1, 0)])
    greet(is_p4, [collector(z, core, 1), collector(z, core, 3), collector(z, 1, 0)])
    greet(is_gate, [collector(z, 0, 1), collector(z, 0, 3), collector(z, 1, 2)] + [collector(z_odd, 0, 0), collector(z_seven, 0, 0)])
    greet(both(is_gate, z % 4 == 0), [collector(z + 1, 1, 0)])
    greet(both(is_gate, both(z < 6, z != 4)), [collector(4, 0, 0), collector(8, 0, 0), collector(4, 1, 0)])
    greet(both(both(is_gate, z > 6), z % 4 != 2), [collector(z_seven, 1, 0)])
    greet(is_hub, [collector(z_seven - 2 + k, 1, 0) for k in (0, 1, 3)])
    greet(is_late_hub, [collector(z_eight, 0, 0), collector(z_eight, 1, 0)])
    greet(both(is_late_hub, z < 12), [collector(8, 0, 0)])
    greet(both(is_late_hub, z > 12), [collector(8, 1, 0)])
    greet(is_p9, [collector(8, 1, 0)])
    greet(
        both(is_gate, z % 8 == 4),
        [collector(z_eight - 2, 1, 0), collector(z_eight + 2, 1, 0), collector(z, 0, 0)],
    )
    greet(is_left_center, [collector(8, 0, 0)])
    greet(is_p6, [collector(z_odd - 1, 1, 0), collector(z_odd, 1, 0)])
    greet(is_p7, [collector(z, 1, 0)])
    greet(is_right_p8, [collector(z, 1, 0)])
    sizes = (
        (is_even, 1),
        (y == 3, 3),
        (both(y == 3, x_even), 1),
        (y == 1, 2),
        (both(y == 1, x_even), 1),
        (both(y == 1, x % 2 == 1), 4),
        (both(both(y == 1, x % 2 == 1), core == 0), 1),
        (both(y == 1, x == 2), 2 + core),
        (both(ty == 1, core == 1), 8),
        (both(both(ty == 1, core == 1), z % 4 != 2), 1),
        (both(both(ty == 1, core == 1), z % 4 == 1), 1),
        (both(both(ty == 1, core == 1), z % 4 == 2), 2),
        (both(both(ty == 1, core == 1), z == 6), 1),
        (both(both(ty == 1, core == 1), both(z % 4 == 2, z > 6)), 3),
        (both(both(ty == 1, core == 1), z == 4), 6),
        (both(both(ty == 1, core == 1), z == 12), 3),
        (both(both(ty == 1, core == 1), z == 8), 2),
        (both(both(ty == 1, core == 0), z % 2 == 1), 2),
        (both(both(ty == 1, core == 0), z % 4 == 2), 4),
        (both(both(ty == 1, core == 0), z == 4), 7),
        (both(both(ty == 1, core == 0), z == 12), 3),
        (both(both(ty == 1, core == 0), z == 8), 8),
    )
    greeted = sum(condition.astype(jnp.int32) * size for condition, size in sizes)
    for load in loads[3:]:
        load.start()

    def remote(source, target, send, recv, device):
        return pltpu.make_async_remote_copy(
            src_ref=source,
            dst_ref=target,
            send_sem=send_sem.at[send],
            recv_sem=recv_sem.at[recv],
            device_id=device,
            device_id_type=MESH,
        )

    left_part, right_part = pl.ds(0, width), pl.ds(width, width)
    narrow = pl.ds(0, leaf_width)

    leaf_up = remote(leaf_coef, child.at[:, narrow], 0, 0, leaf_peer)
    side = jnp.where(
        is_p1,
        y // 2,
        jnp.where(is_p2, x % 2, jnp.where(is_p3, x // 2, jnp.where(is_p4, core, z % 2))),
    )
    steps = ((is_p1, column[2]), (is_p2, my_p3), (is_p3, p4), (is_p4, gate), (is_gate, p6))
    parent = tuple(sum(condition.astype(jnp.int32) * device[k] for condition, device in steps) for k in range(2))
    up_left = remote(coef, child.at[:, left_part], 1, 0, parent)
    up_right = remote(coef, child.at[:, right_part], 1, 1, parent)
    send_cross1 = [remote(cross_sum.at[0, :, narrow], leaf_cross1, 2, 2, left_leaf)]
    send_down1 = [remote(down.at[0, 0, :, narrow], leaf_map1, 3, 3, left_leaf)]
    sides2 = ((0, 0), (1, 0), (3, 1))
    send_cross2 = [remote(cross_sum.at[s], leaf_cross2, 2 + n, 4, column[k]) for n, (k, s) in enumerate(sides2)]
    send_down2 = [remote(down.at[s, 0], leaf_map2, 5 + n, 5, column[k]) for n, (k, s) in enumerate(sides2)]
    send_cross4 = [remote(cross_sum.at[s], cross_a, 2 + s, 11, p3s[s]) for s in range(2)]
    send_up4 = [remote(up.at[s, 0], map_a, 7 + s, 7, p3s[s]) for s in range(2)]
    send_part4 = [remote(path_coef, parts4.at[k], 9, (19, 0)[k], gate) for k in range(2)]
    send_down4 = [remote(down.at[s, 0], map_d, 5 + s, 10, p3s[s]) for s in range(2)]
    send_cross6 = [remote(cross_sum.at[s], cross_b, 2 + s, 12, gates_of_p6[s]) for s in range(2)]
    send_up6 = [remote(up.at[s, 0], map_a, 4 + s, 7, gates_of_p6[s]) for s in range(2)]
    send_down6 = [remote(down.at[s, 0], map_c, 6 + s, 9, gates_of_p6[s]) for s in range(2)]
    halves = [pl.ds(k * (width // 2), width // 2) for k in range(2)]
    send_down6_half = [remote(down.at[0, 0, half], map_c.at[half], (6, 8)[k], 9, gates_of_p6[0]) for k, half in enumerate(halves)]
    send_cross7 = [remote(cross_sum.at[k // 2], cross_a, 2 + k, 11, gates_of_p7[k]) for k in range(4)]
    send_down7 = [remote(down.at[k // 2, 0], map_d, 6 + k, 10, gates_of_p7[k]) for k in range(4)]
    pass_down7 = remote(map_d, map_d, 3, 10, at(z - 1, 1, 0, 0))
    send_cross8 = [remote(top_sum.at[s], cross_c, 7 + s, 18, hubs_of_center[s]) for s in range(2)]
    send_cross8_first = [remote(top_sum.at[0], cross_c, 9 + k, 18, first_gates[k]) for k in range(4)]
    send_cross8_first += [remote(top_sum.at[1], cross_c, 13, 18, first_gates[5])]
    send_top_up7 = remote(up, top_up, 6, 20, hub)
    send_top_up8 = remote(up, top_up, 4, 20, center)
    send_top_cross = remote(cross, top_cross, 8, 14, center)
    send_up8 = [remote(up.at[s, 0], map_e, 4 + s, 21, hubs_of_center[s]) for s in range(2)]
    send_down8 = [remote(down.at[s, 0], map_b, 6 + s, 8, hubs_of_center[s]) for s in range(2)]
    send_down8_first = [remote(down.at[k // 4, 0], map_b, 8 + k, 8, first_gates[k]) for k in range(6)]
    pass_down8 = remote(map_b, map_b, 4, 8, at(z - 1, 1, 0, 0))
    send_cross9 = [remote(cross.at[0, 0], map_f, 2, 22, third_hub), remote(cross.at[0, 0], map_f, 3, 22, fourth_hub)]
    send_cross9 += [remote(cross.at[1, 0], map_f, 4, 22, at(4, 1, 0, 0))]
    send_part6 = [remote(path_coef, parts6.at[k], 2, (14, 15, 16, 16)[k], hub) for k in range(4)]
    send_child7 = remote(top_child, child, 3, 0, p7)
    send_coef7 = [remote(top_coef, top_child.at[:, part], 4, 15 + k, center) for k, part in enumerate((left_part, right_part))]
    send_part8 = [
        [remote(far_out, parts8.at[k], 5 + n, (17, 13)[k], device) for n, device in enumerate((*first_gates, second_hub))]
        for k in range(2)
    ]
    send_part8_right = [remote(far_out, parts8.at[0], 5 + k, 17, (third_hub, fourth_hub)[k]) for k in range(2)]
    send_above7 = [remote(top_out, above, n, 13, gates_of_p7[k]) for n, k in enumerate((3, 0, 1))]
    others = [at(z, 0, 2, 0), p3s_of_gate[0], p3s_of_gate[1], at(z, 0, 0, 0), at(z, 1, 2, 0), p3s_of_gate[2], p3s_of_gate[3]]
    send_above4 = [remote(outgoing.at[n // 4], above, 3 + n, 13, device) for n, device in enumerate(others)]
    head = at(z, core, x - 1, 0)
    send_head_map = remote(head_map, head_map, 0, 23, head)
    send_head_base = remote(cross_sum.at[0], head_base, 1, 24, head)
    send_above2 = [remote(head_out, leaf_above, 9 + k, 6, column[k]) for k in (3, 2, 1)]
    send_above2_right = [remote(outgoing.at[1], leaf_above, 1 + k, 6, column[k]) for k in (1, 3, 2)]

    def start(copies):
        for copy in copies:
            copy.start()

    def dot(a, b):
        return jnp.dot(a, b, preferred_element_type=F32)

    load_rhs.wait()
    load_in.wait()
    load_rank.wait()
    leaf_rank, node_rank = rank[0, 0], rank[0, 1]
    leaf_keep = lax.broadcasted_iota(jnp.int32, (rows, leaf_width), 1) < leaf_rank
    node_keep = lax.broadcasted_iota(jnp.int32, (rows, width), 1) < node_rank
    leaf_coef[...] = jnp.where(leaf_keep, dot(rhs[...], leaf_in[...]), 0.0).astype(BF16)

    pl.semaphore_wait(barrier, greeted)

    @pl.when(is_p1)
    def _():
        pl.semaphore_signal(go_sem, inc=1, device_id=left_leaf, device_id_type=MESH)

    @pl.when(both(both(ty == 1, core == 1), z == 8))
    def _():
        pl.semaphore_signal(late_sem, inc=1, device_id=at(8, 0, 0, 0), device_id_type=MESH)

    def mask_up():
        keep = lax.broadcasted_iota(jnp.int32, (width, width), 1) < node_rank
        for s in range(2):
            up[s, 0] = jnp.where(keep, up[s, 0], jnp.zeros((width, width), BF16))

    def mask_down():
        keep = lax.broadcasted_iota(jnp.int32, (width, width), 0) < node_rank
        for s in range(2):
            down[s, 0] = jnp.where(keep, down[s, 0], jnp.zeros((width, width), BF16))

    def send_up(summed, waits=False):
        coef[...] = jnp.where(node_keep, summed, 0.0).astype(BF16)
        if waits:
            pl.semaphore_wait(go_sem, 1)

        @pl.when(side == 0)
        def _():
            up_left.start()

        @pl.when(side == 1)
        def _():
            up_right.start()

    def cross_terms():
        cross_sum[0] = dot(child[:, right_part], cross[0, 0])
        cross_sum[1] = dot(child[:, left_part], cross[1, 0])

    @pl.when(is_even)
    def _():
        leaf_up.start()

    @pl.when(on_line)
    def _():
        pl.semaphore_wait(go_sem, 1)

    @pl.when(is_p1)
    def _():
        load_up.wait()
        summed = dot(leaf_coef[...], up[1, 0, narrow, :])
        leaf_up.wait_recv()
        send_up(summed + dot(child[:, narrow], up[0, 0, narrow, :]))
        load_cross.wait()
        cross_sum[0, :, narrow] = dot(leaf_coef[...], cross[0, 0, narrow, narrow])
        leaf_cross1[...] = dot(child[:, narrow], cross[1, 0, narrow, narrow])
        start(send_cross1)
        load_down.wait()
        mask_down()
        start(send_down1)
        leaf_map1[...] = down[1, 0, :, narrow]

    def lift(waits=True):
        up_left.wait_recv()
        summed = dot(child[:, left_part], up[0, 0])
        up_right.wait_recv()
        send_up(summed + dot(child[:, right_part], up[1, 0]), waits)

    @pl.when(is_p2)
    def _():
        load_up.wait()
        lift()
        load_cross.wait()
        cross_terms()
        start(send_cross2)
        leaf_cross2[...] = cross_sum[1]
        load_down.wait()
        mask_down()
        start(send_down2)
        leaf_map2[...] = down[1, 0]

    @pl.when(is_p3)
    def _():
        load_up.wait()
        lift()

        @pl.when(core == 0)
        def _():
            send_up4[0].wait_recv()
            path_coef[...] = dot(coef[...], map_a[...]).astype(BF16)
            for k in range(2):

                @pl.when(x // 2 == k)
                def _():
                    send_part4[k].start()

        load_cross.wait()
        cross_terms()
        load_down.wait()
        mask_down()

    @pl.when(is_p4)
    def _():
        load_up.wait()
        mask_up()
        pl.semaphore_wait(go_sem, 1)

        @pl.when(core == 0)
        def _():
            start(send_up4)
            load_down.wait()
            mask_down()
            start(send_down4)
            up_left.wait_recv()
            up_right.wait_recv()

        @pl.when(core == 1)
        def _():
            lift(waits=False)

        load_cross.wait()
        cross_terms()
        start(send_cross4)

        @pl.when(core == 1)
        def _():
            load_down.wait()
            mask_down()
            start(send_down4)

    @pl.when(is_gate)
    def _():
        load_up.wait()
        load_cross.wait()
        load_down.wait()
        mask_down()

        @pl.when(z % 4 == 1)
        def _():
            send_down7[0].wait_recv()
            pass_down7.start()

        map_keep = lax.broadcasted_iota(jnp.int32, (width, width), 1) < node_rank
        send_up6[0].wait_recv()
        for s in range(2):
            ahead = dot(jnp.where(map_keep, up[s, 0], jnp.zeros((width, width), BF16)), map_a[...])
            gate_maps[s] = ahead.astype(BF16)
        for copy in send_part4:
            copy.wait_recv()
        child[:, left_part] = (parts4[0].astype(F32) + parts4[1].astype(F32)).astype(BF16)
        up_right.wait_recv()
        six = dot(child[:, left_part], gate_maps[0]) + dot(child[:, right_part], gate_maps[1])
        path_coef[...] = six.astype(BF16)
        for k in (0, 1, 3):

            @pl.when(z % 4 == k)
            def _():
                send_part6[k].start()

        send_up(dot(child[:, left_part], up[0, 0]) + dot(child[:, right_part], up[1, 0]))

        @pl.when(is_hub)
        def _():
            parts6[2] = path_coef[...]
            send_top_up7.wait_recv()

            @pl.when(is_far_hub)
            def _():
                send_up8[0].wait_recv()
                send_cross9[0].wait_recv()
                map_e[...] = dot(map_e[...], map_f[...]).astype(BF16)

            for k in (0, 1, 3):
                send_part6[k].wait_recv()
            for k, part in enumerate((left_part, right_part)):
                six = parts6[2 * k].astype(F32) + parts6[2 * k + 1].astype(F32)
                top_child[:, part] = six.astype(BF16)
            seven = dot(top_child[:, left_part], top_up[0, 0]) + dot(top_child[:, right_part], top_up[1, 0])
            top_coef[...] = seven.astype(BF16)
            for k in range(2):

                @pl.when(z // 4 % 2 == k)
                def _():
                    send_coef7[k].start()

            @pl.when(is_far_hub)
            def _():
                far_out[...] = dot(top_coef[...], map_e[...]).astype(BF16)
                for k in range(2):

                    @pl.when(z == 10 + 4 * k)
                    def _():
                        start(send_part8[k])

            send_child7.start()

        def center_cross_terms():
            send_top_cross.wait_recv()
            top_sum[0] = dot(top_child[:, right_part], top_cross[0, 0]).astype(BF16)
            top_sum[1] = dot(top_child[:, left_part], top_cross[1, 0]).astype(BF16)

        @pl.when(is_left_center)
        def _():
            send_top_up8.wait_recv()
            send_coef7[0].wait_recv()
            send_coef7[1].wait_recv()
            center_cross_terms()
            start(send_cross8_first)
            send_cross8[1].start()
            cross_c[...] = top_sum[1]
            eight = dot(top_child[:, left_part], top_up[0, 0]) + dot(top_child[:, right_part], top_up[1, 0])
            top_coef[...] = eight.astype(BF16)
            send_cross9[2].wait_recv()
            far_out[...] = dot(top_coef[...], map_f[...]).astype(BF16)
            start(send_part8_right)

        @pl.when(is_right_center)
        def _():
            pl.semaphore_signal(late_sem, inc=1, device_id=p8, device_id_type=MESH)
            send_coef7[1].wait_recv()
            send_coef7[0].wait_recv()
            center_cross_terms()
            start(send_cross8)

        cross_terms()

        @pl.when(z == 1)
        def _():
            send_down8_first[0].wait_recv()
            pass_down8.start()

    @pl.when(is_p6)
    def _():
        load_up.wait()
        mask_up()
        start(send_up6)
        load_cross.wait()
        load_down.wait()
        mask_down()
        for copy in send_up6:
            copy.wait_send()
        send_down6[1].start()

        @pl.when(z % 4 == 1)
        def _():
            send_down6[0].start()

        @pl.when(both(z % 4 == 3, z != 7))
        def _():
            send_down6_half[0].start()

        up_right.wait_recv()

        @pl.when(both(z % 4 == 3, z != 7))
        def _():
            send_down6_half[1].start()

        @pl.when(z == 7)
        def _():
            send_down6[0].start()

        up_left.wait_recv()
        cross_terms()
        start(send_cross6)

    @pl.when(is_p7)
    def _():
        load_up.wait()
        mask_up()
        send_top_up7.start()
        load_down.wait()
        mask_down()
        start(send_down7[1:])
        load_cross.wait()
        send_child7.wait_recv()
        cross_terms()
        start(send_cross7)

    @pl.when(is_p8)
    def _():
        load_up.wait()
        mask_up()
        load_cross.wait()
        send_top_cross.start()
        load_down.wait()
        mask_down()

        @pl.when(is_left_p8)
        def _():
            send_down8[1].start()
            start(send_down8_first[4:])

        @pl.when(is_right_p8)
        def _():
            send_up8[1].start()

        send_cross1[0].wait_recv()

        @pl.when(is_right_p8)
        def _():
            send_down1[0].wait_recv()
            send_up8[0].start()
            pl.semaphore_wait(late_sem, 1)
            start(send_down8)

        @pl.when(is_left_p8)
        def _():
            send_top_up8.start()
            send_down8_first[1].start()
            send_down1[0].wait_recv()
            for k, after in ((1, 3), (3, 2)):
                send_down8_first[k].wait_send()
                send_down8_first[after].start()

    @pl.when(both(on_top, z % 8 == 0))
    def _():
        load_up.wait()
        load_cross.wait()
        load_down.wait()

    @pl.when(is_p9)
    def _():
        send_cross9[0].start()
        pl.semaphore_wait(late_sem, 1)
        send_cross9[1].start()
        send_cross9[2].start()

    load_diag.wait()
    product[...] = dot(rhs[...], diag[...])
    load_out.wait()

    def sent(condition, copies):
        @pl.when(condition)
        def _():
            for copy in copies:
                copy.wait_send()

    sent(is_even, [leaf_up])
    sent(is_p1, [up_left, *send_cross1, *send_down1])
    sent(is_p2, [up_left, *send_cross2, *send_down2])
    sent(both(is_p3, core == 0), [send_part4[0]])
    sent(is_p3, [up_left])
    sent(both(is_p4, core == 0), send_up4)
    sent(both(is_p4, core == 1), [up_left])
    sent(is_p4, [*send_cross4, *send_down4])
    sent(is_gate, [up_left])
    sent(both(is_gate, z % 4 != 2), [send_part6[0]])
    sent(is_hub, [send_coef7[0], send_child7])
    sent(is_far_hub, send_part8[0])
    sent(is_left_center, [*send_cross8_first, send_cross8[1], *send_part8_right])
    sent(is_right_center, send_cross8)
    sent(is_p6, [send_down6[1], *send_cross6])
    sent(both(is_p6, both(z % 4 == 3, z != 7)), send_down6_half)
    sent(both(is_p6, jnp.logical_not(both(z % 4 == 3, z != 7))), [send_down6[0]])
    sent(is_p7, [send_top_up7, *send_down7[1:], *send_cross7])
    sent(is_p8, [send_top_cross, send_down8[1]])
    sent(is_left_p8, [send_top_up8, send_down8_first[2], *send_down8_first[4:]])
    sent(is_right_p8, [*send_up8, send_down8[0]])
    sent(is_p9, send_cross9)

    def lower_hub():
        send_down8[0].wait_recv()
        send_cross8[0].wait_recv()
        send_part8[0][0].wait_recv()

        @pl.when(z == 6)
        def _():
            send_part8[1][0].wait_recv()
            crossed = parts8[0].astype(F32) + parts8[1].astype(F32)
            parts8[0] = crossed.astype(BF16)

        top_out[...] = (cross_c[...].astype(F32) + dot(parts8[0], map_b[...])).astype(BF16)
        send_above7[0].start()

        @pl.when(z > 6)
        def _():
            start(send_above7[1:])

        above[...] = top_out[...]

    @pl.when(is_gate)
    def _():
        @pl.when(z == 10)
        def _():
            lower_hub()

        @pl.when(z % 4 != 1)
        def _():
            send_down7[0].wait_recv()

        @pl.when(z % 4 == 1)
        def _():
            pass_down7.wait_send()

        send_down6[0].wait_recv()
        map_d[...] = dot(map_d[...], map_c[...]).astype(BF16)
        for s in range(2):
            gate_maps[s] = dot(map_d[...], down[s, 0]).astype(BF16)

        @pl.when(both(z < 6, z != 1))
        def _():
            send_down8_first[0].wait_recv()

        @pl.when(z == 1)
        def _():
            pass_down8.wait_send()

        @pl.when(z < 6)
        def _():
            for s in range(2):
                top_up[s, 0] = dot(map_b[...], gate_maps[s]).astype(BF16)

        send_cross7[0].wait_recv()
        send_cross6[0].wait_recv()
        five = (cross_b[...] + dot(cross_a[...].astype(BF16), map_c[...])).astype(BF16)
        for s in range(2):
            cross_sum[s] += dot(five, down[s, 0])

        @pl.when(z < 6)
        def _():
            @pl.when(z != 4)
            def _():
                send_cross8_first[0].wait_recv()

            for k in range(2):
                send_part8[k][0].wait_recv()
            above[...] = (parts8[0].astype(F32) + parts8[1].astype(F32)).astype(BF16)
            for s in range(2):
                four = cross_sum[s] + dot(cross_c[...], gate_maps[s]) + dot(above[...], top_up[s, 0])
                outgoing[s] = four.astype(BF16)
                start(send_above4[4 * s : 4 * s + 4])

        @pl.when(both(is_late_hub, z != 10))
        def _():
            lower_hub()

        @pl.when(both(z > 6, z % 4 != 2))
        def _():
            send_above7[0].wait_recv()

        @pl.when(z >= 6)
        def _():
            for s in range(2):
                outgoing[s] = (cross_sum[s] + dot(above[...], gate_maps[s])).astype(BF16)
                start(send_above4[4 * s : 4 * s + 4])

    @pl.when(is_p3)
    def _():
        send_down4[0].wait_recv()
        head_map[...] = dot(map_d[...], down[0, 0]).astype(BF16)
        send_head_map.start()
        send_cross4[0].wait_recv()
        cross_four = cross_a[...].astype(BF16)
        cross_sum[0] += dot(cross_four, down[0, 0])
        send_head_base.start()
        cross_sum[1] += dot(cross_four, down[1, 0])
        down[1, 0] = dot(map_d[...], down[1, 0]).astype(BF16)
        send_above4[0].wait_recv()
        outgoing[1] = (cross_sum[1] + dot(above[...], down[1, 0])).astype(BF16)
        start(send_above2_right)
        leaf_above[...] = outgoing[1]

    @pl.when(is_head)
    def _():
        send_head_map.wait_recv()
        send_head_base.wait_recv()

        @pl.when(is_gate)
        def _():
            head_out[...] = (head_base[...] + dot(outgoing[1], head_map[...])).astype(BF16)

        @pl.when(jnp.logical_not(is_gate))
        def _():
            send_above4[0].wait_recv()
            head_out[...] = (head_base[...] + dot(above[...], head_map[...])).astype(BF16)

        start(send_above2)
        leaf_above[...] = head_out[...]

    @pl.when(both(is_even, jnp.logical_not(is_p8)))
    def _():
        send_cross1[0].wait_recv()
        send_down1[0].wait_recv()

    @pl.when(jnp.logical_not(is_p2))
    def _():
        send_cross2[0].wait_recv()
        send_down2[0].wait_recv()

    zero = dot(leaf_cross2[...].astype(BF16), leaf_map1[...]) + leaf_cross1[...]
    zero = jnp.where(leaf_keep, zero, 0.0).astype(BF16)
    product[...] += dot(zero, leaf_out[...])
    map_keep = lax.broadcasted_iota(jnp.int32, (width, leaf_width), 1) < leaf_rank
    leaf_map1[...] = jnp.where(map_keep, dot(leaf_map2[...], leaf_map1[...]), 0.0).astype(BF16)
    leaf_map2[...] = dot(leaf_map1[...], leaf_out[...]).astype(BF16)

    @pl.when(y > 0)
    def _():
        send_above2[0].wait_recv()

    product[...] += dot(leaf_above[...], leaf_map2[...])

    sent(is_head, send_above2)
    sent(is_p3, [send_head_map, send_head_base, *send_above2_right])
    sent(is_gate, send_above4)
    sent(is_late_hub, send_above7[:1])
    sent(is_far_hub, send_above7[1:])


def on_device(rhs, diag_blocks, leaf_in, leaf_out, up_maps, cross_maps, down_maps, node_rank):
    rows, leaf = rhs.shape
    width, leaf_width = up_maps.shape[-1], leaf_in.shape[1]
    operands = (rhs, diag_blocks, leaf_in, leaf_out, up_maps, cross_maps, down_maps)

    def vector(*lead, kind=BF16, columns=width):
        return pltpu.VMEM((*lead, rows, columns), kind)

    full_map = pltpu.VMEM((width, width), BF16)
    return pl.pallas_call(
        kernel,
        out_shape=pltpu.VMEM((rows, leaf), F32),
        in_specs=[pl.BlockSpec(memory_space=pl.ANY)] * 8,
        out_specs=pl.BlockSpec(memory_space=pltpu.VMEM),
        scratch_shapes=[pltpu.VMEM(each.shape, each.dtype) for each in operands]
        + [
            pltpu.SMEM(node_rank.shape, node_rank.dtype),
            vector(columns=leaf_width),
            vector(),
            vector(columns=2 * width),
            vector(2, kind=F32),
            vector(),
            vector(2),
            full_map,
            full_map,
            full_map,
            full_map,
            full_map,
            full_map,
            pltpu.VMEM(up_maps.shape, BF16),
            pltpu.VMEM(cross_maps.shape, BF16),
            vector(columns=2 * width),
            vector(),
            vector(2),
            vector(),
            vector(),
            pltpu.VMEM((2, width, width), BF16),
            full_map,
            vector(kind=F32),
            vector(),
            full_map,
            pltpu.VMEM((width, leaf_width), BF16),
            vector(kind=F32),
            vector(kind=F32),
            vector(),
            vector(kind=F32),
            vector(kind=F32, columns=leaf_width),
            vector(),
            vector(),
            vector(2),
            vector(4),
            vector(2),
            pltpu.SemaphoreType.DMA((8,)),
            pltpu.SemaphoreType.DMA((14,)),
            pltpu.SemaphoreType.DMA((25,)),
            pltpu.SemaphoreType.REGULAR,
            pltpu.SemaphoreType.REGULAR,
        ],
        compiler_params=pltpu.CompilerParams(
            collective_id=0, has_side_effects=True, vmem_limit_bytes=60 * 2**20
        ),
    )(*operands, node_rank)


def solution(mesh):
    assert mesh.shape["tx"] == N_Z * N_CORE and mesh.shape["ty"] == N_X * N_Y
    in_specs = (
        P(None, ("tx", "ty")),
        P(("tx", "ty"), None),
        P(("tx", "ty"), None),
        P(("tx", "ty"), None),
        P(None, ("tx", "ty"), None, None),
        P(None, ("tx", "ty"), None, None),
        P(None, ("tx", "ty"), None, None),
        P(("tx", "ty"), None),
    )
    return jax.shard_map(
        on_device, mesh=mesh, in_specs=in_specs, out_specs=P(None, ("tx", "ty")), check_vma=False
    )
```

```python
import functools

import jax
import jax.numpy as jnp
from jax import lax
from jax.experimental import pallas as pl
from jax.experimental.pallas import tpu as pltpu
from jax.sharding import PartitionSpec as P

MESH = pl.DeviceIdType.MESH
F32 = jnp.float32
BF16 = jnp.bfloat16
N_Z, N_CORE, N_X, N_Y = 16, 2, 4, 4


def kernel(
    rhs_hbm,
    diag_hbm,
    in_hbm,
    out_hbm,
    up_hbm,
    cross_hbm,
    down_hbm,
    rank_hbm,
    product,
    rhs,
    diag,
    leaf_in,
    leaf_out,
    up,
    cross,
    down,
    rank,
    leaf_coef,
    coef,
    child,
    cross_sum,
    path_coef,
    outgoing,
    map_a,
    map_b,
    map_c,
    map_d,
    map_e,
    map_f,
    top_up,
    top_cross,
    top_child,
    top_coef,
    top_sum,
    top_out,
    far_out,
    gate_maps,
    head_map,
    head_base,
    head_out,
    leaf_map2,
    leaf_map1,
    cross_a,
    cross_b,
    cross_c,
    leaf_cross2,
    leaf_cross1,
    above,
    leaf_above,
    parts4,
    parts6,
    parts8,
    load_sem,
    send_sem,
    recv_sem,
    go_sem,
    late_sem,
):
    rows, width = coef.shape
    leaf_width = leaf_coef.shape[1]
    loads = [
        pltpu.make_async_copy(source, target, load_sem.at[n])
        for n, (source, target) in enumerate(
            (
                (rhs_hbm, rhs),
                (in_hbm, leaf_in),
                (rank_hbm, rank),
                (up_hbm, up),
                (cross_hbm, cross),
                (down_hbm, down),
                (diag_hbm, diag),
                (out_hbm, leaf_out),
            )
        )
    ]
    load_rhs, load_in, load_rank, load_up, load_cross, load_down, load_diag, load_out = loads
    quarter = in_hbm.shape[0] // 4
    for n in range(4):
        part = pl.ds(n * quarter, quarter)
        pltpu.make_async_copy(in_hbm.at[part], leaf_in.at[part], load_sem.at[1]).start()
    load_rhs.start()
    load_rank.start()

    tx, ty = lax.axis_index("tx"), lax.axis_index("ty")
    z, core = tx // N_CORE, tx % N_CORE
    x, y = ty // N_Y, ty % N_Y

    def at(z, core, x, y):
        return (z * N_CORE + core, x * N_Y + y)

    both = jnp.logical_and
    on_line = ty == 0
    on_top = both(on_line, core == 0)
    is_p1 = y % 2 == 1
    is_p2 = y == 2
    is_p3 = both(y == 0, x % 2 == 1)
    is_p4 = both(y == 0, x == 2)
    is_gate = both(on_line, core == 1)
    is_p6 = both(on_top, z % 2 == 1)
    is_p7 = both(on_top, z % 4 == 2)
    is_p8 = both(on_top, z % 8 == 4)
    is_p9 = both(on_top, z == 8)
    is_even = y % 2 == 0
    is_head = both(y == 0, x % 2 == 0)
    is_hub = both(is_gate, z % 4 == 2)
    is_late_hub = both(is_hub, z > 2)
    is_far_hub = both(is_hub, z >= 8)
    is_left_center = both(is_gate, z == 4)
    is_right_center = both(is_gate, z == 12)
    is_left_p8 = both(on_top, z == 4)
    is_right_p8 = both(on_top, z == 12)

    x_odd = x // 2 * 2 + 1
    z_odd, z_seven, z_eight = z // 2 * 2 + 1, z // 4 * 4 + 2, z // 8 * 8 + 4
    leaf_peer = at(z, core, x, y + 1)
    left_leaf = at(z, core, x, y - 1)
    column = [at(z, core, x, k) for k in range(N_Y)]
    my_p3 = at(z, core, x_odd, 0)
    p3s = [at(z, core, 1, 0), at(z, core, 3, 0)]
    p4 = at(z, core, 2, 0)
    gate = at(z, 1, 0, 0)
    p3s_of_gate = [at(z, c, k, 0) for c in range(N_CORE) for k in (1, 3)]
    p4s_of_gate = [at(z, c, 2, 0) for c in range(N_CORE)]
    p6, p7, p8 = at(z_odd, 0, 0, 0), at(z_seven, 0, 0, 0), at(z_eight, 0, 0, 0)
    gates_of_p6 = [at(z_odd - 1, 1, 0, 0), at(z_odd, 1, 0, 0)]
    gates_of_p7 = [at(z_seven - 2 + k, 1, 0, 0) for k in range(4)]
    hub, center = at(z_seven, 1, 0, 0), at(z_eight, 1, 0, 0)
    hubs_of_center = [at(z_eight - 2, 1, 0, 0), at(z_eight + 2, 1, 0, 0)]
    first_gates = [at(k, 1, 0, 0) for k in range(6)]
    second_hub, third_hub, fourth_hub = at(6, 1, 0, 0), at(10, 1, 0, 0), at(14, 1, 0, 0)

    barrier = pltpu.get_barrier_semaphore()

    def greet(condition, devices):
        @pl.when(condition)
        def _():
            for device in devices:
                pl.semaphore_signal(barrier, inc=1, device_id=device, device_id_type=MESH)

    def collector(z, core, x):
        return at(z, core, x, 1)

    x_even = x % 2 == 0
    next_p3 = collector(z, core, x_odd)
    greet(is_p1, [left_leaf])
    greet(y == 1, [column[3]])
    greet(y == 3, [collector(z, core, x)])
    greet(is_p2, [column[1], column[3]])
    greet(both(is_p2, x % 2 == 1), [column[1]])
    greet(on_top, [collector(z, 1, 0)])
    greet(y == 0, [column[1], column[3]])
    greet(both(y == 0, x_even), [next_p3])
    greet(is_p3, [at(z, core, x - 1, 3), collector(z, core, 2), collector(z, 1, 0)])
    greet(is_p4, [collector(z, core, 1), collector(z, core, 3), collector(z, 1, 0)])
    greet(is_gate, [collector(z, 0, 1), collector(z, 0, 3), collector(z, 1, 2)] + [collector(z_odd, 0, 0), collector(z_seven, 0, 0)])
    greet(both(is_gate, z % 4 == 0), [collector(z + 1, 1, 0)])
    greet(both(is_gate, both(z < 6, z != 4)), [collector(4, 0, 0), collector(8, 0, 0), collector(4, 1, 0)])
    greet(both(both(is_gate, z > 6), z % 4 != 2), [collector(z_seven, 1, 0)])
    greet(is_hub, [collector(z_seven - 2 + k, 1, 0) for k in (0, 1, 3)])
    greet(is_late_hub, [collector(z_eight, 0, 0), collector(z_eight, 1, 0)])
    greet(both(is_late_hub, z < 12), [collector(8, 0, 0)])
    greet(both(is_late_hub, z > 12), [collector(8, 1, 0)])
    greet(is_p9, [collector(8, 1, 0)])
    greet(
        both(is_gate, z % 8 == 4),
        [collector(z_eight - 2, 1, 0), collector(z_eight + 2, 1, 0), collector(z, 0, 0)],
    )
    greet(is_left_center, [collector(8, 0, 0)])
    greet(is_p6, [collector(z_odd - 1, 1, 0), collector(z_odd, 1, 0)])
    greet(is_p7, [collector(z, 1, 0)])
    greet(is_right_p8, [collector(z, 1, 0)])
    sizes = (
        (is_even, 1),
        (y == 3, 3),
        (both(y == 3, x_even), 1),
        (y == 1, 2),
        (both(y == 1, x_even), 1),
        (both(y == 1, x % 2 == 1), 4),
        (both(both(y == 1, x % 2 == 1), core == 0), 1),
        (both(y == 1, x == 2), 2 + core),
        (both(ty == 1, core == 1), 8),
        (both(both(ty == 1, core == 1), z % 4 != 2), 1),
        (both(both(ty == 1, core == 1), z % 4 == 1), 1),
        (both(both(ty == 1, core == 1), z % 4 == 2), 2),
        (both(both(ty == 1, core == 1), z == 6), 1),
        (both(both(ty == 1, core == 1), both(z % 4 == 2, z > 6)), 3),
        (both(both(ty == 1, core == 1), z == 4), 6),
        (both(both(ty == 1, core == 1), z == 12), 3),
        (both(both(ty == 1, core == 1), z == 8), 2),
        (both(both(ty == 1, core == 0), z % 2 == 1), 2),
        (both(both(ty == 1, core == 0), z % 4 == 2), 4),
        (both(both(ty == 1, core == 0), z == 4), 7),
        (both(both(ty == 1, core == 0), z == 12), 3),
        (both(both(ty == 1, core == 0), z == 8), 8),
    )
    greeted = sum(condition.astype(jnp.int32) * size for condition, size in sizes)
    for load in loads[3:]:
        load.start()

    def remote(source, target, send, recv, device):
        return pltpu.make_async_remote_copy(
            src_ref=source,
            dst_ref=target,
            send_sem=send_sem.at[send],
            recv_sem=recv_sem.at[recv],
            device_id=device,
            device_id_type=MESH,
        )

    left_part, right_part = pl.ds(0, width), pl.ds(width, width)
    narrow = pl.ds(0, leaf_width)

    leaf_up = remote(leaf_coef, child.at[:, narrow], 0, 0, leaf_peer)
    side = jnp.where(
        is_p1,
        y // 2,
        jnp.where(is_p2, x % 2, jnp.where(is_p3, x // 2, jnp.where(is_p4, core, z % 2))),
    )
    steps = ((is_p1, column[2]), (is_p2, my_p3), (is_p3, p4), (is_p4, gate), (is_gate, p6))
    parent = tuple(sum(condition.astype(jnp.int32) * device[k] for condition, device in steps) for k in range(2))
    up_left = remote(coef, child.at[:, left_part], 1, 0, parent)
    up_right = remote(coef, child.at[:, right_part], 1, 1, parent)
    send_cross1 = [remote(cross_sum.at[0, :, narrow], leaf_cross1, 2, 2, left_leaf)]
    send_down1 = [remote(down.at[0, 0, :, narrow], leaf_map1, 3, 3, left_leaf)]
    sides2 = ((0, 0), (1, 0), (3, 1))
    send_cross2 = [remote(cross_sum.at[s], leaf_cross2, 2 + n, 4, column[k]) for n, (k, s) in enumerate(sides2)]
    send_down2 = [remote(down.at[s, 0], leaf_map2, 5 + n, 5, column[k]) for n, (k, s) in enumerate(sides2)]
    send_cross4 = [remote(cross_sum.at[s], cross_a, 2 + s, 11, p3s[s]) for s in range(2)]
    send_up4 = [remote(up.at[s, 0], map_a, 7 + s, 7, p3s[s]) for s in range(2)]
    send_part4 = [remote(path_coef, parts4.at[k], 9, (19, 0)[k], gate) for k in range(2)]
    send_down4 = [remote(down.at[s, 0], map_d, 5 + s, 10, p3s[s]) for s in range(2)]
    send_cross6 = [remote(cross_sum.at[s], cross_b, 2 + s, 12, gates_of_p6[s]) for s in range(2)]
    send_up6 = [remote(up.at[s, 0], map_a, 4 + s, 7, gates_of_p6[s]) for s in range(2)]
    send_down6 = [remote(down.at[s, 0], map_c, 6 + s, 9, gates_of_p6[s]) for s in range(2)]
    halves = [pl.ds(k * (width // 2), width // 2) for k in range(2)]
    send_down6_half = [remote(down.at[0, 0, half], map_c.at[half], (6, 8)[k], 9, gates_of_p6[0]) for k, half in enumerate(halves)]
    send_cross7 = [remote(cross_sum.at[k // 2], cross_a, 2 + k, 11, gates_of_p7[k]) for k in range(4)]
    send_down7 = [remote(down.at[k // 2, 0], map_d, 6 + k, 10, gates_of_p7[k]) for k in range(4)]
    pass_down7 = remote(map_d, map_d, 3, 10, at(z - 1, 1, 0, 0))
    send_cross8 = [remote(top_sum.at[s], cross_c, 7 + s, 18, hubs_of_center[s]) for s in range(2)]
    send_cross8_first = [remote(top_sum.at[0], cross_c, 9 + k, 18, first_gates[k]) for k in range(4)]
    send_cross8_first += [remote(top_sum.at[1], cross_c, 13, 18, first_gates[5])]
    send_top_up7 = remote(up, top_up, 6, 20, hub)
    send_top_up8 = remote(up, top_up, 4, 20, center)
    send_top_cross = remote(cross, top_cross, 8, 14, center)
    send_up8 = [remote(up.at[s, 0], map_e, 4 + s, 21, hubs_of_center[s]) for s in range(2)]
    send_down8 = [remote(down.at[s, 0], map_b, 6 + s, 8, hubs_of_center[s]) for s in range(2)]
    send_down8_first = [remote(down.at[k // 4, 0], map_b, 8 + k, 8, first_gates[k]) for k in range(6)]
    pass_down8 = remote(map_b, map_b, 4, 8, at(z - 1, 1, 0, 0))
    send_cross9 = [remote(cross.at[0, 0], map_f, 2, 22, third_hub), remote(cross.at[0, 0], map_f, 3, 22, fourth_hub)]
    send_cross9 += [remote(cross.at[1, 0], map_f, 4, 22, at(4, 1, 0, 0))]
    send_part6 = [remote(path_coef, parts6.at[k], 2, (14, 15, 16, 16)[k], hub) for k in range(4)]
    send_child7 = remote(top_child, child, 3, 0, p7)
    send_coef7 = [remote(top_coef, top_child.at[:, part], 4, 15 + k, center) for k, part in enumerate((left_part, right_part))]
    send_part8 = [
        [remote(far_out, parts8.at[k], 5 + n, (17, 13)[k], device) for n, device in enumerate((*first_gates, second_hub))]
        for k in range(2)
    ]
    send_part8_right = [remote(far_out, parts8.at[0], 5 + k, 17, (third_hub, fourth_hub)[k]) for k in range(2)]
    send_above7 = [remote(top_out, above, n, 13, gates_of_p7[k]) for n, k in enumerate((3, 0, 1))]
    others = [at(z, 0, 2, 0), p3s_of_gate[0], p3s_of_gate[1], at(z, 0, 0, 0), at(z, 1, 2, 0), p3s_of_gate[2], p3s_of_gate[3]]
    send_above4 = [remote(outgoing.at[n // 4], above, 3 + n, 13, device) for n, device in enumerate(others)]
    head = at(z, core, x - 1, 0)
    send_head_map = remote(head_map, head_map, 0, 23, head)
    send_head_base = remote(cross_sum.at[0], head_base, 1, 24, head)
    send_above2 = [remote(head_out, leaf_above, 9 + k, 6, column[k]) for k in (1, 3, 2)]
    send_above2_right = [remote(outgoing.at[1], leaf_above, 1 + k, 6, column[k]) for k in (1, 3, 2)]

    def start(copies):
        for copy in copies:
            copy.start()

    def dot(a, b):
        return jnp.dot(a, b, preferred_element_type=F32)

    load_rhs.wait()
    load_in.wait()
    load_rank.wait()
    leaf_rank, node_rank = rank[0, 0], rank[0, 1]
    leaf_keep = lax.broadcasted_iota(jnp.int32, (rows, leaf_width), 1) < leaf_rank
    node_keep = lax.broadcasted_iota(jnp.int32, (rows, width), 1) < node_rank
    leaf_coef[...] = jnp.where(leaf_keep, dot(rhs[...], leaf_in[...]), 0.0).astype(BF16)

    pl.semaphore_wait(barrier, greeted)

    @pl.when(is_p1)
    def _():
        pl.semaphore_signal(go_sem, inc=1, device_id=left_leaf, device_id_type=MESH)

    @pl.when(both(both(ty == 1, core == 1), z == 8))
    def _():
        pl.semaphore_signal(late_sem, inc=1, device_id=at(8, 0, 0, 0), device_id_type=MESH)

    def mask_up():
        keep = lax.broadcasted_iota(jnp.int32, (width, width), 1) < node_rank
        for s in range(2):
            up[s, 0] = jnp.where(keep, up[s, 0], jnp.zeros((width, width), BF16))

    def mask_down():
        keep = lax.broadcasted_iota(jnp.int32, (width, width), 0) < node_rank
        for s in range(2):
            down[s, 0] = jnp.where(keep, down[s, 0], jnp.zeros((width, width), BF16))

    def send_up(summed, waits=False):
        coef[...] = jnp.where(node_keep, summed, 0.0).astype(BF16)
        if waits:
            pl.semaphore_wait(go_sem, 1)

        @pl.when(side == 0)
        def _():
            up_left.start()

        @pl.when(side == 1)
        def _():
            up_right.start()

    def cross_terms():
        cross_sum[0] = dot(child[:, right_part], cross[0, 0])
        cross_sum[1] = dot(child[:, left_part], cross[1, 0])

    @pl.when(is_even)
    def _():
        leaf_up.start()

    @pl.when(on_line)
    def _():
        pl.semaphore_wait(go_sem, 1)

    @pl.when(is_p1)
    def _():
        load_up.wait()
        summed = dot(leaf_coef[...], up[1, 0, narrow, :])
        leaf_up.wait_recv()
        send_up(summed + dot(child[:, narrow], up[0, 0, narrow, :]))
        load_cross.wait()
        cross_sum[0, :, narrow] = dot(leaf_coef[...], cross[0, 0, narrow, narrow])
        leaf_cross1[...] = dot(child[:, narrow], cross[1, 0, narrow, narrow])
        start(send_cross1)
        load_down.wait()
        mask_down()
        start(send_down1)
        leaf_map1[...] = down[1, 0, :, narrow]

    def lift(waits=True):
        up_left.wait_recv()
        summed = dot(child[:, left_part], up[0, 0])
        up_right.wait_recv()
        send_up(summed + dot(child[:, right_part], up[1, 0]), waits)

    @pl.when(is_p2)
    def _():
        load_up.wait()
        lift()
        load_cross.wait()
        cross_terms()
        start(send_cross2)
        leaf_cross2[...] = cross_sum[1]
        load_down.wait()
        mask_down()
        start(send_down2)
        leaf_map2[...] = down[1, 0]

    @pl.when(is_p3)
    def _():
        load_up.wait()
        lift()

        @pl.when(core == 0)
        def _():
            send_up4[0].wait_recv()
            path_coef[...] = dot(coef[...], map_a[...]).astype(BF16)
            for k in range(2):

                @pl.when(x // 2 == k)
                def _():
                    send_part4[k].start()

        load_cross.wait()
        cross_terms()
        load_down.wait()
        mask_down()

    @pl.when(is_p4)
    def _():
        load_up.wait()
        mask_up()
        pl.semaphore_wait(go_sem, 1)

        @pl.when(core == 0)
        def _():
            start(send_up4)
            load_down.wait()
            mask_down()
            start(send_down4)
            up_left.wait_recv()
            up_right.wait_recv()

        @pl.when(core == 1)
        def _():
            lift(waits=False)

        load_cross.wait()
        cross_terms()
        start(send_cross4)

        @pl.when(core == 1)
        def _():
            load_down.wait()
            mask_down()
            start(send_down4)

    @pl.when(is_gate)
    def _():
        load_up.wait()
        load_cross.wait()
        load_down.wait()
        mask_down()

        @pl.when(z % 4 == 1)
        def _():
            send_down7[0].wait_recv()
            pass_down7.start()

        map_keep = lax.broadcasted_iota(jnp.int32, (width, width), 1) < node_rank
        send_up6[0].wait_recv()
        for s in range(2):
            ahead = dot(jnp.where(map_keep, up[s, 0], jnp.zeros((width, width), BF16)), map_a[...])
            gate_maps[s] = ahead.astype(BF16)
        for copy in send_part4:
            copy.wait_recv()
        child[:, left_part] = (parts4[0].astype(F32) + parts4[1].astype(F32)).astype(BF16)
        up_right.wait_recv()
        six = dot(child[:, left_part], gate_maps[0]) + dot(child[:, right_part], gate_maps[1])
        path_coef[...] = six.astype(BF16)
        for k in (0, 1, 3):

            @pl.when(z % 4 == k)
            def _():
                send_part6[k].start()

        send_up(dot(child[:, left_part], up[0, 0]) + dot(child[:, right_part], up[1, 0]))

        @pl.when(is_hub)
        def _():
            parts6[2] = path_coef[...]
            send_top_up7.wait_recv()

            @pl.when(is_far_hub)
            def _():
                send_up8[0].wait_recv()
                send_cross9[0].wait_recv()
                map_e[...] = dot(map_e[...], map_f[...]).astype(BF16)

                @pl.when(z == 10)
                def _():
                    for k in range(2):
                        top_cross[k, 0] = dot(top_up[k, 0], map_e[...]).astype(BF16)

            for k in (0, 1, 3):
                send_part6[k].wait_recv()
            for k, part in enumerate((left_part, right_part)):
                six = parts6[2 * k].astype(F32) + parts6[2 * k + 1].astype(F32)
                top_child[:, part] = six.astype(BF16)

            @pl.when(z == 10)
            def _():
                far = dot(top_child[:, left_part], top_cross[0, 0]) + dot(top_child[:, right_part], top_cross[1, 0])
                far_out[...] = far.astype(BF16)
                start(send_part8[0])

            seven = dot(top_child[:, left_part], top_up[0, 0]) + dot(top_child[:, right_part], top_up[1, 0])
            top_coef[...] = seven.astype(BF16)
            for k in range(2):

                @pl.when(z // 4 % 2 == k)
                def _():
                    send_coef7[k].start()

            @pl.when(z == 14)
            def _():
                far_out[...] = dot(top_coef[...], map_e[...]).astype(BF16)
                start(send_part8[1])

            send_child7.start()

        def center_cross_terms():
            send_top_cross.wait_recv()
            top_sum[0] = dot(top_child[:, right_part], top_cross[0, 0]).astype(BF16)
            top_sum[1] = dot(top_child[:, left_part], top_cross[1, 0]).astype(BF16)

        @pl.when(is_left_center)
        def _():
            send_top_up8.wait_recv()
            send_coef7[0].wait_recv()
            send_coef7[1].wait_recv()
            center_cross_terms()
            start(send_cross8_first)
            send_cross8[1].start()
            cross_c[...] = top_sum[1]
            eight = dot(top_child[:, left_part], top_up[0, 0]) + dot(top_child[:, right_part], top_up[1, 0])
            top_coef[...] = eight.astype(BF16)
            send_cross9[2].wait_recv()
            far_out[...] = dot(top_coef[...], map_f[...]).astype(BF16)
            start(send_part8_right)

        @pl.when(is_right_center)
        def _():
            pl.semaphore_signal(late_sem, inc=1, device_id=p8, device_id_type=MESH)
            send_coef7[1].wait_recv()
            send_coef7[0].wait_recv()
            center_cross_terms()
            start(send_cross8)

        cross_terms()

        @pl.when(z == 1)
        def _():
            send_down8_first[0].wait_recv()
            pass_down8.start()

    @pl.when(is_p6)
    def _():
        load_up.wait()
        mask_up()
        start(send_up6)
        load_cross.wait()
        load_down.wait()
        mask_down()
        for copy in send_up6:
            copy.wait_send()
        send_down6[1].start()

        @pl.when(z % 4 == 1)
        def _():
            send_down6[0].start()

        @pl.when(both(z % 4 == 3, z != 7))
        def _():
            send_down6_half[0].start()

        up_right.wait_recv()

        @pl.when(both(z % 4 == 3, z != 7))
        def _():
            send_down6_half[1].start()

        @pl.when(z == 7)
        def _():
            send_down6[0].start()

        up_left.wait_recv()
        cross_terms()
        start(send_cross6)

    @pl.when(is_p7)
    def _():
        load_up.wait()
        mask_up()
        send_top_up7.start()
        load_down.wait()
        mask_down()
        start(send_down7[1:])
        load_cross.wait()
        send_child7.wait_recv()
        cross_terms()
        start(send_cross7)

    @pl.when(is_p8)
    def _():
        load_up.wait()
        mask_up()
        load_cross.wait()
        send_top_cross.start()
        load_down.wait()
        mask_down()

        @pl.when(is_left_p8)
        def _():
            send_down8[1].start()
            start(send_down8_first[4:])

        @pl.when(is_right_p8)
        def _():
            send_up8[1].start()

        send_cross1[0].wait_recv()

        @pl.when(is_right_p8)
        def _():
            send_down1[0].wait_recv()
            send_up8[0].start()
            pl.semaphore_wait(late_sem, 1)
            start(send_down8)

        @pl.when(is_left_p8)
        def _():
            send_top_up8.start()
            send_down8_first[1].start()
            send_down1[0].wait_recv()
            for k, after in ((1, 3), (3, 2)):
                send_down8_first[k].wait_send()
                send_down8_first[after].start()

    @pl.when(both(on_top, z % 8 == 0))
    def _():
        load_up.wait()
        load_cross.wait()
        load_down.wait()

    @pl.when(is_p9)
    def _():
        send_cross9[0].start()
        pl.semaphore_wait(late_sem, 1)
        send_cross9[1].start()
        send_cross9[2].start()

    load_diag.wait()
    product[...] = dot(rhs[...], diag[...])
    load_out.wait()

    def sent(condition, copies):
        @pl.when(condition)
        def _():
            for copy in copies:
                copy.wait_send()

    sent(is_even, [leaf_up])
    sent(is_p1, [up_left, *send_cross1, *send_down1])
    sent(is_p2, [up_left, *send_cross2, *send_down2])
    sent(both(is_p3, core == 0), [send_part4[0]])
    sent(is_p3, [up_left])
    sent(both(is_p4, core == 0), send_up4)
    sent(both(is_p4, core == 1), [up_left])
    sent(is_p4, [*send_cross4, *send_down4])
    sent(is_gate, [up_left])
    sent(both(is_gate, z % 4 != 2), [send_part6[0]])
    sent(is_hub, [send_coef7[0], send_child7])
    sent(is_far_hub, send_part8[0])
    sent(is_left_center, [*send_cross8_first, send_cross8[1], *send_part8_right])
    sent(is_right_center, send_cross8)
    sent(is_p6, [send_down6[1], *send_cross6])
    sent(both(is_p6, both(z % 4 == 3, z != 7)), send_down6_half)
    sent(both(is_p6, jnp.logical_not(both(z % 4 == 3, z != 7))), [send_down6[0]])
    sent(is_p7, [send_top_up7, *send_down7[1:], *send_cross7])
    sent(is_p8, [send_top_cross, send_down8[1]])
    sent(is_left_p8, [send_top_up8, send_down8_first[2], *send_down8_first[4:]])
    sent(is_right_p8, [*send_up8, send_down8[0]])
    sent(is_p9, send_cross9)

    def lower_hub():
        send_down8[0].wait_recv()
        send_cross8[0].wait_recv()
        send_part8[0][0].wait_recv()

        @pl.when(z == 6)
        def _():
            send_part8[1][0].wait_recv()
            crossed = parts8[0].astype(F32) + parts8[1].astype(F32)
            parts8[0] = crossed.astype(BF16)

        top_out[...] = (cross_c[...].astype(F32) + dot(parts8[0], map_b[...])).astype(BF16)
        send_above7[0].start()

        @pl.when(z > 6)
        def _():
            start(send_above7[1:])

        above[...] = top_out[...]

    @pl.when(is_gate)
    def _():
        @pl.when(z == 10)
        def _():
            lower_hub()

        @pl.when(z % 4 != 1)
        def _():
            send_down7[0].wait_recv()

        @pl.when(z % 4 == 1)
        def _():
            pass_down7.wait_send()

        send_down6[0].wait_recv()
        map_d[...] = dot(map_d[...], map_c[...]).astype(BF16)
        for s in range(2):
            gate_maps[s] = dot(map_d[...], down[s, 0]).astype(BF16)

        @pl.when(both(z < 6, z != 1))
        def _():
            send_down8_first[0].wait_recv()

        @pl.when(z == 1)
        def _():
            pass_down8.wait_send()

        @pl.when(z < 6)
        def _():
            for s in range(2):
                top_up[s, 0] = dot(map_b[...], gate_maps[s]).astype(BF16)

        send_cross7[0].wait_recv()
        send_cross6[0].wait_recv()
        five = (cross_b[...] + dot(cross_a[...].astype(BF16), map_c[...])).astype(BF16)
        for s in range(2):
            cross_sum[s] += dot(five, down[s, 0])

        @pl.when(z < 6)
        def _():
            send_part8[1][0].wait_recv()
            for s in range(2):
                cross_sum[s] += dot(parts8[1], top_up[s, 0])

            @pl.when(z != 4)
            def _():
                send_cross8_first[0].wait_recv()

            send_part8[0][0].wait_recv()
            for s in range(2):
                four = cross_sum[s] + dot(cross_c[...], gate_maps[s]) + dot(parts8[0], top_up[s, 0])
                outgoing[s] = four.astype(BF16)
                start(send_above4[4 * s : 4 * s + 4])

        @pl.when(both(is_late_hub, z != 10))
        def _():
            lower_hub()

        @pl.when(both(z > 6, z % 4 != 2))
        def _():
            send_above7[0].wait_recv()

        @pl.when(z >= 6)
        def _():
            for s in range(2):
                outgoing[s] = (cross_sum[s] + dot(above[...], gate_maps[s])).astype(BF16)
                start(send_above4[4 * s : 4 * s + 4])

    @pl.when(is_p3)
    def _():
        send_down4[0].wait_recv()
        head_map[...] = dot(map_d[...], down[0, 0]).astype(BF16)
        send_head_map.start()
        send_cross4[0].wait_recv()
        cross_four = cross_a[...].astype(BF16)
        cross_sum[0] += dot(cross_four, down[0, 0])
        send_head_base.start()
        cross_sum[1] += dot(cross_four, down[1, 0])
        down[1, 0] = dot(map_d[...], down[1, 0]).astype(BF16)
        send_above4[0].wait_recv()
        outgoing[1] = (cross_sum[1] + dot(above[...], down[1, 0])).astype(BF16)
        start(send_above2_right)
        leaf_above[...] = outgoing[1]

    @pl.when(is_head)
    def _():
        send_head_map.wait_recv()
        send_head_base.wait_recv()

        @pl.when(is_gate)
        def _():
            head_out[...] = (head_base[...] + dot(outgoing[1], head_map[...])).astype(BF16)

        @pl.when(jnp.logical_not(is_gate))
        def _():
            send_above4[0].wait_recv()
            head_out[...] = (head_base[...] + dot(above[...], head_map[...])).astype(BF16)

        start(send_above2)
        leaf_above[...] = head_out[...]

    @pl.when(both(is_even, jnp.logical_not(is_p8)))
    def _():
        send_cross1[0].wait_recv()
        send_down1[0].wait_recv()

    @pl.when(jnp.logical_not(is_p2))
    def _():
        send_cross2[0].wait_recv()
        send_down2[0].wait_recv()

    zero = dot(leaf_cross2[...].astype(BF16), leaf_map1[...]) + leaf_cross1[...]
    zero = jnp.where(leaf_keep, zero, 0.0).astype(BF16)
    product[...] += dot(zero, leaf_out[...])
    map_keep = lax.broadcasted_iota(jnp.int32, (width, leaf_width), 1) < leaf_rank
    leaf_map1[...] = jnp.where(map_keep, dot(leaf_map2[...], leaf_map1[...]), 0.0).astype(BF16)
    leaf_map2[...] = dot(leaf_map1[...], leaf_out[...]).astype(BF16)

    @pl.when(y > 0)
    def _():
        send_above2[0].wait_recv()

    product[...] += dot(leaf_above[...], leaf_map2[...])

    sent(is_head, send_above2)
    sent(is_p3, [send_head_map, send_head_base, *send_above2_right])
    sent(is_gate, send_above4)
    sent(is_late_hub, send_above7[:1])
    sent(is_far_hub, send_above7[1:])


def on_device(rhs, diag_blocks, leaf_in, leaf_out, up_maps, cross_maps, down_maps, node_rank):
    rows, leaf = rhs.shape
    width, leaf_width = up_maps.shape[-1], leaf_in.shape[1]
    operands = (rhs, diag_blocks, leaf_in, leaf_out, up_maps, cross_maps, down_maps)

    def vector(*lead, kind=BF16, columns=width):
        return pltpu.VMEM((*lead, rows, columns), kind)

    full_map = pltpu.VMEM((width, width), BF16)
    return pl.pallas_call(
        kernel,
        out_shape=pltpu.VMEM((rows, leaf), F32),
        in_specs=[pl.BlockSpec(memory_space=pl.ANY)] * 8,
        out_specs=pl.BlockSpec(memory_space=pltpu.VMEM),
        scratch_shapes=[pltpu.VMEM(each.shape, each.dtype) for each in operands]
        + [
            pltpu.SMEM(node_rank.shape, node_rank.dtype),
            vector(columns=leaf_width),
            vector(),
            vector(columns=2 * width),
            vector(2, kind=F32),
            vector(),
            vector(2),
            full_map,
            full_map,
            full_map,
            full_map,
            full_map,
            full_map,
            pltpu.VMEM(up_maps.shape, BF16),
            pltpu.VMEM(cross_maps.shape, BF16),
            vector(columns=2 * width),
            vector(),
            vector(2),
            vector(),
            vector(),
            pltpu.VMEM((2, width, width), BF16),
            full_map,
            vector(kind=F32),
            vector(),
            full_map,
            pltpu.VMEM((width, leaf_width), BF16),
            vector(kind=F32),
            vector(kind=F32),
            vector(),
            vector(kind=F32),
            vector(kind=F32, columns=leaf_width),
            vector(),
            vector(),
            vector(2),
            vector(4),
            vector(2),
            pltpu.SemaphoreType.DMA((8,)),
            pltpu.SemaphoreType.DMA((14,)),
            pltpu.SemaphoreType.DMA((25,)),
            pltpu.SemaphoreType.REGULAR,
            pltpu.SemaphoreType.REGULAR,
        ],
        compiler_params=pltpu.CompilerParams(
            collective_id=0, has_side_effects=True, vmem_limit_bytes=60 * 2**20
        ),
    )(*operands, node_rank)


def solution(mesh):
    assert mesh.shape["tx"] == N_Z * N_CORE and mesh.shape["ty"] == N_X * N_Y
    in_specs = (
        P(None, ("tx", "ty")),
        P(("tx", "ty"), None),
        P(("tx", "ty"), None),
        P(("tx", "ty"), None),
        P(None, ("tx", "ty"), None, None),
        P(None, ("tx", "ty"), None, None),
        P(None, ("tx", "ty"), None, None),
        P(("tx", "ty"), None),
    )
    return jax.shard_map(
        on_device, mesh=mesh, in_specs=in_specs, out_specs=P(None, ("tx", "ty")), check_vma=False
    )
```

```python
import functools

import jax
import jax.numpy as jnp
from jax import lax
from jax.experimental import pallas as pl
from jax.experimental.pallas import tpu as pltpu
from jax.sharding import PartitionSpec as P

MESH = pl.DeviceIdType.MESH
F32 = jnp.float32
BF16 = jnp.bfloat16
N_Z, N_CORE, N_X, N_Y = 16, 2, 4, 4


def kernel(
    rhs_hbm,
    diag_hbm,
    in_hbm,
    out_hbm,
    up_hbm,
    cross_hbm,
    down_hbm,
    rank_hbm,
    product,
    rhs,
    diag,
    leaf_in,
    leaf_out,
    up,
    cross,
    down,
    rank,
    leaf_coef,
    coef,
    child,
    cross_sum,
    path_coef,
    outgoing,
    map_a,
    map_b,
    map_c,
    map_d,
    map_e,
    map_f,
    top_up,
    top_cross,
    top_child,
    top_coef,
    top_sum,
    top_out,
    far_out,
    gate_maps,
    head_map,
    head_base,
    head_out,
    map_0,
    base_0,
    above_0,
    out_0,
    leaf_map2,
    leaf_map1,
    cross_a,
    cross_b,
    cross_c,
    leaf_cross2,
    leaf_cross1,
    above,
    leaf_above,
    parts4,
    parts6,
    parts8,
    load_sem,
    send_sem,
    recv_sem,
    go_sem,
    late_sem,
):
    rows, width = coef.shape
    leaf_width = leaf_coef.shape[1]
    loads = [
        pltpu.make_async_copy(source, target, load_sem.at[n])
        for n, (source, target) in enumerate(
            (
                (rhs_hbm, rhs),
                (in_hbm, leaf_in),
                (rank_hbm, rank),
                (up_hbm, up),
                (cross_hbm, cross),
                (down_hbm, down),
                (diag_hbm, diag),
                (out_hbm, leaf_out),
            )
        )
    ]
    load_rhs, load_in, load_rank, load_up, load_cross, load_down, load_diag, load_out = loads
    quarter = in_hbm.shape[0] // 4
    for n in range(4):
        part = pl.ds(n * quarter, quarter)
        pltpu.make_async_copy(in_hbm.at[part], leaf_in.at[part], load_sem.at[1]).start()
    load_rhs.start()
    load_rank.start()

    tx, ty = lax.axis_index("tx"), lax.axis_index("ty")
    z, core = tx // N_CORE, tx % N_CORE
    x, y = ty // N_Y, ty % N_Y

    def at(z, core, x, y):
        return (z * N_CORE + core, x * N_Y + y)

    both = jnp.logical_and
    on_line = ty == 0
    on_top = both(on_line, core == 0)
    is_p1 = y % 2 == 1
    is_p2 = y == 2
    is_p3 = both(y == 0, x % 2 == 1)
    is_p4 = both(y == 0, x == 2)
    is_gate = both(on_line, core == 1)
    is_p6 = both(on_top, z % 2 == 1)
    is_p7 = both(on_top, z % 4 == 2)
    is_p8 = both(on_top, z % 8 == 4)
    is_p9 = both(on_top, z == 8)
    is_even = y % 2 == 0
    is_head = both(y == 0, x % 2 == 0)
    is_hub = both(is_gate, z % 4 == 2)
    is_late_hub = both(is_hub, z > 2)
    is_far_hub = both(is_hub, z >= 8)
    is_left_center = both(is_gate, z == 4)
    is_right_center = both(is_gate, z == 12)
    is_left_p8 = both(on_top, z == 4)
    is_right_p8 = both(on_top, z == 12)

    x_odd = x // 2 * 2 + 1
    z_odd, z_seven, z_eight = z // 2 * 2 + 1, z // 4 * 4 + 2, z // 8 * 8 + 4
    leaf_peer = at(z, core, x, y + 1)
    left_leaf = at(z, core, x, y - 1)
    column = [at(z, core, x, k) for k in range(N_Y)]
    my_p3 = at(z, core, x_odd, 0)
    p3s = [at(z, core, 1, 0), at(z, core, 3, 0)]
    p4 = at(z, core, 2, 0)
    gate = at(z, 1, 0, 0)
    p3s_of_gate = [at(z, c, k, 0) for c in range(N_CORE) for k in (1, 3)]
    p4s_of_gate = [at(z, c, 2, 0) for c in range(N_CORE)]
    p6, p7, p8 = at(z_odd, 0, 0, 0), at(z_seven, 0, 0, 0), at(z_eight, 0, 0, 0)
    gates_of_p6 = [at(z_odd - 1, 1, 0, 0), at(z_odd, 1, 0, 0)]
    gates_of_p7 = [at(z_seven - 2 + k, 1, 0, 0) for k in range(4)]
    hub, center = at(z_seven, 1, 0, 0), at(z_eight, 1, 0, 0)
    hubs_of_center = [at(z_eight - 2, 1, 0, 0), at(z_eight + 2, 1, 0, 0)]
    first_gates = [at(k, 1, 0, 0) for k in range(6)]
    second_hub, third_hub, fourth_hub = at(6, 1, 0, 0), at(10, 1, 0, 0), at(14, 1, 0, 0)

    barrier = pltpu.get_barrier_semaphore()

    def greet(condition, devices):
        @pl.when(condition)
        def _():
            for device in devices:
                pl.semaphore_signal(barrier, inc=1, device_id=device, device_id_type=MESH)

    def collector(z, core, x):
        return at(z, core, x, 1)

    x_even = x % 2 == 0
    next_p3 = collector(z, core, x_odd)
    greet(is_p1, [left_leaf])
    greet(y == 1, [column[3]])
    on_one = core == 1
    greet(core == 0, [collector(z, 1, x)])
    greet(both(y == 3, on_one), [collector(z, core, x)])
    greet(is_p2, [column[1], column[3]])
    greet(both(both(is_p2, x % 2 == 1), on_one), [column[1]])
    greet(y == 0, [column[1], column[3]])
    greet(both(is_head, on_one), [next_p3, collector(z, 0, x_odd)])
    greet(is_p3, [at(z, core, x - 1, 3), collector(z, core, 2)])
    greet(both(is_p3, on_one), [collector(z, 1, 0), collector(z, 0, x)])
    greet(is_p4, [collector(z, core, 1), collector(z, core, 3)])
    greet(both(is_p4, on_one), [collector(z, 1, 0)])
    greet(is_gate, [collector(z, 0, 1), collector(z, 0, 3), collector(z, 1, 2)] + [collector(z_odd, 0, 0), collector(z_seven, 0, 0)])
    greet(both(is_gate, z % 4 == 0), [collector(z + 1, 1, 0)])
    greet(both(is_gate, both(z < 6, z != 4)), [collector(4, 0, 0), collector(8, 0, 0), collector(4, 1, 0)])
    greet(both(both(is_gate, z > 6), z % 4 != 2), [collector(z_seven, 1, 0)])
    greet(is_hub, [collector(z_seven - 2 + k, 1, 0) for k in (0, 1, 3)])
    greet(is_late_hub, [collector(z_eight, 0, 0), collector(z_eight, 1, 0)])
    greet(both(is_late_hub, z < 12), [collector(8, 0, 0)])
    greet(both(is_late_hub, z > 12), [collector(8, 1, 0)])
    greet(is_p9, [collector(8, 1, 0)])
    greet(
        both(is_gate, z % 8 == 4),
        [collector(z_eight - 2, 1, 0), collector(z_eight + 2, 1, 0), collector(z, 0, 0)],
    )
    greet(is_left_center, [collector(8, 0, 0)])
    greet(is_p6, [collector(z_odd - 1, 1, 0), collector(z_odd, 1, 0)])
    greet(is_p7, [collector(z, 1, 0)])
    greet(is_right_p8, [collector(z, 1, 0)])
    sizes = (
        (is_even, 1),
        (y == 3, 3),
        (both(y == 3, x_even), 1),
        (y == 1, 2),
        (both(y == 1, on_one), 4),
        (both(both(y == 1, x_even), on_one), 1),
        (both(y == 1, x % 2 == 1), 4),
        (both(y == 1, x == 2), 2 + core),
        (both(ty == 1, core == 1), 4),
        (both(both(ty == 1, core == 1), z % 4 != 2), 1),
        (both(both(ty == 1, core == 1), z % 4 == 1), 1),
        (both(both(ty == 1, core == 1), z % 4 == 2), 2),
        (both(both(ty == 1, core == 1), z == 6), 1),
        (both(both(ty == 1, core == 1), both(z % 4 == 2, z > 6)), 3),
        (both(both(ty == 1, core == 1), z == 4), 6),
        (both(both(ty == 1, core == 1), z == 12), 3),
        (both(both(ty == 1, core == 1), z == 8), 2),
        (both(both(ty == 1, core == 0), z % 2 == 1), 2),
        (both(both(ty == 1, core == 0), z % 4 == 2), 4),
        (both(both(ty == 1, core == 0), z == 4), 7),
        (both(both(ty == 1, core == 0), z == 12), 3),
        (both(both(ty == 1, core == 0), z == 8), 8),
    )
    greeted = sum(condition.astype(jnp.int32) * size for condition, size in sizes)
    for load in loads[3:]:
        load.start()

    def remote(source, target, send, recv, device):
        return pltpu.make_async_remote_copy(
            src_ref=source,
            dst_ref=target,
            send_sem=send_sem.at[send],
            recv_sem=recv_sem.at[recv],
            device_id=device,
            device_id_type=MESH,
        )

    left_part, right_part = pl.ds(0, width), pl.ds(width, width)
    narrow = pl.ds(0, leaf_width)

    leaf_up = remote(leaf_coef, child.at[:, narrow], 0, 0, leaf_peer)
    side = jnp.where(
        is_p1,
        y // 2,
        jnp.where(is_p2, x % 2, jnp.where(is_p3, x // 2, jnp.where(is_p4, core, z % 2))),
    )
    steps = ((is_p1, column[2]), (is_p2, my_p3), (is_p3, p4), (is_p4, gate), (is_gate, p6))
    parent = tuple(sum(condition.astype(jnp.int32) * device[k] for condition, device in steps) for k in range(2))
    up_left = remote(coef, child.at[:, left_part], 1, 0, parent)
    up_right = remote(coef, child.at[:, right_part], 1, 1, parent)
    send_cross1 = [remote(cross_sum.at[0, :, narrow], leaf_cross1, 2, 2, left_leaf)]
    send_down1 = [remote(down.at[0, 0, :, narrow], leaf_map1, 3, 3, left_leaf)]
    sides2 = ((0, 0), (1, 0), (3, 1))
    send_cross2 = [remote(cross_sum.at[s], leaf_cross2, 2 + n, 4, column[k]) for n, (k, s) in enumerate(sides2)]
    send_down2 = [remote(down.at[s, 0], leaf_map2, 5 + n, 5, column[k]) for n, (k, s) in enumerate(sides2)]
    send_cross4 = [remote(cross_sum.at[s], cross_a, 2 + s, 11, p3s[s]) for s in range(2)]
    send_up4 = [remote(up.at[s, 0], map_a, 7 + s, 7, p3s[s]) for s in range(2)]
    send_part4 = [remote(path_coef, parts4.at[k], 9, (19, 0)[k], gate) for k in range(2)]
    send_down4 = [remote(down.at[s, 0], map_d, 5 + s, 10, p3s[s]) for s in range(2)]
    send_cross6 = [remote(cross_sum.at[s], cross_b, 2 + s, 12, gates_of_p6[s]) for s in range(2)]
    send_up6 = [remote(up.at[s, 0], map_a, 4 + s, 7, gates_of_p6[s]) for s in range(2)]
    send_down6 = [remote(down.at[s, 0], map_c, 6 + s, 9, gates_of_p6[s]) for s in range(2)]
    halves = [pl.ds(k * (width // 2), width // 2) for k in range(2)]
    send_down6_half = [remote(down.at[0, 0, half], map_c.at[half], (6, 8)[k], 9, gates_of_p6[0]) for k, half in enumerate(halves)]
    send_cross7 = [remote(cross_sum.at[k // 2], cross_a, 2 + k, 11, gates_of_p7[k]) for k in range(4)]
    send_down7 = [remote(down.at[k // 2, 0], map_d, 6 + k, 10, gates_of_p7[k]) for k in range(4)]
    pass_down7 = remote(map_d, map_d, 3, 10, at(z - 1, 1, 0, 0))
    send_cross8 = [remote(top_sum.at[s], cross_c, 7 + s, 18, hubs_of_center[s]) for s in range(2)]
    send_cross8_first = [remote(top_sum.at[0], cross_c, 9 + k, 18, first_gates[k]) for k in range(4)]
    send_cross8_first += [remote(top_sum.at[1], cross_c, 13, 18, first_gates[5])]
    send_top_up7 = remote(up, top_up, 6, 20, hub)
    send_top_up8 = remote(up, top_up, 4, 20, center)
    send_top_cross = remote(cross, top_cross, 8, 14, center)
    send_up8 = [remote(up.at[s, 0], map_e, 4 + s, 21, hubs_of_center[s]) for s in range(2)]
    send_down8 = [remote(down.at[s, 0], map_b, 6 + s, 8, hubs_of_center[s]) for s in range(2)]
    send_down8_first = [remote(down.at[k // 4, 0], map_b, 8 + k, 8, first_gates[k]) for k in range(6)]
    pass_down8 = remote(map_b, map_b, 4, 8, at(z - 1, 1, 0, 0))
    send_cross9 = [remote(cross.at[0, 0], map_f, 2, 22, third_hub), remote(cross.at[0, 0], map_f, 3, 22, fourth_hub)]
    send_cross9 += [remote(cross.at[1, 0], map_f, 4, 22, at(4, 1, 0, 0))]
    send_part6 = [remote(path_coef, parts6.at[k], 2, (14, 15, 16, 16)[k], hub) for k in range(4)]
    send_child7 = remote(top_child, child, 3, 0, p7)
    send_coef7 = [remote(top_coef, top_child.at[:, part], 4, 15 + k, center) for k, part in enumerate((left_part, right_part))]
    send_part8 = [
        [remote(far_out, parts8.at[k], 5 + n, (17, 13)[k], device) for n, device in enumerate((*first_gates, second_hub))]
        for k in range(2)
    ]
    send_part8_right = [remote(far_out, parts8.at[0], 5 + k, 17, (third_hub, fourth_hub)[k]) for k in range(2)]
    send_above7 = [remote(top_out, above, n, 13, gates_of_p7[k]) for n, k in enumerate((3, 0, 1))]
    servers = [at(z, 1, 2, 0), at(z, 1, 1, 0), at(z, 1, 3, 0)]
    send_above4 = [remote(outgoing.at[0], above_0, 3 + n, 27, device) for n, device in enumerate(servers)]
    send_above4 += [remote(outgoing.at[1], above, 6 + n, 13, device) for n, device in enumerate(servers)]
    head = at(z, 1, x - 1, 0)
    send_head_map = remote(head_map, head_map, 0, 23, head)
    send_head_base = remote(cross_sum.at[0], head_base, 1, 24, head)
    send_head_map_0 = remote(head_map, map_0, 0, 25, head)
    send_head_base_0 = remote(cross_sum.at[0], base_0, 1, 26, head)
    send_map_0 = remote(down.at[1, 0], map_0, 2, 25, at(z, 1, x, 0))
    send_base_0 = remote(cross_sum.at[1], base_0, 3, 26, at(z, 1, x, 0))
    send_above2_0 = [remote(out_0, leaf_above, (13, 9, 14, 15)[n], 6, at(z, 0, x, k)) for n, k in enumerate((1, 3, 2, 0))]
    send_above2 = [remote(head_out, leaf_above, 9 + k, 6, column[k]) for k in (1, 3, 2)]
    send_above2_right = [remote(outgoing.at[1], leaf_above, 1 + k, 6, column[k]) for k in (1, 3, 2)]

    def start(copies):
        for copy in copies:
            copy.start()

    def dot(a, b):
        return jnp.dot(a, b, preferred_element_type=F32)

    load_rhs.wait()
    load_in.wait()
    load_rank.wait()
    leaf_rank, node_rank = rank[0, 0], rank[0, 1]
    leaf_keep = lax.broadcasted_iota(jnp.int32, (rows, leaf_width), 1) < leaf_rank
    node_keep = lax.broadcasted_iota(jnp.int32, (rows, width), 1) < node_rank
    leaf_coef[...] = jnp.where(leaf_keep, dot(rhs[...], leaf_in[...]), 0.0).astype(BF16)

    pl.semaphore_wait(barrier, greeted)

    @pl.when(is_p1)
    def _():
        pl.semaphore_signal(go_sem, inc=1, device_id=left_leaf, device_id_type=MESH)

    @pl.when(both(both(ty == 1, core == 1), z == 8))
    def _():
        pl.semaphore_signal(late_sem, inc=1, device_id=at(8, 0, 0, 0), device_id_type=MESH)

    def mask_up():
        keep = lax.broadcasted_iota(jnp.int32, (width, width), 1) < node_rank
        for s in range(2):
            up[s, 0] = jnp.where(keep, up[s, 0], jnp.zeros((width, width), BF16))

    def mask_down():
        keep = lax.broadcasted_iota(jnp.int32, (width, width), 0) < node_rank
        for s in range(2):
            down[s, 0] = jnp.where(keep, down[s, 0], jnp.zeros((width, width), BF16))

    def send_up(summed, waits=False):
        coef[...] = jnp.where(node_keep, summed, 0.0).astype(BF16)
        if waits:
            pl.semaphore_wait(go_sem, 1)

        @pl.when(side == 0)
        def _():
            up_left.start()

        @pl.when(side == 1)
        def _():
            up_right.start()

    def cross_terms():
        cross_sum[0] = dot(child[:, right_part], cross[0, 0])
        cross_sum[1] = dot(child[:, left_part], cross[1, 0])

    @pl.when(is_even)
    def _():
        leaf_up.start()

    @pl.when(on_line)
    def _():
        pl.semaphore_wait(go_sem, 1)

    @pl.when(is_p1)
    def _():
        load_up.wait()
        summed = dot(leaf_coef[...], up[1, 0, narrow, :])
        leaf_up.wait_recv()
        send_up(summed + dot(child[:, narrow], up[0, 0, narrow, :]))
        load_cross.wait()
        cross_sum[0, :, narrow] = dot(leaf_coef[...], cross[0, 0, narrow, narrow])
        leaf_cross1[...] = dot(child[:, narrow], cross[1, 0, narrow, narrow])
        start(send_cross1)
        load_down.wait()
        mask_down()
        start(send_down1)
        leaf_map1[...] = down[1, 0, :, narrow]

    def lift(waits=True):
        up_left.wait_recv()
        summed = dot(child[:, left_part], up[0, 0])
        up_right.wait_recv()
        send_up(summed + dot(child[:, right_part], up[1, 0]), waits)

    @pl.when(is_p2)
    def _():
        load_up.wait()
        lift()
        load_cross.wait()
        cross_terms()
        start(send_cross2)
        leaf_cross2[...] = cross_sum[1]
        load_down.wait()
        mask_down()
        start(send_down2)
        leaf_map2[...] = down[1, 0]

    @pl.when(is_p3)
    def _():
        load_up.wait()
        lift()

        @pl.when(core == 0)
        def _():
            send_up4[0].wait_recv()
            path_coef[...] = dot(coef[...], map_a[...]).astype(BF16)
            for k in range(2):

                @pl.when(x // 2 == k)
                def _():
                    send_part4[k].start()

        load_cross.wait()
        cross_terms()
        load_down.wait()
        mask_down()

    @pl.when(is_p4)
    def _():
        load_up.wait()
        mask_up()
        pl.semaphore_wait(go_sem, 1)

        @pl.when(core == 0)
        def _():
            start(send_up4)
            load_down.wait()
            mask_down()
            start(send_down4)
            up_left.wait_recv()
            up_right.wait_recv()

        @pl.when(core == 1)
        def _():
            lift(waits=False)

        load_cross.wait()
        cross_terms()
        start(send_cross4)

        @pl.when(core == 1)
        def _():
            load_down.wait()
            mask_down()
            start(send_down4)

    @pl.when(is_gate)
    def _():
        load_up.wait()
        load_cross.wait()
        load_down.wait()
        mask_down()

        @pl.when(z % 4 == 1)
        def _():
            send_down7[0].wait_recv()
            pass_down7.start()

        map_keep = lax.broadcasted_iota(jnp.int32, (width, width), 1) < node_rank
        send_up6[0].wait_recv()
        for s in range(2):
            ahead = dot(jnp.where(map_keep, up[s, 0], jnp.zeros((width, width), BF16)), map_a[...])
            gate_maps[s] = ahead.astype(BF16)
        for copy in send_part4:
            copy.wait_recv()
        child[:, left_part] = (parts4[0].astype(F32) + parts4[1].astype(F32)).astype(BF16)
        up_right.wait_recv()
        six = dot(child[:, left_part], gate_maps[0]) + dot(child[:, right_part], gate_maps[1])
        path_coef[...] = six.astype(BF16)
        for k in (0, 1, 3):

            @pl.when(z % 4 == k)
            def _():
                send_part6[k].start()

        send_up(dot(child[:, left_part], up[0, 0]) + dot(child[:, right_part], up[1, 0]))

        @pl.when(is_hub)
        def _():
            parts6[2] = path_coef[...]
            send_top_up7.wait_recv()

            @pl.when(is_far_hub)
            def _():
                send_up8[0].wait_recv()
                send_cross9[0].wait_recv()
                map_e[...] = dot(map_e[...], map_f[...]).astype(BF16)

                @pl.when(z == 10)
                def _():
                    for k in range(2):
                        top_cross[k, 0] = dot(top_up[k, 0], map_e[...]).astype(BF16)

            for k in (0, 1, 3):
                send_part6[k].wait_recv()
            for k, part in enumerate((left_part, right_part)):
                six = parts6[2 * k].astype(F32) + parts6[2 * k + 1].astype(F32)
                top_child[:, part] = six.astype(BF16)

            @pl.when(z == 10)
            def _():
                far = dot(top_child[:, left_part], top_cross[0, 0]) + dot(top_child[:, right_part], top_cross[1, 0])
                far_out[...] = far.astype(BF16)
                start(send_part8[0])

            seven = dot(top_child[:, left_part], top_up[0, 0]) + dot(top_child[:, right_part], top_up[1, 0])
            top_coef[...] = seven.astype(BF16)
            for k in range(2):

                @pl.when(z // 4 % 2 == k)
                def _():
                    send_coef7[k].start()

            @pl.when(z == 14)
            def _():
                far_out[...] = dot(top_coef[...], map_e[...]).astype(BF16)
                start(send_part8[1])

            send_child7.start()

        def center_cross_terms():
            send_top_cross.wait_recv()
            top_sum[0] = dot(top_child[:, right_part], top_cross[0, 0]).astype(BF16)
            top_sum[1] = dot(top_child[:, left_part], top_cross[1, 0]).astype(BF16)

        @pl.when(is_left_center)
        def _():
            send_top_up8.wait_recv()
            send_coef7[0].wait_recv()
            send_coef7[1].wait_recv()
            center_cross_terms()
            start(send_cross8_first)
            send_cross8[1].start()
            cross_c[...] = top_sum[1]
            eight = dot(top_child[:, left_part], top_up[0, 0]) + dot(top_child[:, right_part], top_up[1, 0])
            top_coef[...] = eight.astype(BF16)
            send_cross9[2].wait_recv()
            far_out[...] = dot(top_coef[...], map_f[...]).astype(BF16)
            start(send_part8_right)

        @pl.when(is_right_center)
        def _():
            pl.semaphore_signal(late_sem, inc=1, device_id=p8, device_id_type=MESH)
            send_coef7[1].wait_recv()
            send_coef7[0].wait_recv()
            center_cross_terms()
            start(send_cross8)

        cross_terms()

        @pl.when(z == 1)
        def _():
            send_down8_first[0].wait_recv()
            pass_down8.start()

    @pl.when(is_p6)
    def _():
        load_up.wait()
        mask_up()
        start(send_up6)
        load_cross.wait()
        load_down.wait()
        mask_down()
        for copy in send_up6:
            copy.wait_send()
        send_down6[1].start()

        @pl.when(z % 4 == 1)
        def _():
            send_down6[0].start()

        @pl.when(both(z % 4 == 3, z != 7))
        def _():
            send_down6_half[0].start()

        up_right.wait_recv()

        @pl.when(both(z % 4 == 3, z != 7))
        def _():
            send_down6_half[1].start()

        @pl.when(z == 7)
        def _():
            send_down6[0].start()

        up_left.wait_recv()
        cross_terms()
        start(send_cross6)

    @pl.when(is_p7)
    def _():
        load_up.wait()
        mask_up()
        send_top_up7.start()
        load_down.wait()
        mask_down()
        start(send_down7[1:])
        load_cross.wait()
        send_child7.wait_recv()
        cross_terms()
        start(send_cross7)

    @pl.when(is_p8)
    def _():
        load_up.wait()
        mask_up()
        load_cross.wait()
        send_top_cross.start()
        load_down.wait()
        mask_down()

        @pl.when(is_left_p8)
        def _():
            send_down8[1].start()
            start(send_down8_first[4:])

        @pl.when(is_right_p8)
        def _():
            send_up8[1].start()

        send_cross1[0].wait_recv()

        @pl.when(is_right_p8)
        def _():
            send_down1[0].wait_recv()
            send_up8[0].start()
            pl.semaphore_wait(late_sem, 1)
            start(send_down8)

        @pl.when(is_left_p8)
        def _():
            send_top_up8.start()
            send_down8_first[1].start()
            send_down1[0].wait_recv()
            for k, after in ((1, 3), (3, 2)):
                send_down8_first[k].wait_send()
                send_down8_first[after].start()

    @pl.when(both(on_top, z % 8 == 0))
    def _():
        load_up.wait()
        load_cross.wait()
        load_down.wait()

    @pl.when(is_p9)
    def _():
        send_cross9[0].start()
        pl.semaphore_wait(late_sem, 1)
        send_cross9[1].start()
        send_cross9[2].start()

    load_diag.wait()
    product[...] = dot(rhs[...], diag[...])
    load_out.wait()

    def sent(condition, copies):
        @pl.when(condition)
        def _():
            for copy in copies:
                copy.wait_send()

    sent(is_even, [leaf_up])
    sent(is_p1, [up_left, *send_cross1, *send_down1])
    sent(is_p2, [up_left, *send_cross2, *send_down2])
    sent(both(is_p3, core == 0), [send_part4[0]])
    sent(is_p3, [up_left])
    sent(both(is_p4, core == 0), send_up4)
    sent(both(is_p4, core == 1), [up_left])
    sent(is_p4, [*send_cross4, *send_down4])
    sent(is_gate, [up_left])
    sent(both(is_gate, z % 4 != 2), [send_part6[0]])
    sent(is_hub, [send_coef7[0], send_child7])
    sent(is_far_hub, send_part8[0])
    sent(is_left_center, [*send_cross8_first, send_cross8[1], *send_part8_right])
    sent(is_right_center, send_cross8)
    sent(is_p6, [send_down6[1], *send_cross6])
    sent(both(is_p6, both(z % 4 == 3, z != 7)), send_down6_half)
    sent(both(is_p6, jnp.logical_not(both(z % 4 == 3, z != 7))), [send_down6[0]])
    sent(is_p7, [send_top_up7, *send_down7[1:], *send_cross7])
    sent(is_p8, [send_top_cross, send_down8[1]])
    sent(is_left_p8, [send_top_up8, send_down8_first[2], *send_down8_first[4:]])
    sent(is_right_p8, [*send_up8, send_down8[0]])
    sent(is_p9, send_cross9)

    def lower_hub():
        send_down8[0].wait_recv()
        send_cross8[0].wait_recv()
        send_part8[0][0].wait_recv()

        @pl.when(z == 6)
        def _():
            send_part8[1][0].wait_recv()
            crossed = parts8[0].astype(F32) + parts8[1].astype(F32)
            parts8[0] = crossed.astype(BF16)

        top_out[...] = (cross_c[...].astype(F32) + dot(parts8[0], map_b[...])).astype(BF16)
        send_above7[0].start()

        @pl.when(z > 6)
        def _():
            start(send_above7[1:])

        above[...] = top_out[...]

    @pl.when(is_gate)
    def _():
        @pl.when(z == 10)
        def _():
            lower_hub()

        @pl.when(z % 4 != 1)
        def _():
            send_down7[0].wait_recv()

        @pl.when(z % 4 == 1)
        def _():
            pass_down7.wait_send()

        send_down6[0].wait_recv()
        map_d[...] = dot(map_d[...], map_c[...]).astype(BF16)
        for s in range(2):
            gate_maps[s] = dot(map_d[...], down[s, 0]).astype(BF16)

        @pl.when(both(z < 6, z != 1))
        def _():
            send_down8_first[0].wait_recv()

        @pl.when(z == 1)
        def _():
            pass_down8.wait_send()

        @pl.when(z < 6)
        def _():
            for s in range(2):
                top_up[s, 0] = dot(map_b[...], gate_maps[s]).astype(BF16)

        send_cross7[0].wait_recv()
        send_cross6[0].wait_recv()
        five = (cross_b[...] + dot(cross_a[...].astype(BF16), map_c[...])).astype(BF16)
        for s in range(2):
            cross_sum[s] += dot(five, down[s, 0])

        @pl.when(z < 6)
        def _():
            send_part8[1][0].wait_recv()
            for s in range(2):
                cross_sum[s] += dot(parts8[1], top_up[s, 0])

            @pl.when(z != 4)
            def _():
                send_cross8_first[0].wait_recv()

            send_part8[0][0].wait_recv()
            for s in range(2):
                four = cross_sum[s] + dot(cross_c[...], gate_maps[s]) + dot(parts8[0], top_up[s, 0])
                outgoing[s] = four.astype(BF16)
                start(send_above4[3 * s : 3 * s + 3])

        @pl.when(both(is_late_hub, z != 10))
        def _():
            lower_hub()

        @pl.when(both(z > 6, z % 4 != 2))
        def _():
            send_above7[0].wait_recv()

        @pl.when(z >= 6)
        def _():
            for s in range(2):
                outgoing[s] = (cross_sum[s] + dot(above[...], gate_maps[s])).astype(BF16)
                start(send_above4[3 * s : 3 * s + 3])

    @pl.when(is_p3)
    def _():
        send_down4[0].wait_recv()
        head_map[...] = dot(map_d[...], down[0, 0]).astype(BF16)

        @pl.when(core == 0)
        def _():
            send_head_map_0.start()

        @pl.when(core == 1)
        def _():
            send_head_map.start()

        send_cross4[0].wait_recv()
        cross_four = cross_a[...].astype(BF16)
        cross_sum[0] += dot(cross_four, down[0, 0])

        @pl.when(core == 0)
        def _():
            send_head_base_0.start()

        @pl.when(core == 1)
        def _():
            send_head_base.start()

        cross_sum[1] += dot(cross_four, down[1, 0])
        down[1, 0] = dot(map_d[...], down[1, 0]).astype(BF16)

        @pl.when(core == 0)
        def _():
            send_map_0.start()
            send_base_0.start()

    is_server = both(y == 0, core == 1)

    @pl.when(is_server)
    def _():
        send_map_0.wait_recv()
        send_base_0.wait_recv()

        @pl.when(is_gate)
        def _():
            above_0[...] = outgoing[0]

        @pl.when(jnp.logical_not(is_gate))
        def _():
            send_above4[0].wait_recv()

        out_0[...] = (base_0[...] + dot(above_0[...], map_0[...])).astype(BF16)
        start(send_above2_0)

    @pl.when(both(is_p3, core == 1))
    def _():
        send_above4[3].wait_recv()
        outgoing[1] = (cross_sum[1] + dot(above[...], down[1, 0])).astype(BF16)
        start(send_above2_right)
        leaf_above[...] = outgoing[1]

    @pl.when(both(is_head, core == 1))
    def _():
        send_head_map.wait_recv()
        send_head_base.wait_recv()

        @pl.when(is_gate)
        def _():
            above[...] = outgoing[1]

        @pl.when(jnp.logical_not(is_gate))
        def _():
            send_above4[3].wait_recv()

        head_out[...] = (head_base[...] + dot(above[...], head_map[...])).astype(BF16)
        start(send_above2)
        leaf_above[...] = head_out[...]

    @pl.when(both(is_even, jnp.logical_not(is_p8)))
    def _():
        send_cross1[0].wait_recv()
        send_down1[0].wait_recv()

    @pl.when(jnp.logical_not(is_p2))
    def _():
        send_cross2[0].wait_recv()
        send_down2[0].wait_recv()

    zero = dot(leaf_cross2[...].astype(BF16), leaf_map1[...]) + leaf_cross1[...]
    zero = jnp.where(leaf_keep, zero, 0.0).astype(BF16)
    product[...] += dot(zero, leaf_out[...])
    map_keep = lax.broadcasted_iota(jnp.int32, (width, leaf_width), 1) < leaf_rank
    leaf_map1[...] = jnp.where(map_keep, dot(leaf_map2[...], leaf_map1[...]), 0.0).astype(BF16)
    leaf_map2[...] = dot(leaf_map1[...], leaf_out[...]).astype(BF16)

    @pl.when(jnp.logical_not(is_server))
    def _():
        send_above2[0].wait_recv()

    product[...] += dot(leaf_above[...], leaf_map2[...])

    sent(is_server, send_above2_0)
    sent(both(is_head, core == 1), send_above2)
    sent(both(is_p3, core == 1), [send_head_map, send_head_base, *send_above2_right])
    sent(both(is_p3, core == 0), [send_head_map_0, send_head_base_0, send_map_0, send_base_0])
    sent(is_gate, send_above4)
    sent(is_late_hub, send_above7[:1])
    sent(is_far_hub, send_above7[1:])


def on_device(rhs, diag_blocks, leaf_in, leaf_out, up_maps, cross_maps, down_maps, node_rank):
    rows, leaf = rhs.shape
    width, leaf_width = up_maps.shape[-1], leaf_in.shape[1]
    operands = (rhs, diag_blocks, leaf_in, leaf_out, up_maps, cross_maps, down_maps)

    def vector(*lead, kind=BF16, columns=width):
        return pltpu.VMEM((*lead, rows, columns), kind)

    full_map = pltpu.VMEM((width, width), BF16)
    return pl.pallas_call(
        kernel,
        out_shape=pltpu.VMEM((rows, leaf), F32),
        in_specs=[pl.BlockSpec(memory_space=pl.ANY)] * 8,
        out_specs=pl.BlockSpec(memory_space=pltpu.VMEM),
        scratch_shapes=[pltpu.VMEM(each.shape, each.dtype) for each in operands]
        + [
            pltpu.SMEM(node_rank.shape, node_rank.dtype),
            vector(columns=leaf_width),
            vector(),
            vector(columns=2 * width),
            vector(2, kind=F32),
            vector(),
            vector(2),
            full_map,
            full_map,
            full_map,
            full_map,
            full_map,
            full_map,
            pltpu.VMEM(up_maps.shape, BF16),
            pltpu.VMEM(cross_maps.shape, BF16),
            vector(columns=2 * width),
            vector(),
            vector(2),
            vector(),
            vector(),
            pltpu.VMEM((2, width, width), BF16),
            full_map,
            vector(kind=F32),
            vector(),
            full_map,
            vector(kind=F32),
            vector(),
            vector(),
            full_map,
            pltpu.VMEM((width, leaf_width), BF16),
            vector(kind=F32),
            vector(kind=F32),
            vector(),
            vector(kind=F32),
            vector(kind=F32, columns=leaf_width),
            vector(),
            vector(),
            vector(2),
            vector(4),
            vector(2),
            pltpu.SemaphoreType.DMA((8,)),
            pltpu.SemaphoreType.DMA((16,)),
            pltpu.SemaphoreType.DMA((28,)),
            pltpu.SemaphoreType.REGULAR,
            pltpu.SemaphoreType.REGULAR,
        ],
        compiler_params=pltpu.CompilerParams(
            collective_id=0, has_side_effects=True, vmem_limit_bytes=60 * 2**20
        ),
    )(*operands, node_rank)


def solution(mesh):
    assert mesh.shape["tx"] == N_Z * N_CORE and mesh.shape["ty"] == N_X * N_Y
    in_specs = (
        P(None, ("tx", "ty")),
        P(("tx", "ty"), None),
        P(("tx", "ty"), None),
        P(("tx", "ty"), None),
        P(None, ("tx", "ty"), None, None),
        P(None, ("tx", "ty"), None, None),
        P(None, ("tx", "ty"), None, None),
        P(("tx", "ty"), None),
    )
    return jax.shard_map(
        on_device, mesh=mesh, in_specs=in_specs, out_specs=P(None, ("tx", "ty")), check_vma=False
    )
```

```python
import functools

import jax
import jax.numpy as jnp
from jax import lax
from jax.experimental import pallas as pl
from jax.experimental.pallas import tpu as pltpu
from jax.sharding import PartitionSpec as P

MESH = pl.DeviceIdType.MESH
F32 = jnp.float32
BF16 = jnp.bfloat16
N_Z, N_CORE, N_X, N_Y = 16, 2, 4, 4


def kernel(
    rhs_hbm,
    diag_hbm,
    in_hbm,
    out_hbm,
    up_hbm,
    cross_hbm,
    down_hbm,
    rank_hbm,
    product,
    rhs,
    diag,
    leaf_in,
    leaf_out,
    up,
    cross,
    down,
    rank,
    leaf_coef,
    coef,
    child,
    cross_sum,
    path_coef,
    outgoing,
    map_a,
    map_b,
    map_c,
    map_d,
    map_e,
    map_f,
    top_up,
    top_cross,
    top_child,
    top_coef,
    top_sum,
    top_out,
    far_out,
    gate_maps,
    head_map,
    head_base,
    head_out,
    map_0,
    base_0,
    above_0,
    out_0,
    leaf_map2,
    leaf_map1,
    cross_a,
    cross_b,
    cross_c,
    leaf_cross2,
    leaf_cross1,
    above,
    leaf_above,
    parts4,
    parts6,
    parts8,
    load_sem,
    send_sem,
    recv_sem,
    go_sem,
    late_sem,
):
    rows, width = coef.shape
    leaf_width = leaf_coef.shape[1]
    loads = [
        pltpu.make_async_copy(source, target, load_sem.at[n])
        for n, (source, target) in enumerate(
            (
                (rhs_hbm, rhs),
                (in_hbm, leaf_in),
                (rank_hbm, rank),
                (up_hbm, up),
                (cross_hbm, cross),
                (down_hbm, down),
                (diag_hbm, diag),
                (out_hbm, leaf_out),
            )
        )
    ]
    load_rhs, load_in, load_rank, load_up, load_cross, load_down, load_diag, load_out = loads
    quarter = in_hbm.shape[0] // 4
    for n in range(4):
        part = pl.ds(n * quarter, quarter)
        pltpu.make_async_copy(in_hbm.at[part], leaf_in.at[part], load_sem.at[1]).start()
    load_rhs.start()
    load_rank.start()

    tx, ty = lax.axis_index("tx"), lax.axis_index("ty")
    z, core = tx // N_CORE, tx % N_CORE
    x, y = ty // N_Y, ty % N_Y

    def at(z, core, x, y):
        return (z * N_CORE + core, x * N_Y + y)

    both = jnp.logical_and
    on_line = ty == 0
    on_top = both(on_line, core == 0)
    is_p1 = y % 2 == 1
    is_p2 = y == 2
    is_p3 = both(y == 0, x % 2 == 1)
    is_p4 = both(y == 0, x == 2)
    is_gate = both(on_line, core == 1)
    is_p6 = both(on_top, z % 2 == 1)
    is_p7 = both(on_top, z % 4 == 2)
    is_p8 = both(on_top, z % 8 == 4)
    is_p9 = both(on_top, z == 8)
    is_even = y % 2 == 0
    is_head = both(y == 0, x % 2 == 0)
    is_hub = both(is_gate, z % 4 == 2)
    is_late_hub = both(is_hub, z > 2)
    is_far_hub = both(is_hub, z >= 8)
    is_left_center = both(is_gate, z == 4)
    is_right_center = both(is_gate, z == 12)
    is_left_p8 = both(on_top, z == 4)
    is_right_p8 = both(on_top, z == 12)

    x_odd = x // 2 * 2 + 1
    z_odd, z_seven, z_eight = z // 2 * 2 + 1, z // 4 * 4 + 2, z // 8 * 8 + 4
    leaf_peer = at(z, core, x, y + 1)
    left_leaf = at(z, core, x, y - 1)
    column = [at(z, core, x, k) for k in range(N_Y)]
    my_p3 = at(z, core, x_odd, 0)
    p3s = [at(z, core, 1, 0), at(z, core, 3, 0)]
    p4 = at(z, core, 2, 0)
    gate = at(z, 1, 0, 0)
    p3s_of_gate = [at(z, c, k, 0) for c in range(N_CORE) for k in (1, 3)]
    p4s_of_gate = [at(z, c, 2, 0) for c in range(N_CORE)]
    p6, p7, p8 = at(z_odd, 0, 0, 0), at(z_seven, 0, 0, 0), at(z_eight, 0, 0, 0)
    gates_of_p6 = [at(z_odd - 1, 1, 0, 0), at(z_odd, 1, 0, 0)]
    gates_of_p7 = [at(z_seven - 2 + k, 1, 0, 0) for k in range(4)]
    hub, center = at(z_seven, 1, 0, 0), at(z_eight, 1, 0, 0)
    hubs_of_center = [at(z_eight - 2, 1, 0, 0), at(z_eight + 2, 1, 0, 0)]
    first_gates = [at(k, 1, 0, 0) for k in range(6)]
    second_hub, third_hub, fourth_hub = at(6, 1, 0, 0), at(10, 1, 0, 0), at(14, 1, 0, 0)

    barrier = pltpu.get_barrier_semaphore()

    def greet(condition, devices):
        @pl.when(condition)
        def _():
            for device in devices:
                pl.semaphore_signal(barrier, inc=1, device_id=device, device_id_type=MESH)

    def collector(z, core, x):
        return at(z, core, x, 1)

    x_even = x % 2 == 0
    next_p3 = collector(z, core, x_odd)
    greet(is_p1, [left_leaf])
    greet(y == 1, [column[3]])
    on_one = core == 1
    greet(core == 0, [collector(z, 1, x)])
    greet(both(y == 3, on_one), [collector(z, core, x)])
    greet(is_p2, [column[1], column[3]])
    greet(both(both(is_p2, x % 2 == 1), on_one), [column[1]])
    greet(y == 0, [column[1], column[3]])
    greet(both(is_head, on_one), [next_p3, collector(z, 0, x_odd)])
    greet(is_p3, [at(z, core, x - 1, 3), collector(z, core, 2)])
    greet(both(is_p3, on_one), [collector(z, 1, 0), collector(z, 0, x)])
    greet(is_p4, [collector(z, core, 1), collector(z, core, 3)])
    greet(both(is_p4, on_one), [collector(z, 1, 0)])
    greet(is_gate, [collector(z, 0, 1), collector(z, 0, 3), collector(z, 1, 2)] + [collector(z_odd, 0, 0), collector(z_seven, 0, 0)])
    greet(both(is_gate, z % 4 == 0), [collector(z + 1, 1, 0)])
    greet(both(is_gate, both(z < 6, z != 4)), [collector(4, 0, 0), collector(8, 0, 0), collector(4, 1, 0)])
    greet(both(both(is_gate, z > 6), z % 4 != 2), [collector(z_seven, 1, 0)])
    greet(is_hub, [collector(z_seven - 2 + k, 1, 0) for k in (0, 1, 3)])
    greet(is_late_hub, [collector(z_eight, 0, 0), collector(z_eight, 1, 0)])
    greet(both(is_late_hub, z < 12), [collector(8, 0, 0)])
    greet(both(is_late_hub, z > 12), [collector(8, 1, 0)])
    greet(is_p9, [collector(8, 1, 0)])
    greet(
        both(is_gate, z % 8 == 4),
        [collector(z_eight - 2, 1, 0), collector(z_eight + 2, 1, 0), collector(z, 0, 0)],
    )
    greet(is_left_center, [collector(8, 0, 0)])
    greet(is_p6, [collector(z_odd - 1, 1, 0), collector(z_odd, 1, 0)])
    greet(is_p7, [collector(z, 1, 0)])
    greet(is_right_p8, [collector(z, 1, 0)])
    sizes = (
        (is_even, 1),
        (y == 3, 3),
        (both(y == 3, x_even), 1),
        (y == 1, 2),
        (both(y == 1, on_one), 4),
        (both(both(y == 1, x_even), on_one), 1),
        (both(y == 1, x % 2 == 1), 4),
        (both(y == 1, x == 2), 2 + core),
        (both(ty == 1, core == 1), 4),
        (both(both(ty == 1, core == 1), z % 4 != 2), 1),
        (both(both(ty == 1, core == 1), z % 4 == 1), 1),
        (both(both(ty == 1, core == 1), z % 4 == 2), 2),
        (both(both(ty == 1, core == 1), z == 6), 1),
        (both(both(ty == 1, core == 1), both(z % 4 == 2, z > 6)), 3),
        (both(both(ty == 1, core == 1), z == 4), 6),
        (both(both(ty == 1, core == 1), z == 12), 3),
        (both(both(ty == 1, core == 1), z == 8), 2),
        (both(both(ty == 1, core == 0), z % 2 == 1), 2),
        (both(both(ty == 1, core == 0), z % 4 == 2), 4),
        (both(both(ty == 1, core == 0), z == 4), 7),
        (both(both(ty == 1, core == 0), z == 12), 3),
        (both(both(ty == 1, core == 0), z == 8), 8),
    )
    greeted = sum(condition.astype(jnp.int32) * size for condition, size in sizes)
    for load in loads[3:]:
        load.start()

    def remote(source, target, send, recv, device):
        return pltpu.make_async_remote_copy(
            src_ref=source,
            dst_ref=target,
            send_sem=send_sem.at[send],
            recv_sem=recv_sem.at[recv],
            device_id=device,
            device_id_type=MESH,
        )

    left_part, right_part = pl.ds(0, width), pl.ds(width, width)
    narrow = pl.ds(0, leaf_width)

    leaf_up = remote(leaf_coef, child.at[:, narrow], 0, 0, leaf_peer)
    side = jnp.where(
        is_p1,
        y // 2,
        jnp.where(is_p2, x % 2, jnp.where(is_p3, x // 2, jnp.where(is_p4, core, z % 2))),
    )
    steps = ((is_p1, column[2]), (is_p2, my_p3), (is_p3, p4), (is_p4, gate), (is_gate, p6))
    parent = tuple(sum(condition.astype(jnp.int32) * device[k] for condition, device in steps) for k in range(2))
    up_left = remote(coef, child.at[:, left_part], 1, 0, parent)
    up_right = remote(coef, child.at[:, right_part], 1, 1, parent)
    send_cross1 = [remote(cross_sum.at[0, :, narrow], leaf_cross1, 2, 2, left_leaf)]
    send_down1 = [remote(down.at[0, 0, :, narrow], leaf_map1, 3, 3, left_leaf)]
    sides2 = ((0, 0), (1, 0), (3, 1))
    send_cross2 = [remote(cross_sum.at[s], leaf_cross2, 2 + n, 4, column[k]) for n, (k, s) in enumerate(sides2)]
    send_down2 = [remote(down.at[s, 0], leaf_map2, 5 + n, 5, column[k]) for n, (k, s) in enumerate(sides2)]
    send_cross4 = [remote(cross_sum.at[s], cross_a, 2 + s, 11, p3s[s]) for s in range(2)]
    send_up4 = [remote(up.at[s, 0], map_a, 7 + s, 7, p3s[s]) for s in range(2)]
    send_part4 = [remote(path_coef, parts4.at[k], 9, (19, 0)[k], gate) for k in range(2)]
    send_down4 = [remote(down.at[s, 0], map_d, 5 + s, 10, p3s[s]) for s in range(2)]
    send_cross6 = [remote(cross_sum.at[s], cross_b, 2 + s, 12, gates_of_p6[s]) for s in range(2)]
    send_up6 = [remote(up.at[s, 0], map_a, 4 + s, 7, gates_of_p6[s]) for s in range(2)]
    send_down6 = [remote(down.at[s, 0], map_c, 6 + s, 9, gates_of_p6[s]) for s in range(2)]
    halves = [pl.ds(k * (width // 2), width // 2) for k in range(2)]
    send_down6_half = [remote(down.at[0, 0, half], map_c.at[half], (6, 8)[k], 9, gates_of_p6[0]) for k, half in enumerate(halves)]
    send_cross7 = [remote(cross_sum.at[k // 2], cross_a, 2 + k, 11, gates_of_p7[k]) for k in range(4)]
    send_down7 = [remote(down.at[k // 2, 0], map_d, 6 + k, 10, gates_of_p7[k]) for k in range(4)]
    pass_down7 = remote(map_d, map_d, 3, 10, at(z - 1, 1, 0, 0))
    send_cross8 = [remote(top_sum.at[s], cross_c, 7 + s, 18, hubs_of_center[s]) for s in range(2)]
    send_cross8_first = [remote(top_sum.at[0], cross_c, 9 + k, 18, first_gates[k]) for k in range(4)]
    send_cross8_first += [remote(top_sum.at[1], cross_c, 13, 18, first_gates[5])]
    send_top_up7 = remote(up, top_up, 6, 20, hub)
    send_top_up8 = remote(up, top_up, 4, 20, center)
    send_top_cross = remote(cross, top_cross, 8, 14, center)
    send_up8 = [remote(up.at[s, 0], map_e, 4 + s, 21, hubs_of_center[s]) for s in range(2)]
    send_down8 = [remote(down.at[s, 0], map_b, 6 + s, 8, hubs_of_center[s]) for s in range(2)]
    send_down8_first = [remote(down.at[k // 4, 0], map_b, 8 + k, 8, first_gates[k]) for k in range(6)]
    pass_down8 = remote(map_b, map_b, 4, 8, at(z - 1, 1, 0, 0))
    send_cross9 = [remote(cross.at[0, 0], map_f, 2, 22, third_hub), remote(cross.at[0, 0], map_f, 3, 22, fourth_hub)]
    send_cross9 += [remote(cross.at[1, 0], map_f, 4, 22, at(4, 1, 0, 0))]
    send_part6 = [remote(path_coef, parts6.at[k], 2, (14, 15, 16, 16)[k], hub) for k in range(4)]
    send_child7 = remote(top_child, child, 3, 0, p7)
    send_coef7 = [remote(top_coef, top_child.at[:, part], 4, 15 + k, center) for k, part in enumerate((left_part, right_part))]
    send_part8 = [
        [remote(far_out, parts8.at[k], 5 + n, (17, 13)[k], device) for n, device in enumerate((*first_gates, second_hub))]
        for k in range(2)
    ]
    send_part8_right = [remote(far_out, parts8.at[0], 5 + k, 17, (third_hub, fourth_hub)[k]) for k in range(2)]
    send_above7 = [remote(top_out, above, n, 13, gates_of_p7[k]) for n, k in enumerate((3, 0, 1))]
    servers = [at(z, 1, 1, 0), at(z, 1, 2, 0), at(z, 1, 3, 0)]
    send_above4 = [remote(outgoing.at[0], above_0, 3 + n, 27, device) for n, device in enumerate(servers)]
    send_above4 += [remote(outgoing.at[1], above, 6 + n, 13, device) for n, device in enumerate(servers)]
    head = at(z, 1, x - 1, 0)
    send_head_map = remote(head_map, head_map, 0, 23, head)
    send_head_base = remote(cross_sum.at[0], head_base, 1, 24, head)
    send_head_map_0 = remote(head_map, map_0, 0, 25, head)
    send_head_base_0 = remote(cross_sum.at[0], base_0, 1, 26, head)
    send_map_0 = remote(down.at[1, 0], map_0, 2, 25, at(z, 1, x, 0))
    send_base_0 = remote(cross_sum.at[1], base_0, 3, 26, at(z, 1, x, 0))
    send_above2_0 = [remote(out_0, leaf_above, (13, 9, 14, 15)[n], 6, at(z, 0, x, k)) for n, k in enumerate((1, 3, 2, 0))]
    send_above2 = [remote(head_out, leaf_above, 9 + k, 6, column[k]) for k in (1, 3, 2)]
    send_above2_right = [remote(outgoing.at[1], leaf_above, 1 + k, 6, column[k]) for k in (1, 3, 2)]

    def start(copies):
        for copy in copies:
            copy.start()

    def dot(a, b):
        return jnp.dot(a, b, preferred_element_type=F32)

    load_rhs.wait()
    load_in.wait()
    load_rank.wait()
    leaf_rank, node_rank = rank[0, 0], rank[0, 1]
    leaf_keep = lax.broadcasted_iota(jnp.int32, (rows, leaf_width), 1) < leaf_rank
    node_keep = lax.broadcasted_iota(jnp.int32, (rows, width), 1) < node_rank
    leaf_coef[...] = jnp.where(leaf_keep, dot(rhs[...], leaf_in[...]), 0.0).astype(BF16)

    pl.semaphore_wait(barrier, greeted)

    @pl.when(is_p1)
    def _():
        pl.semaphore_signal(go_sem, inc=1, device_id=left_leaf, device_id_type=MESH)

    @pl.when(both(both(ty == 1, core == 1), z == 8))
    def _():
        pl.semaphore_signal(late_sem, inc=1, device_id=at(8, 0, 0, 0), device_id_type=MESH)

    def mask_up():
        keep = lax.broadcasted_iota(jnp.int32, (width, width), 1) < node_rank
        for s in range(2):
            up[s, 0] = jnp.where(keep, up[s, 0], jnp.zeros((width, width), BF16))

    def mask_down():
        keep = lax.broadcasted_iota(jnp.int32, (width, width), 0) < node_rank
        for s in range(2):
            down[s, 0] = jnp.where(keep, down[s, 0], jnp.zeros((width, width), BF16))

    def send_up(summed, waits=False):
        coef[...] = jnp.where(node_keep, summed, 0.0).astype(BF16)
        if waits:
            pl.semaphore_wait(go_sem, 1)

        @pl.when(side == 0)
        def _():
            up_left.start()

        @pl.when(side == 1)
        def _():
            up_right.start()

    def cross_terms():
        cross_sum[0] = dot(child[:, right_part], cross[0, 0])
        cross_sum[1] = dot(child[:, left_part], cross[1, 0])

    @pl.when(is_even)
    def _():
        leaf_up.start()

    @pl.when(on_line)
    def _():
        pl.semaphore_wait(go_sem, 1)

    @pl.when(is_p1)
    def _():
        load_up.wait()
        summed = dot(leaf_coef[...], up[1, 0, narrow, :])
        leaf_up.wait_recv()
        send_up(summed + dot(child[:, narrow], up[0, 0, narrow, :]))
        load_cross.wait()
        cross_sum[0, :, narrow] = dot(leaf_coef[...], cross[0, 0, narrow, narrow])
        leaf_cross1[...] = dot(child[:, narrow], cross[1, 0, narrow, narrow])
        start(send_cross1)
        load_down.wait()
        mask_down()
        start(send_down1)
        leaf_map1[...] = down[1, 0, :, narrow]

    def lift(waits=True):
        up_left.wait_recv()
        summed = dot(child[:, left_part], up[0, 0])
        up_right.wait_recv()
        send_up(summed + dot(child[:, right_part], up[1, 0]), waits)

    @pl.when(is_p2)
    def _():
        load_up.wait()
        lift()
        load_cross.wait()
        cross_terms()
        start(send_cross2)
        leaf_cross2[...] = cross_sum[1]
        load_down.wait()
        mask_down()
        start(send_down2)
        leaf_map2[...] = down[1, 0]

    @pl.when(is_p3)
    def _():
        load_up.wait()
        lift()

        @pl.when(core == 0)
        def _():
            send_up4[0].wait_recv()
            path_coef[...] = dot(coef[...], map_a[...]).astype(BF16)
            for k in range(2):

                @pl.when(x // 2 == k)
                def _():
                    send_part4[k].start()

        load_cross.wait()
        cross_terms()
        load_down.wait()
        mask_down()

    @pl.when(is_p4)
    def _():
        load_up.wait()
        mask_up()
        pl.semaphore_wait(go_sem, 1)

        @pl.when(core == 0)
        def _():
            start(send_up4)
            load_down.wait()
            mask_down()
            start(send_down4)
            up_left.wait_recv()
            up_right.wait_recv()

        @pl.when(core == 1)
        def _():
            lift(waits=False)

        load_cross.wait()
        cross_terms()
        start(send_cross4)

        @pl.when(core == 1)
        def _():
            load_down.wait()
            mask_down()
            start(send_down4)

    @pl.when(is_gate)
    def _():
        load_up.wait()
        load_cross.wait()
        load_down.wait()
        mask_down()

        @pl.when(z % 4 == 1)
        def _():
            send_down7[0].wait_recv()
            pass_down7.start()

        map_keep = lax.broadcasted_iota(jnp.int32, (width, width), 1) < node_rank
        send_up6[0].wait_recv()
        for s in range(2):
            ahead = dot(jnp.where(map_keep, up[s, 0], jnp.zeros((width, width), BF16)), map_a[...])
            gate_maps[s] = ahead.astype(BF16)
        for copy in send_part4:
            copy.wait_recv()
        child[:, left_part] = (parts4[0].astype(F32) + parts4[1].astype(F32)).astype(BF16)
        up_right.wait_recv()
        six = dot(child[:, left_part], gate_maps[0]) + dot(child[:, right_part], gate_maps[1])
        path_coef[...] = six.astype(BF16)
        for k in (0, 1, 3):

            @pl.when(z % 4 == k)
            def _():
                send_part6[k].start()

        send_up(dot(child[:, left_part], up[0, 0]) + dot(child[:, right_part], up[1, 0]))

        @pl.when(is_hub)
        def _():
            parts6[2] = path_coef[...]
            send_top_up7.wait_recv()

            @pl.when(is_far_hub)
            def _():
                send_up8[0].wait_recv()
                send_cross9[0].wait_recv()
                map_e[...] = dot(map_e[...], map_f[...]).astype(BF16)

                @pl.when(z == 10)
                def _():
                    for k in range(2):
                        top_cross[k, 0] = dot(top_up[k, 0], map_e[...]).astype(BF16)

            for k in (0, 1, 3):
                send_part6[k].wait_recv()
            for k, part in enumerate((left_part, right_part)):
                six = parts6[2 * k].astype(F32) + parts6[2 * k + 1].astype(F32)
                top_child[:, part] = six.astype(BF16)

            @pl.when(z == 10)
            def _():
                far = dot(top_child[:, left_part], top_cross[0, 0]) + dot(top_child[:, right_part], top_cross[1, 0])
                far_out[...] = far.astype(BF16)
                start(send_part8[0])

            seven = dot(top_child[:, left_part], top_up[0, 0]) + dot(top_child[:, right_part], top_up[1, 0])
            top_coef[...] = seven.astype(BF16)
            for k in range(2):

                @pl.when(z // 4 % 2 == k)
                def _():
                    send_coef7[k].start()

            @pl.when(z == 14)
            def _():
                far_out[...] = dot(top_coef[...], map_e[...]).astype(BF16)
                start(send_part8[1])

            send_child7.start()

        def center_cross_terms():
            send_top_cross.wait_recv()
            top_sum[0] = dot(top_child[:, right_part], top_cross[0, 0]).astype(BF16)
            top_sum[1] = dot(top_child[:, left_part], top_cross[1, 0]).astype(BF16)

        @pl.when(is_left_center)
        def _():
            send_top_up8.wait_recv()
            send_coef7[0].wait_recv()
            send_coef7[1].wait_recv()
            center_cross_terms()
            start(send_cross8_first)
            send_cross8[1].start()
            cross_c[...] = top_sum[1]
            eight = dot(top_child[:, left_part], top_up[0, 0]) + dot(top_child[:, right_part], top_up[1, 0])
            top_coef[...] = eight.astype(BF16)
            send_cross9[2].wait_recv()
            far_out[...] = dot(top_coef[...], map_f[...]).astype(BF16)
            start(send_part8_right)

        @pl.when(is_right_center)
        def _():
            pl.semaphore_signal(late_sem, inc=1, device_id=p8, device_id_type=MESH)
            send_coef7[1].wait_recv()
            send_coef7[0].wait_recv()
            center_cross_terms()
            start(send_cross8)

        cross_terms()

        @pl.when(z == 1)
        def _():
            send_down8_first[0].wait_recv()
            pass_down8.start()

    @pl.when(is_p6)
    def _():
        load_up.wait()
        mask_up()
        start(send_up6)
        load_cross.wait()
        load_down.wait()
        mask_down()
        for copy in send_up6:
            copy.wait_send()
        send_down6[1].start()

        @pl.when(z % 4 == 1)
        def _():
            send_down6[0].start()

        @pl.when(both(z % 4 == 3, z != 7))
        def _():
            send_down6_half[0].start()

        up_right.wait_recv()

        @pl.when(both(z % 4 == 3, z != 7))
        def _():
            send_down6_half[1].start()

        @pl.when(z == 7)
        def _():
            send_down6[0].start()

        up_left.wait_recv()
        cross_terms()
        start(send_cross6)

    @pl.when(is_p7)
    def _():
        load_up.wait()
        mask_up()
        send_top_up7.start()
        load_down.wait()
        mask_down()
        start(send_down7[1:])
        load_cross.wait()
        send_child7.wait_recv()
        cross_terms()
        start(send_cross7)

    @pl.when(is_p8)
    def _():
        load_up.wait()
        mask_up()
        load_cross.wait()
        send_top_cross.start()
        load_down.wait()
        mask_down()

        @pl.when(is_left_p8)
        def _():
            send_down8[1].start()
            send_down8_first[1].start()
            start(send_down8_first[4:])

        @pl.when(is_right_p8)
        def _():
            send_up8[1].start()

        send_cross1[0].wait_recv()

        @pl.when(is_right_p8)
        def _():
            send_down1[0].wait_recv()
            send_up8[0].start()
            pl.semaphore_wait(late_sem, 1)
            start(send_down8)

        @pl.when(is_left_p8)
        def _():
            send_top_up8.start()
            send_down1[0].wait_recv()
            for k, after in ((1, 3), (3, 2)):
                send_down8_first[k].wait_send()
                send_down8_first[after].start()

    @pl.when(both(on_top, z % 8 == 0))
    def _():
        load_up.wait()
        load_cross.wait()
        load_down.wait()

    @pl.when(is_p9)
    def _():
        send_cross9[0].start()
        pl.semaphore_wait(late_sem, 1)
        send_cross9[1].start()
        send_cross9[2].start()

    load_diag.wait()
    product[...] = dot(rhs[...], diag[...])
    load_out.wait()

    def sent(condition, copies):
        @pl.when(condition)
        def _():
            for copy in copies:
                copy.wait_send()

    sent(is_even, [leaf_up])
    sent(is_p1, [up_left, *send_cross1, *send_down1])
    sent(is_p2, [up_left, *send_cross2, *send_down2])
    sent(both(is_p3, core == 0), [send_part4[0]])
    sent(is_p3, [up_left])
    sent(both(is_p4, core == 0), send_up4)
    sent(both(is_p4, core == 1), [up_left])
    sent(is_p4, [*send_cross4, *send_down4])
    sent(is_gate, [up_left])
    sent(both(is_gate, z % 4 != 2), [send_part6[0]])
    sent(is_hub, [send_coef7[0], send_child7])
    sent(is_far_hub, send_part8[0])
    sent(is_left_center, [*send_cross8_first, send_cross8[1], *send_part8_right])
    sent(is_right_center, send_cross8)
    sent(is_p6, [send_down6[1], *send_cross6])
    sent(both(is_p6, both(z % 4 == 3, z != 7)), send_down6_half)
    sent(both(is_p6, jnp.logical_not(both(z % 4 == 3, z != 7))), [send_down6[0]])
    sent(is_p7, [send_top_up7, *send_down7[1:], *send_cross7])
    sent(is_p8, [send_top_cross, send_down8[1]])
    sent(is_left_p8, [send_top_up8, send_down8_first[2], *send_down8_first[4:]])
    sent(is_right_p8, [*send_up8, send_down8[0]])
    sent(is_p9, send_cross9)

    def lower_hub():
        send_down8[0].wait_recv()
        send_cross8[0].wait_recv()
        send_part8[0][0].wait_recv()

        @pl.when(z == 6)
        def _():
            send_part8[1][0].wait_recv()
            crossed = parts8[0].astype(F32) + parts8[1].astype(F32)
            parts8[0] = crossed.astype(BF16)

        top_out[...] = (cross_c[...].astype(F32) + dot(parts8[0], map_b[...])).astype(BF16)
        send_above7[0].start()

        @pl.when(z > 6)
        def _():
            start(send_above7[1:])

        above[...] = top_out[...]

    @pl.when(is_gate)
    def _():
        @pl.when(z == 10)
        def _():
            lower_hub()

        @pl.when(z % 4 != 1)
        def _():
            send_down7[0].wait_recv()

        @pl.when(z % 4 == 1)
        def _():
            pass_down7.wait_send()

        send_down6[0].wait_recv()
        map_d[...] = dot(map_d[...], map_c[...]).astype(BF16)
        for s in range(2):
            gate_maps[s] = dot(map_d[...], down[s, 0]).astype(BF16)

        @pl.when(both(z < 6, z != 1))
        def _():
            send_down8_first[0].wait_recv()

        @pl.when(z == 1)
        def _():
            pass_down8.wait_send()

        @pl.when(z < 6)
        def _():
            for s in range(2):
                top_up[s, 0] = dot(map_b[...], gate_maps[s]).astype(BF16)

        send_cross7[0].wait_recv()
        send_cross6[0].wait_recv()
        five = (cross_b[...] + dot(cross_a[...].astype(BF16), map_c[...])).astype(BF16)
        for s in range(2):
            cross_sum[s] += dot(five, down[s, 0])

        @pl.when(z < 6)
        def _():
            send_part8[1][0].wait_recv()
            for s in range(2):
                cross_sum[s] += dot(parts8[1], top_up[s, 0])

            @pl.when(z != 4)
            def _():
                send_cross8_first[0].wait_recv()

            send_part8[0][0].wait_recv()
            for s in range(2):
                four = cross_sum[s] + dot(cross_c[...], gate_maps[s]) + dot(parts8[0], top_up[s, 0])
                outgoing[s] = four.astype(BF16)
                start(send_above4[3 * s : 3 * s + 3])

        @pl.when(both(is_late_hub, z != 10))
        def _():
            lower_hub()

        @pl.when(both(z > 6, z % 4 != 2))
        def _():
            send_above7[0].wait_recv()

        @pl.when(z >= 6)
        def _():
            for s in range(2):
                outgoing[s] = (cross_sum[s] + dot(above[...], gate_maps[s])).astype(BF16)
                start(send_above4[3 * s : 3 * s + 3])

    @pl.when(is_p3)
    def _():
        send_down4[0].wait_recv()
        head_map[...] = dot(map_d[...], down[0, 0]).astype(BF16)

        @pl.when(core == 0)
        def _():
            send_head_map_0.start()

        @pl.when(core == 1)
        def _():
            send_head_map.start()

        send_cross4[0].wait_recv()
        cross_four = cross_a[...].astype(BF16)
        cross_sum[0] += dot(cross_four, down[0, 0])

        @pl.when(core == 0)
        def _():
            send_head_base_0.start()

        @pl.when(core == 1)
        def _():
            send_head_base.start()

        cross_sum[1] += dot(cross_four, down[1, 0])
        down[1, 0] = dot(map_d[...], down[1, 0]).astype(BF16)

        @pl.when(core == 0)
        def _():
            send_map_0.start()
            send_base_0.start()

    is_server = both(y == 0, core == 1)

    @pl.when(is_server)
    def _():
        send_map_0.wait_recv()
        send_base_0.wait_recv()

        @pl.when(is_gate)
        def _():
            above_0[...] = outgoing[0]

        @pl.when(jnp.logical_not(is_gate))
        def _():
            send_above4[0].wait_recv()

        out_0[...] = (base_0[...] + dot(above_0[...], map_0[...])).astype(BF16)
        start(send_above2_0[:3])

    @pl.when(both(is_p3, core == 1))
    def _():
        send_above4[3].wait_recv()
        outgoing[1] = (cross_sum[1] + dot(above[...], down[1, 0])).astype(BF16)
        start(send_above2_right)
        send_above2_0[3].start()
        leaf_above[...] = outgoing[1]

    @pl.when(both(is_head, core == 1))
    def _():
        send_head_map.wait_recv()
        send_head_base.wait_recv()

        @pl.when(is_gate)
        def _():
            above[...] = outgoing[1]

        @pl.when(jnp.logical_not(is_gate))
        def _():
            send_above4[3].wait_recv()

        head_out[...] = (head_base[...] + dot(above[...], head_map[...])).astype(BF16)
        start(send_above2)
        send_above2_0[3].start()
        leaf_above[...] = head_out[...]

    @pl.when(both(is_even, jnp.logical_not(is_p8)))
    def _():
        send_cross1[0].wait_recv()
        send_down1[0].wait_recv()

    @pl.when(jnp.logical_not(is_p2))
    def _():
        send_cross2[0].wait_recv()
        send_down2[0].wait_recv()

    zero = dot(leaf_cross2[...].astype(BF16), leaf_map1[...]) + leaf_cross1[...]
    zero = jnp.where(leaf_keep, zero, 0.0).astype(BF16)
    product[...] += dot(zero, leaf_out[...])
    map_keep = lax.broadcasted_iota(jnp.int32, (width, leaf_width), 1) < leaf_rank
    leaf_map1[...] = jnp.where(map_keep, dot(leaf_map2[...], leaf_map1[...]), 0.0).astype(BF16)
    leaf_map2[...] = dot(leaf_map1[...], leaf_out[...]).astype(BF16)

    @pl.when(jnp.logical_not(is_server))
    def _():
        send_above2[0].wait_recv()

    product[...] += dot(leaf_above[...], leaf_map2[...])

    sent(is_server, send_above2_0)
    sent(both(is_head, core == 1), send_above2)
    sent(both(is_p3, core == 1), [send_head_map, send_head_base, *send_above2_right])
    sent(both(is_p3, core == 0), [send_head_map_0, send_head_base_0, send_map_0, send_base_0])
    sent(is_gate, send_above4)
    sent(is_late_hub, send_above7[:1])
    sent(is_far_hub, send_above7[1:])


def on_device(rhs, diag_blocks, leaf_in, leaf_out, up_maps, cross_maps, down_maps, node_rank):
    rows, leaf = rhs.shape
    width, leaf_width = up_maps.shape[-1], leaf_in.shape[1]
    operands = (rhs, diag_blocks, leaf_in, leaf_out, up_maps, cross_maps, down_maps)

    def vector(*lead, kind=BF16, columns=width):
        return pltpu.VMEM((*lead, rows, columns), kind)

    full_map = pltpu.VMEM((width, width), BF16)
    return pl.pallas_call(
        kernel,
        out_shape=pltpu.VMEM((rows, leaf), F32),
        in_specs=[pl.BlockSpec(memory_space=pl.ANY)] * 8,
        out_specs=pl.BlockSpec(memory_space=pltpu.VMEM),
        scratch_shapes=[pltpu.VMEM(each.shape, each.dtype) for each in operands]
        + [
            pltpu.SMEM(node_rank.shape, node_rank.dtype),
            vector(columns=leaf_width),
            vector(),
            vector(columns=2 * width),
            vector(2, kind=F32),
            vector(),
            vector(2),
            full_map,
            full_map,
            full_map,
            full_map,
            full_map,
            full_map,
            pltpu.VMEM(up_maps.shape, BF16),
            pltpu.VMEM(cross_maps.shape, BF16),
            vector(columns=2 * width),
            vector(),
            vector(2),
            vector(),
            vector(),
            pltpu.VMEM((2, width, width), BF16),
            full_map,
            vector(kind=F32),
            vector(),
            full_map,
            vector(kind=F32),
            vector(),
            vector(),
            full_map,
            pltpu.VMEM((width, leaf_width), BF16),
            vector(kind=F32),
            vector(kind=F32),
            vector(),
            vector(kind=F32),
            vector(kind=F32, columns=leaf_width),
            vector(),
            vector(),
            vector(2),
            vector(4),
            vector(2),
            pltpu.SemaphoreType.DMA((8,)),
            pltpu.SemaphoreType.DMA((16,)),
            pltpu.SemaphoreType.DMA((28,)),
            pltpu.SemaphoreType.REGULAR,
            pltpu.SemaphoreType.REGULAR,
        ],
        compiler_params=pltpu.CompilerParams(
            collective_id=0, has_side_effects=True, vmem_limit_bytes=60 * 2**20
        ),
    )(*operands, node_rank)


def solution(mesh):
    assert mesh.shape["tx"] == N_Z * N_CORE and mesh.shape["ty"] == N_X * N_Y
    in_specs = (
        P(None, ("tx", "ty")),
        P(("tx", "ty"), None),
        P(("tx", "ty"), None),
        P(("tx", "ty"), None),
        P(None, ("tx", "ty"), None, None),
        P(None, ("tx", "ty"), None, None),
        P(None, ("tx", "ty"), None, None),
        P(("tx", "ty"), None),
    )
    return jax.shard_map(
        on_device, mesh=mesh, in_specs=in_specs, out_specs=P(None, ("tx", "ty")), check_vma=False
    )
```

```python
import functools

import jax
import jax.numpy as jnp
from jax import lax
from jax.experimental import pallas as pl
from jax.experimental.pallas import tpu as pltpu
from jax.sharding import PartitionSpec as P

MESH = pl.DeviceIdType.MESH
F32 = jnp.float32
BF16 = jnp.bfloat16
N_Z, N_CORE, N_X, N_Y = 16, 2, 4, 4


def kernel(
    rhs_hbm,
    diag_hbm,
    in_hbm,
    out_hbm,
    up_hbm,
    cross_hbm,
    down_hbm,
    rank_hbm,
    product,
    rhs,
    diag,
    leaf_in,
    leaf_out,
    up,
    cross,
    down,
    rank,
    leaf_coef,
    coef,
    child,
    cross_sum,
    path_coef,
    outgoing,
    map_a,
    map_b,
    map_c,
    map_d,
    map_e,
    map_f,
    top_up,
    top_cross,
    top_child,
    top_coef,
    top_sum,
    top_out,
    far_out,
    gate_maps,
    head_map,
    head_base,
    head_out,
    map_0,
    base_0,
    above_0,
    out_0,
    leaf_map2,
    leaf_map1,
    cross_a,
    cross_b,
    cross_c,
    leaf_cross2,
    leaf_cross1,
    above,
    leaf_above,
    parts4,
    parts6,
    parts8,
    load_sem,
    send_sem,
    recv_sem,
    go_sem,
    late_sem,
):
    rows, width = coef.shape
    leaf_width = leaf_coef.shape[1]
    loads = [
        pltpu.make_async_copy(source, target, load_sem.at[n])
        for n, (source, target) in enumerate(
            (
                (rhs_hbm, rhs),
                (in_hbm, leaf_in),
                (rank_hbm, rank),
                (up_hbm, up),
                (cross_hbm, cross),
                (down_hbm, down),
                (diag_hbm, diag),
                (out_hbm, leaf_out),
            )
        )
    ]
    load_rhs, load_in, load_rank, load_up, load_cross, load_down, load_diag, load_out = loads
    quarter = in_hbm.shape[0] // 4
    for n in range(4):
        part = pl.ds(n * quarter, quarter)
        pltpu.make_async_copy(in_hbm.at[part], leaf_in.at[part], load_sem.at[1]).start()
    load_rhs.start()
    load_rank.start()

    tx, ty = lax.axis_index("tx"), lax.axis_index("ty")
    z, core = tx // N_CORE, tx % N_CORE
    x, y = ty // N_Y, ty % N_Y

    def at(z, core, x, y):
        return (z * N_CORE + core, x * N_Y + y)

    both = jnp.logical_and
    on_line = ty == 0
    on_top = both(on_line, core == 0)
    is_p1 = y % 2 == 1
    is_p2 = y == 2
    is_p3 = both(y == 0, x % 2 == 1)
    is_p4 = both(y == 0, x == 2)
    is_gate = both(on_line, core == 1)
    is_p6 = both(on_top, z % 2 == 1)
    is_p7 = both(on_top, z % 4 == 2)
    is_p8 = both(on_top, z % 8 == 4)
    is_p9 = both(on_top, z == 8)
    is_even = y % 2 == 0
    is_head = both(y == 0, x % 2 == 0)
    is_hub = both(is_gate, z % 4 == 2)
    is_late_hub = both(is_hub, z > 2)
    is_far_hub = both(is_hub, z >= 8)
    is_left_center = both(is_gate, z == 4)
    is_right_center = both(is_gate, z == 12)
    is_left_p8 = both(on_top, z == 4)
    is_right_p8 = both(on_top, z == 12)

    x_odd = x // 2 * 2 + 1
    z_odd, z_seven, z_eight = z // 2 * 2 + 1, z // 4 * 4 + 2, z // 8 * 8 + 4
    leaf_peer = at(z, core, x, y + 1)
    left_leaf = at(z, core, x, y - 1)
    column = [at(z, core, x, k) for k in range(N_Y)]
    my_p3 = at(z, core, x_odd, 0)
    p3s = [at(z, core, 1, 0), at(z, core, 3, 0)]
    p4 = at(z, core, 2, 0)
    gate = at(z, 1, 0, 0)
    p3s_of_gate = [at(z, c, k, 0) for c in range(N_CORE) for k in (1, 3)]
    p4s_of_gate = [at(z, c, 2, 0) for c in range(N_CORE)]
    p6, p7, p8 = at(z_odd, 0, 0, 0), at(z_seven, 0, 0, 0), at(z_eight, 0, 0, 0)
    gates_of_p6 = [at(z_odd - 1, 1, 0, 0), at(z_odd, 1, 0, 0)]
    gates_of_p7 = [at(z_seven - 2 + k, 1, 0, 0) for k in range(4)]
    hub, center = at(z_seven, 1, 0, 0), at(z_eight, 1, 0, 0)
    hubs_of_center = [at(z_eight - 2, 1, 0, 0), at(z_eight + 2, 1, 0, 0)]
    first_gates = [at(k, 1, 0, 0) for k in range(6)]
    second_hub, third_hub, fourth_hub = at(6, 1, 0, 0), at(10, 1, 0, 0), at(14, 1, 0, 0)

    barrier = pltpu.get_barrier_semaphore()

    def greet(condition, devices):
        @pl.when(condition)
        def _():
            for device in devices:
                pl.semaphore_signal(barrier, inc=1, device_id=device, device_id_type=MESH)

    def collector(z, core, x):
        return at(z, core, x, 1)

    x_even = x % 2 == 0
    next_p3 = collector(z, core, x_odd)
    greet(is_p1, [left_leaf])
    greet(y == 1, [column[3]])
    on_one = core == 1
    greet(core == 0, [collector(z, 1, x)])
    greet(both(y == 3, on_one), [collector(z, core, x)])
    greet(is_p2, [column[1], column[3]])
    greet(both(both(is_p2, x % 2 == 1), on_one), [column[1]])
    greet(y == 0, [column[1], column[3]])
    greet(both(is_head, on_one), [next_p3, collector(z, 0, x_odd)])
    greet(is_p3, [at(z, core, x - 1, 3), collector(z, core, 2)])
    greet(both(is_p3, on_one), [collector(z, 1, 0), collector(z, 0, x)])
    greet(is_p4, [collector(z, core, 1), collector(z, core, 3)])
    greet(both(is_p4, on_one), [collector(z, 1, 0)])
    greet(is_gate, [collector(z, 0, 1), collector(z, 0, 3), collector(z, 1, 2)] + [collector(z_odd, 0, 0), collector(z_seven, 0, 0)])
    greet(both(is_gate, z % 4 == 0), [collector(z + 1, 1, 0)])
    greet(both(is_gate, both(z < 6, z != 4)), [collector(4, 0, 0), collector(8, 0, 0), collector(4, 1, 0)])
    greet(both(both(is_gate, z > 6), z % 4 != 2), [collector(z_seven, 1, 0)])
    greet(is_hub, [collector(z_seven - 2 + k, 1, 0) for k in (0, 1, 3)])
    greet(is_late_hub, [collector(z_eight, 0, 0), collector(z_eight, 1, 0)])
    greet(both(is_late_hub, z < 12), [collector(8, 0, 0)])
    greet(both(is_late_hub, z > 12), [collector(8, 1, 0)])
    greet(is_p9, [collector(8, 1, 0)])
    greet(
        both(is_gate, z % 8 == 4),
        [collector(z_eight - 2, 1, 0), collector(z_eight + 2, 1, 0), collector(z, 0, 0)],
    )
    greet(is_left_center, [collector(8, 0, 0)])
    greet(is_p6, [collector(z_odd - 1, 1, 0), collector(z_odd, 1, 0)])
    greet(is_p7, [collector(z, 1, 0)])
    greet(is_right_p8, [collector(z, 1, 0)])
    sizes = (
        (is_even, 1),
        (y == 3, 3),
        (both(y == 3, x_even), 1),
        (y == 1, 2),
        (both(y == 1, on_one), 4),
        (both(both(y == 1, x_even), on_one), 1),
        (both(y == 1, x % 2 == 1), 4),
        (both(y == 1, x == 2), 2 + core),
        (both(ty == 1, core == 1), 4),
        (both(both(ty == 1, core == 1), z % 4 != 2), 1),
        (both(both(ty == 1, core == 1), z % 4 == 1), 1),
        (both(both(ty == 1, core == 1), z % 4 == 2), 2),
        (both(both(ty == 1, core == 1), z == 6), 1),
        (both(both(ty == 1, core == 1), both(z % 4 == 2, z > 6)), 3),
        (both(both(ty == 1, core == 1), z == 4), 6),
        (both(both(ty == 1, core == 1), z == 12), 3),
        (both(both(ty == 1, core == 1), z == 8), 2),
        (both(both(ty == 1, core == 0), z % 2 == 1), 2),
        (both(both(ty == 1, core == 0), z % 4 == 2), 4),
        (both(both(ty == 1, core == 0), z == 4), 7),
        (both(both(ty == 1, core == 0), z == 12), 3),
        (both(both(ty == 1, core == 0), z == 8), 8),
    )
    greeted = sum(condition.astype(jnp.int32) * size for condition, size in sizes)
    for load in loads[3:]:
        load.start()

    def remote(source, target, send, recv, device):
        return pltpu.make_async_remote_copy(
            src_ref=source,
            dst_ref=target,
            send_sem=send_sem.at[send],
            recv_sem=recv_sem.at[recv],
            device_id=device,
            device_id_type=MESH,
        )

    left_part, right_part = pl.ds(0, width), pl.ds(width, width)
    narrow = pl.ds(0, leaf_width)

    leaf_up = remote(leaf_coef, child.at[:, narrow], 0, 0, leaf_peer)
    side = jnp.where(
        is_p1,
        y // 2,
        jnp.where(is_p2, x % 2, jnp.where(is_p3, x // 2, jnp.where(is_p4, core, z % 2))),
    )
    steps = ((is_p1, column[2]), (is_p2, my_p3), (is_p3, p4), (is_p4, gate), (is_gate, p6))
    parent = tuple(sum(condition.astype(jnp.int32) * device[k] for condition, device in steps) for k in range(2))
    up_left = remote(coef, child.at[:, left_part], 1, 0, parent)
    up_right = remote(coef, child.at[:, right_part], 1, 1, parent)
    send_cross1 = [remote(cross_sum.at[0, :, narrow], leaf_cross1, 2, 2, left_leaf)]
    send_down1 = [remote(down.at[0, 0, :, narrow], leaf_map1, 3, 3, left_leaf)]
    sides2 = ((0, 0), (1, 0), (3, 1))
    send_cross2 = [remote(cross_sum.at[s], leaf_cross2, 2 + n, 4, column[k]) for n, (k, s) in enumerate(sides2)]
    send_down2 = [remote(down.at[s, 0], leaf_map2, 5 + n, 5, column[k]) for n, (k, s) in enumerate(sides2)]
    send_cross4 = [remote(cross_sum.at[s], cross_a, 2 + s, 11, p3s[s]) for s in range(2)]
    send_up4 = [remote(up.at[s, 0], map_a, 7 + s, 7, p3s[s]) for s in range(2)]
    send_part4 = [remote(path_coef, parts4.at[k], 9, (19, 0)[k], gate) for k in range(2)]
    send_down4 = [remote(down.at[s, 0], map_d, 5 + s, 10, p3s[s]) for s in range(2)]
    send_cross6 = [remote(cross_sum.at[s], cross_b, 2 + s, 12, gates_of_p6[s]) for s in range(2)]
    send_up6 = [remote(up.at[s, 0], map_a, 4 + s, 7, gates_of_p6[s]) for s in range(2)]
    send_down6 = [remote(down.at[s, 0], map_c, 6 + s, 9, gates_of_p6[s]) for s in range(2)]
    halves = [pl.ds(k * (width // 2), width // 2) for k in range(2)]
    send_down6_half = [remote(down.at[0, 0, half], map_c.at[half], (6, 8)[k], 9, gates_of_p6[0]) for k, half in enumerate(halves)]
    send_cross7 = [remote(cross_sum.at[k // 2], cross_a, 2 + k, 11, gates_of_p7[k]) for k in range(4)]
    send_down7 = [remote(down.at[k // 2, 0], map_d, 6 + k, 10, gates_of_p7[k]) for k in range(4)]
    pass_down7 = remote(map_d, map_d, 3, 10, at(z - 1, 1, 0, 0))
    send_cross8 = [remote(top_sum.at[s], cross_c, 7 + s, 18, hubs_of_center[s]) for s in range(2)]
    send_cross8_first = [remote(top_sum.at[0], cross_c, 9 + k, 18, first_gates[k]) for k in range(4)]
    send_cross8_first += [remote(top_sum.at[1], cross_c, 13, 18, first_gates[5])]
    send_top_up7 = remote(up, top_up, 6, 20, hub)
    send_top_up8 = remote(up, top_up, 4, 20, center)
    send_top_cross = remote(cross, top_cross, 8, 14, center)
    send_up8 = [remote(up.at[s, 0], map_e, 4 + s, 21, hubs_of_center[s]) for s in range(2)]
    send_down8 = [remote(down.at[s, 0], map_b, 6 + s, 8, hubs_of_center[s]) for s in range(2)]
    send_down8_first = [remote(down.at[k // 4, 0], map_b, 8 + k, 8, first_gates[k]) for k in range(6)]
    pass_down8 = remote(map_b, map_b, 4, 8, at(z - 1, 1, 0, 0))
    send_cross9 = [remote(cross.at[0, 0], map_f, 2, 22, third_hub), remote(cross.at[0, 0], map_f, 3, 22, fourth_hub)]
    send_cross9 += [remote(cross.at[1, 0], map_f, 4, 22, at(4, 1, 0, 0))]
    send_part6 = [remote(path_coef, parts6.at[k], 2, (14, 15, 16, 16)[k], hub) for k in range(4)]
    send_child7 = remote(top_child, child, 3, 0, p7)
    send_coef7 = [remote(top_coef, top_child.at[:, part], 4, 15 + k, center) for k, part in enumerate((left_part, right_part))]
    send_part8 = [
        [remote(far_out, parts8.at[k], 5 + n, (17, 13)[k], device) for n, device in enumerate((*first_gates, second_hub))]
        for k in range(2)
    ]
    send_part8_right = [remote(far_out, parts8.at[0], 5 + k, 17, (third_hub, fourth_hub)[k]) for k in range(2)]
    send_above7 = [remote(top_out, above, n, 13, gates_of_p7[k]) for n, k in enumerate((3, 0, 1))]
    servers = [at(z, 1, 1, 0), at(z, 1, 2, 0), at(z, 1, 3, 0)]
    send_above4 = [remote(outgoing.at[0], above_0, 3 + n, 27, device) for n, device in enumerate(servers)]
    send_above4 += [remote(outgoing.at[1], above, 6 + n, 13, device) for n, device in enumerate(servers)]
    head = at(z, 1, x - 1, 0)
    send_head_map = remote(head_map, head_map, 0, 23, head)
    send_head_base = remote(cross_sum.at[0], head_base, 1, 24, head)
    send_head_map_0 = remote(head_map, map_0, 0, 25, head)
    send_head_base_0 = remote(cross_sum.at[0], base_0, 1, 26, head)
    send_map_0 = remote(down.at[1, 0], map_0, 2, 25, at(z, 1, x, 0))
    send_base_0 = remote(cross_sum.at[1], base_0, 3, 26, at(z, 1, x, 0))
    send_above2_0 = [remote(out_0, leaf_above, (13, 9, 14, 15)[n], 6, at(z, 0, x, k)) for n, k in enumerate((1, 3, 2, 0))]
    send_above2 = [remote(head_out, leaf_above, 9 + k, 6, column[k]) for k in (1, 3, 2)]
    send_above2_right = [remote(outgoing.at[1], leaf_above, 1 + k, 6, column[k]) for k in (1, 3, 2)]

    def start(copies):
        for copy in copies:
            copy.start()

    def dot(a, b):
        return jnp.dot(a, b, preferred_element_type=F32)

    load_rhs.wait()
    load_in.wait()
    load_rank.wait()
    leaf_rank, node_rank = rank[0, 0], rank[0, 1]
    leaf_keep = lax.broadcasted_iota(jnp.int32, (rows, leaf_width), 1) < leaf_rank
    node_keep = lax.broadcasted_iota(jnp.int32, (rows, width), 1) < node_rank
    leaf_coef[...] = jnp.where(leaf_keep, dot(rhs[...], leaf_in[...]), 0.0).astype(BF16)

    pl.semaphore_wait(barrier, greeted)

    @pl.when(is_p1)
    def _():
        pl.semaphore_signal(go_sem, inc=1, device_id=left_leaf, device_id_type=MESH)

    @pl.when(both(both(ty == 1, core == 1), z == 8))
    def _():
        pl.semaphore_signal(late_sem, inc=1, device_id=at(8, 0, 0, 0), device_id_type=MESH)

    def mask_up():
        keep = lax.broadcasted_iota(jnp.int32, (width, width), 1) < node_rank
        for s in range(2):
            up[s, 0] = jnp.where(keep, up[s, 0], jnp.zeros((width, width), BF16))

    def mask_down():
        keep = lax.broadcasted_iota(jnp.int32, (width, width), 0) < node_rank
        for s in range(2):
            down[s, 0] = jnp.where(keep, down[s, 0], jnp.zeros((width, width), BF16))

    def send_up(summed, waits=False):
        coef[...] = jnp.where(node_keep, summed, 0.0).astype(BF16)
        if waits:
            pl.semaphore_wait(go_sem, 1)

        @pl.when(side == 0)
        def _():
            up_left.start()

        @pl.when(side == 1)
        def _():
            up_right.start()

    def cross_terms():
        cross_sum[0] = dot(child[:, right_part], cross[0, 0])
        cross_sum[1] = dot(child[:, left_part], cross[1, 0])

    @pl.when(is_even)
    def _():
        leaf_up.start()

    @pl.when(on_line)
    def _():
        pl.semaphore_wait(go_sem, 1)

    @pl.when(is_p1)
    def _():
        load_up.wait()
        summed = dot(leaf_coef[...], up[1, 0, narrow, :])
        leaf_up.wait_recv()
        send_up(summed + dot(child[:, narrow], up[0, 0, narrow, :]))
        load_cross.wait()
        cross_sum[0, :, narrow] = dot(leaf_coef[...], cross[0, 0, narrow, narrow])
        leaf_cross1[...] = dot(child[:, narrow], cross[1, 0, narrow, narrow])
        start(send_cross1)
        load_down.wait()
        mask_down()
        start(send_down1)
        leaf_map1[...] = down[1, 0, :, narrow]

    def lift(waits=True):
        up_left.wait_recv()
        summed = dot(child[:, left_part], up[0, 0])
        up_right.wait_recv()
        send_up(summed + dot(child[:, right_part], up[1, 0]), waits)

    @pl.when(is_p2)
    def _():
        load_up.wait()
        lift()
        load_cross.wait()
        cross_terms()
        start(send_cross2)
        leaf_cross2[...] = cross_sum[1]
        load_down.wait()
        mask_down()
        start(send_down2)
        leaf_map2[...] = down[1, 0]

    @pl.when(is_p3)
    def _():
        load_up.wait()
        lift()

        @pl.when(core == 0)
        def _():
            send_up4[0].wait_recv()
            path_coef[...] = dot(coef[...], map_a[...]).astype(BF16)
            for k in range(2):

                @pl.when(x // 2 == k)
                def _():
                    send_part4[k].start()

        load_cross.wait()
        cross_terms()
        load_down.wait()
        mask_down()

    @pl.when(is_p4)
    def _():
        load_up.wait()
        mask_up()
        pl.semaphore_wait(go_sem, 1)

        @pl.when(core == 0)
        def _():
            start(send_up4)
            load_down.wait()
            mask_down()
            start(send_down4)
            up_left.wait_recv()
            up_right.wait_recv()

        @pl.when(core == 1)
        def _():
            lift(waits=False)

        load_cross.wait()
        cross_terms()
        start(send_cross4)

        @pl.when(core == 1)
        def _():
            load_down.wait()
            mask_down()
            start(send_down4)

    @pl.when(is_gate)
    def _():
        load_up.wait()
        load_cross.wait()
        load_down.wait()
        mask_down()

        @pl.when(z % 4 == 1)
        def _():
            send_down7[0].wait_recv()
            pass_down7.start()

        map_keep = lax.broadcasted_iota(jnp.int32, (width, width), 1) < node_rank
        send_up6[0].wait_recv()
        for s in range(2):
            ahead = dot(jnp.where(map_keep, up[s, 0], jnp.zeros((width, width), BF16)), map_a[...])
            gate_maps[s] = ahead.astype(BF16)
        for copy in send_part4:
            copy.wait_recv()
        child[:, left_part] = (parts4[0].astype(F32) + parts4[1].astype(F32)).astype(BF16)
        up_right.wait_recv()
        six = dot(child[:, left_part], gate_maps[0]) + dot(child[:, right_part], gate_maps[1])
        path_coef[...] = six.astype(BF16)
        for k in (0, 1, 3):

            @pl.when(z % 4 == k)
            def _():
                send_part6[k].start()

        send_up(dot(child[:, left_part], up[0, 0]) + dot(child[:, right_part], up[1, 0]))

        @pl.when(is_hub)
        def _():
            parts6[2] = path_coef[...]
            send_top_up7.wait_recv()

            @pl.when(is_far_hub)
            def _():
                send_up8[0].wait_recv()
                send_cross9[0].wait_recv()
                map_e[...] = dot(map_e[...], map_f[...]).astype(BF16)

                @pl.when(z == 10)
                def _():
                    for k in range(2):
                        top_cross[k, 0] = dot(top_up[k, 0], map_e[...]).astype(BF16)

            for k in (0, 1, 3):
                send_part6[k].wait_recv()
            for k, part in enumerate((left_part, right_part)):
                six = parts6[2 * k].astype(F32) + parts6[2 * k + 1].astype(F32)
                top_child[:, part] = six.astype(BF16)

            @pl.when(z == 10)
            def _():
                far = dot(top_child[:, left_part], top_cross[0, 0]) + dot(top_child[:, right_part], top_cross[1, 0])
                far_out[...] = far.astype(BF16)
                start(send_part8[0])

            seven = dot(top_child[:, left_part], top_up[0, 0]) + dot(top_child[:, right_part], top_up[1, 0])
            top_coef[...] = seven.astype(BF16)
            for k in range(2):

                @pl.when(z // 4 % 2 == k)
                def _():
                    send_coef7[k].start()

            @pl.when(z == 14)
            def _():
                far_out[...] = dot(top_coef[...], map_e[...]).astype(BF16)
                start(send_part8[1])

            send_child7.start()

        def center_cross_terms():
            send_top_cross.wait_recv()
            top_sum[0] = dot(top_child[:, right_part], top_cross[0, 0]).astype(BF16)
            top_sum[1] = dot(top_child[:, left_part], top_cross[1, 0]).astype(BF16)

        @pl.when(is_left_center)
        def _():
            send_top_up8.wait_recv()
            send_coef7[0].wait_recv()
            send_coef7[1].wait_recv()
            center_cross_terms()
            start(send_cross8_first)
            send_cross8[1].start()
            cross_c[...] = top_sum[1]
            eight = dot(top_child[:, left_part], top_up[0, 0]) + dot(top_child[:, right_part], top_up[1, 0])
            top_coef[...] = eight.astype(BF16)
            send_cross9[2].wait_recv()
            far_out[...] = dot(top_coef[...], map_f[...]).astype(BF16)
            start(send_part8_right)

        @pl.when(is_right_center)
        def _():
            pl.semaphore_signal(late_sem, inc=1, device_id=p8, device_id_type=MESH)
            send_coef7[1].wait_recv()
            send_coef7[0].wait_recv()
            center_cross_terms()
            start(send_cross8)

        cross_terms()

        @pl.when(z == 1)
        def _():
            send_down8_first[0].wait_recv()
            pass_down8.start()

    @pl.when(is_p6)
    def _():
        load_up.wait()
        mask_up()
        start(send_up6)
        load_cross.wait()
        load_down.wait()
        mask_down()
        for copy in send_up6:
            copy.wait_send()
        send_down6[1].start()

        @pl.when(z % 4 == 1)
        def _():
            send_down6[0].start()

        @pl.when(both(z % 4 == 3, z != 7))
        def _():
            send_down6_half[0].start()

        up_right.wait_recv()

        @pl.when(both(z % 4 == 3, z != 7))
        def _():
            send_down6_half[1].start()

        @pl.when(z == 7)
        def _():
            send_down6[0].start()

        up_left.wait_recv()
        cross_terms()
        start(send_cross6)

    @pl.when(is_p7)
    def _():
        load_up.wait()
        mask_up()
        send_top_up7.start()
        load_down.wait()
        mask_down()
        start(send_down7[1:])
        load_cross.wait()
        send_child7.wait_recv()
        cross_terms()
        start(send_cross7)

    @pl.when(is_p8)
    def _():
        load_up.wait()
        mask_up()
        load_cross.wait()
        send_top_cross.start()
        load_down.wait()
        mask_down()

        @pl.when(is_left_p8)
        def _():
            send_down8[1].start()
            send_down8_first[1].start()
            start(send_down8_first[4:])

        @pl.when(is_right_p8)
        def _():
            send_up8[1].start()

        send_cross1[0].wait_recv()

        @pl.when(is_right_p8)
        def _():
            send_down1[0].wait_recv()
            send_up8[0].start()
            pl.semaphore_wait(late_sem, 1)
            start(send_down8)

        @pl.when(is_left_p8)
        def _():
            send_top_up8.start()
            send_down1[0].wait_recv()
            for k, after in ((1, 3), (3, 2)):
                send_down8_first[k].wait_send()
                send_down8_first[after].start()

    @pl.when(both(on_top, z % 8 == 0))
    def _():
        load_up.wait()
        load_cross.wait()
        load_down.wait()

    @pl.when(is_p9)
    def _():
        send_cross9[0].start()
        pl.semaphore_wait(late_sem, 1)
        send_cross9[1].start()
        send_cross9[2].start()

    load_diag.wait()
    product[...] = dot(rhs[...], diag[...])
    load_out.wait()

    def sent(condition, copies):
        @pl.when(condition)
        def _():
            for copy in copies:
                copy.wait_send()

    sent(is_even, [leaf_up])
    sent(is_p1, [up_left, *send_cross1, *send_down1])
    sent(is_p2, [up_left, *send_cross2, *send_down2])
    sent(both(is_p3, core == 0), [send_part4[0]])
    sent(is_p3, [up_left])
    sent(both(is_p4, core == 0), send_up4)
    sent(both(is_p4, core == 1), [up_left])
    sent(is_p4, [*send_cross4, *send_down4])
    sent(is_gate, [up_left])
    sent(both(is_gate, z % 4 != 2), [send_part6[0]])
    sent(is_hub, [send_coef7[0], send_child7])
    sent(is_far_hub, send_part8[0])
    sent(is_left_center, [*send_cross8_first, send_cross8[1], *send_part8_right])
    sent(is_right_center, send_cross8)
    sent(is_p6, [send_down6[1], *send_cross6])
    sent(both(is_p6, both(z % 4 == 3, z != 7)), send_down6_half)
    sent(both(is_p6, jnp.logical_not(both(z % 4 == 3, z != 7))), [send_down6[0]])
    sent(is_p7, [send_top_up7, *send_down7[1:], *send_cross7])
    sent(is_p8, [send_top_cross, send_down8[1]])
    sent(is_left_p8, [send_top_up8, send_down8_first[2], *send_down8_first[4:]])
    sent(is_right_p8, [*send_up8, send_down8[0]])
    sent(is_p9, send_cross9)

    def lower_hub():
        send_down8[0].wait_recv()
        send_cross8[0].wait_recv()
        send_part8[0][0].wait_recv()

        @pl.when(z == 6)
        def _():
            send_part8[1][0].wait_recv()
            crossed = parts8[0].astype(F32) + parts8[1].astype(F32)
            parts8[0] = crossed.astype(BF16)

        top_out[...] = (cross_c[...].astype(F32) + dot(parts8[0], map_b[...])).astype(BF16)
        send_above7[0].start()

        @pl.when(z > 6)
        def _():
            start(send_above7[1:])

        above[...] = top_out[...]

    @pl.when(is_gate)
    def _():
        @pl.when(z == 10)
        def _():
            lower_hub()

        @pl.when(z % 4 != 1)
        def _():
            send_down7[0].wait_recv()

        @pl.when(z % 4 == 1)
        def _():
            pass_down7.wait_send()

        send_down6[0].wait_recv()
        map_d[...] = dot(map_d[...], map_c[...]).astype(BF16)
        for s in range(2):
            gate_maps[s] = dot(map_d[...], down[s, 0]).astype(BF16)

        @pl.when(both(z < 6, z != 1))
        def _():
            send_down8_first[0].wait_recv()

        @pl.when(z == 1)
        def _():
            pass_down8.wait_send()

        @pl.when(z < 6)
        def _():
            for s in range(2):
                top_up[s, 0] = dot(map_b[...], gate_maps[s]).astype(BF16)

        send_cross7[0].wait_recv()
        send_cross6[0].wait_recv()
        five = (cross_b[...] + dot(cross_a[...].astype(BF16), map_c[...])).astype(BF16)
        for s in range(2):
            cross_sum[s] += dot(five, down[s, 0])

        @pl.when(z < 6)
        def _():
            send_part8[1][0].wait_recv()
            for s in range(2):
                cross_sum[s] += dot(parts8[1], top_up[s, 0])

            @pl.when(z != 4)
            def _():
                send_cross8_first[0].wait_recv()

            send_part8[0][0].wait_recv()
            for s in range(2):
                four = cross_sum[s] + dot(cross_c[...], gate_maps[s]) + dot(parts8[0], top_up[s, 0])
                outgoing[s] = four.astype(BF16)
                start(send_above4[3 * s : 3 * s + 3])

        @pl.when(both(is_late_hub, z != 10))
        def _():
            lower_hub()

        @pl.when(both(z > 6, z % 4 != 2))
        def _():
            send_above7[0].wait_recv()

        @pl.when(z >= 6)
        def _():
            for s in range(2):
                outgoing[s] = (cross_sum[s] + dot(above[...], gate_maps[s])).astype(BF16)
                start(send_above4[3 * s : 3 * s + 3])

    @pl.when(is_p3)
    def _():
        send_down4[0].wait_recv()
        head_map[...] = dot(map_d[...], down[0, 0]).astype(BF16)

        @pl.when(core == 0)
        def _():
            send_head_map_0.start()

        @pl.when(core == 1)
        def _():
            send_head_map.start()

        send_cross4[0].wait_recv()
        cross_four = cross_a[...].astype(BF16)
        cross_sum[0] += dot(cross_four, down[0, 0])

        @pl.when(core == 0)
        def _():
            send_head_base_0.start()

        @pl.when(core == 1)
        def _():
            send_head_base.start()

        cross_sum[1] += dot(cross_four, down[1, 0])
        down[1, 0] = dot(map_d[...], down[1, 0]).astype(BF16)

        @pl.when(core == 0)
        def _():
            send_map_0.start()
            send_base_0.start()

    is_server = both(y == 0, core == 1)

    @pl.when(is_server)
    def _():
        send_map_0.wait_recv()
        send_base_0.wait_recv()

        @pl.when(is_gate)
        def _():
            above_0[...] = outgoing[0]

        @pl.when(jnp.logical_not(is_gate))
        def _():
            send_above4[0].wait_recv()

        out_0[...] = (base_0[...] + dot(above_0[...], map_0[...])).astype(BF16)
        start([send_above2_0[0], send_above2_0[2]])

    @pl.when(both(is_p3, core == 1))
    def _():
        send_above4[3].wait_recv()
        outgoing[1] = (cross_sum[1] + dot(above[...], down[1, 0])).astype(BF16)
        start(send_above2_right)
        start([send_above2_0[1], send_above2_0[3]])
        leaf_above[...] = outgoing[1]

    @pl.when(both(is_head, core == 1))
    def _():
        send_head_map.wait_recv()
        send_head_base.wait_recv()

        @pl.when(is_gate)
        def _():
            above[...] = outgoing[1]

        @pl.when(jnp.logical_not(is_gate))
        def _():
            send_above4[3].wait_recv()

        head_out[...] = (head_base[...] + dot(above[...], head_map[...])).astype(BF16)
        start(send_above2)
        start([send_above2_0[1], send_above2_0[3]])
        leaf_above[...] = head_out[...]

    @pl.when(both(is_even, jnp.logical_not(is_p8)))
    def _():
        send_cross1[0].wait_recv()
        send_down1[0].wait_recv()

    @pl.when(jnp.logical_not(is_p2))
    def _():
        send_cross2[0].wait_recv()
        send_down2[0].wait_recv()

    zero = dot(leaf_cross2[...].astype(BF16), leaf_map1[...]) + leaf_cross1[...]
    zero = jnp.where(leaf_keep, zero, 0.0).astype(BF16)
    product[...] += dot(zero, leaf_out[...])
    map_keep = lax.broadcasted_iota(jnp.int32, (width, leaf_width), 1) < leaf_rank
    leaf_map1[...] = jnp.where(map_keep, dot(leaf_map2[...], leaf_map1[...]), 0.0).astype(BF16)
    leaf_map2[...] = dot(leaf_map1[...], leaf_out[...]).astype(BF16)

    @pl.when(jnp.logical_not(is_server))
    def _():
        send_above2[0].wait_recv()

    product[...] += dot(leaf_above[...], leaf_map2[...])

    sent(is_server, send_above2_0)
    sent(both(is_head, core == 1), send_above2)
    sent(both(is_p3, core == 1), [send_head_map, send_head_base, *send_above2_right])
    sent(both(is_p3, core == 0), [send_head_map_0, send_head_base_0, send_map_0, send_base_0])
    sent(is_gate, send_above4)
    sent(is_late_hub, send_above7[:1])
    sent(is_far_hub, send_above7[1:])


def on_device(rhs, diag_blocks, leaf_in, leaf_out, up_maps, cross_maps, down_maps, node_rank):
    rows, leaf = rhs.shape
    width, leaf_width = up_maps.shape[-1], leaf_in.shape[1]
    operands = (rhs, diag_blocks, leaf_in, leaf_out, up_maps, cross_maps, down_maps)

    def vector(*lead, kind=BF16, columns=width):
        return pltpu.VMEM((*lead, rows, columns), kind)

    full_map = pltpu.VMEM((width, width), BF16)
    return pl.pallas_call(
        kernel,
        out_shape=pltpu.VMEM((rows, leaf), F32),
        in_specs=[pl.BlockSpec(memory_space=pl.ANY)] * 8,
        out_specs=pl.BlockSpec(memory_space=pltpu.VMEM),
        scratch_shapes=[pltpu.VMEM(each.shape, each.dtype) for each in operands]
        + [
            pltpu.SMEM(node_rank.shape, node_rank.dtype),
            vector(columns=leaf_width),
            vector(),
            vector(columns=2 * width),
            vector(2, kind=F32),
            vector(),
            vector(2),
            full_map,
            full_map,
            full_map,
            full_map,
            full_map,
            full_map,
            pltpu.VMEM(up_maps.shape, BF16),
            pltpu.VMEM(cross_maps.shape, BF16),
            vector(columns=2 * width),
            vector(),
            vector(2),
            vector(),
            vector(),
            pltpu.VMEM((2, width, width), BF16),
            full_map,
            vector(kind=F32),
            vector(),
            full_map,
            vector(kind=F32),
            vector(),
            vector(),
            full_map,
            pltpu.VMEM((width, leaf_width), BF16),
            vector(kind=F32),
            vector(kind=F32),
            vector(),
            vector(kind=F32),
            vector(kind=F32, columns=leaf_width),
            vector(),
            vector(),
            vector(2),
            vector(4),
            vector(2),
            pltpu.SemaphoreType.DMA((8,)),
            pltpu.SemaphoreType.DMA((16,)),
            pltpu.SemaphoreType.DMA((28,)),
            pltpu.SemaphoreType.REGULAR,
            pltpu.SemaphoreType.REGULAR,
        ],
        compiler_params=pltpu.CompilerParams(
            collective_id=0, has_side_effects=True, vmem_limit_bytes=60 * 2**20
        ),
    )(*operands, node_rank)


def solution(mesh):
    assert mesh.shape["tx"] == N_Z * N_CORE and mesh.shape["ty"] == N_X * N_Y
    in_specs = (
        P(None, ("tx", "ty")),
        P(("tx", "ty"), None),
        P(("tx", "ty"), None),
        P(("tx", "ty"), None),
        P(None, ("tx", "ty"), None, None),
        P(None, ("tx", "ty"), None, None),
        P(None, ("tx", "ty"), None, None),
        P(("tx", "ty"), None),
    )
    return jax.shard_map(
        on_device, mesh=mesh, in_specs=in_specs, out_specs=P(None, ("tx", "ty")), check_vma=False
    )
```
